512 devices in a mesh: domain: 64 (over z_hi, x, y), band: 8 (over z_lo, core).
Axes of the slice: x: 4, y: 8, z: 8 (z_hi: 2, z_lo: 4; z = z_hi * 4 + z_lo), core: 2. Of those that a mesh axis runs over, the one named last changes fastest.
Arguments:
- start_block: bfloat16 [64896, 1024], P('domain', 'band'), may hold values from -2700 to 2700
- resident: bfloat16 [64896, 1024], P('domain', 'band'), may hold values from -16 to 16
- cell_kernel: bfloat16 [343, 343], replicated, may hold values from -0.3054414 to 3.3054414, as said below
- cell_scale: float32 [256], P('domain'), may hold values from 0.5 to 2
- potential: float32 [64896], P('domain'), may hold values from 0 to 4
- cell_nodes: int32 [256, 343], P('domain'), may hold values from 0 to 1182, as said below
- send_rows: int32 [10816], P('domain'), may hold values from 0 to 1013, as said below
Outputs:
- filtered_block: bfloat16 [64896, 1024], P('domain', 'band')
- margin: float32 [1024, 1024], P('domain', 'band')
The draws below stay inside these ranges and needn't reach their ends.
Inputs may be any that keep to these rules, and one draw needn't show every extreme that they name: `cell_nodes`: cell c of slab s is a hexahedron of 7 by 7 by 7 nodes, node k = (kz * 7 + ky) * 7 + kx; the slab's cells form a 2 by 2 layer, neighbours share their faces' nodes; values below 1014 are the slab's own rows, value 1014 + j is the j-th entry of the next slab's send_rows (its node kz = 6 plane). `send_rows`: slab s's 169 entries are distinct rows of that slab, its nodes with kz = 0, in the order in which the slab below numbers them. `cell_kernel`: symmetric.
All inputs are finite; a program needn't handle non-finite values.
Results may differ from the reference program's by a relative error of at most 0.0033.
Values may be sent and summed in bfloat16 or wider, within the bound.
A program may use at most 64 MiB of HBM per device.

```python
import math
import jax
import jax.numpy as jnp
from jax import lax

EDGE = 7
CELL_NODES = 343
ORB = 128
RESIDENT = 1024
DEGREE = 8
CX = 2
CELLS_DEV = 4
NXN = 13
PLANE = 169
OWNED = 1014
EXTENDED = 1183
SLABS = 64
NODES = 64896
CELLS = 256
FILTERED = 1024
N_DOMAIN = 64


def slab_places(key):
    keys = jax.random.split(key, N_DOMAIN)

    def shuffled(one_key):
        return jax.random.permutation(one_key, OWNED).astype(jnp.int32)
    places = jax.vmap(shuffled)(keys)
    middle = 1 + jax.random.permutation(jax.random.fold_in(key, 5), OWNED - 2).astype(jnp.int32)
    leading = jnp.concatenate([jnp.array([OWNED - 1, 0], jnp.int32), middle])
    return places.at[0].set(leading)


def draw_send_rows(key, part):
    places = slab_places(key)
    return places[:, :PLANE].reshape(-1).astype(jnp.int32)


def draw_cell_nodes(key, part):
    places = slab_places(key)
    cell_index = jnp.arange(CELLS_DEV, dtype=jnp.int32)
    cell_x = cell_index % CX
    cell_y = cell_index // CX
    local = jnp.arange(CELL_NODES, dtype=jnp.int32)
    node_x = local % EDGE
    node_y = local // EDGE % EDGE
    node_z = local // (EDGE * EDGE)
    grid_x = cell_x[:, None] * (EDGE - 1) + node_x[None, :]
    grid_y = cell_y[:, None] * (EDGE - 1) + node_y[None, :]
    grid_z = jnp.broadcast_to(node_z[None, :], grid_x.shape)
    flat = grid_y * NXN + grid_x
    structured = jnp.minimum(grid_z, EDGE - 2) * PLANE + flat

    def one_slab(place):
        return jnp.where(grid_z == EDGE - 1, OWNED + flat, place[structured])
    return jax.vmap(one_slab)(places).reshape(CELLS, CELL_NODES).astype(jnp.int32)


def draw_cell_kernel(key, part):
    key = jax.random.fold_in(key, 7)
    shape = (CELL_NODES, CELL_NODES)
    raw = jax.random.truncated_normal(key, -4.0, 4.0, shape, jnp.float32)
    raw = raw * (2.0 * CELL_NODES) ** (-0.5)
    kernel = raw + raw.T + 3.0 * jnp.eye(CELL_NODES, dtype=jnp.float32)
    return kernel.astype(jnp.bfloat16)


def draw_start_block(key, part):
    key = jax.random.fold_in(key, 13)
    key_base, key_row, key_col = jax.random.split(key, 3)
    shape = (NODES, FILTERED)
    base = jax.random.truncated_normal(key_base, -3.0, 3.0, shape, jnp.float32)
    rising = 3.0
    row_scale = 10.0 ** jax.random.uniform(key_row, (NODES, 1), jnp.float32)
    col_scale = 10.0 ** jax.random.uniform(key_col, (1, FILTERED), jnp.float32)
    position = jnp.arange(NODES, dtype=jnp.float32)[:, None] / NODES
    return (base * row_scale * col_scale * rising ** position).astype(jnp.bfloat16)


def strengthened(values, own_key, source, target, blocks, factor):
    owner, partner = [(jnp.arange(values.shape[dim]) // (values.shape[dim] // blocks)).reshape([-1 if axis == dim else 1 for axis in range(values.ndim)]) for dim in (source, target)]
    chosen = jax.random.permutation(own_key, blocks)[partner]
    strong = (owner == chosen) | (owner == (partner + blocks // 2) % blocks)
    return jnp.where(strong, factor * values, values)


def steps_of(own_key, extent, cuts, low, high):
    gain = 1.0
    for axis_at, parts in cuts:
        draws = jax.random.uniform(jax.random.fold_in(jax.random.fold_in(own_key, 6), axis_at), (parts,), jnp.float32, low / len(cuts), high / len(cuts))
        gain = gain * jnp.repeat(jnp.exp(draws), extent[axis_at] // parts).reshape((-1,) + (1,) * (len(extent) - 1 - axis_at))
    return gain


def gaussian_with(stream_key, dims, spread, bound, cuts, heavy, held_as=jnp.bfloat16):
    values = spread * jax.random.normal(stream_key, dims, jnp.float32)
    if cuts:
        values = values * steps_of(stream_key, dims, cuts, -0.22, 0.18)
    return jnp.clip(strengthened(values, jax.random.fold_in(stream_key, 3), *heavy), -bound, bound).astype(held_as)


def setup_inputs(seed: int = 0) -> dict:
    arg_keys = jax.random.split(jax.random.key(seed), 8)
    start_block = draw_start_block(jax.random.fold_in(arg_keys[7], 71), 0)
    resident = gaussian_with(arg_keys[1], (NODES, RESIDENT), 1.0, 16.0, ((0, 64), (1, 8)), (0, 1, 64, 4.0))
    cell_kernel = draw_cell_kernel(jax.random.fold_in(arg_keys[7], 71), 0)
    cell_scale = jnp.clip(jnp.exp(math.log(2.0) - 1.3862944 * jax.random.uniform(arg_keys[3], (CELLS,), jnp.float32) ** steps_of(arg_keys[3], (CELLS,), ((0, 64),), -0.2, 0.2)), 0.5, 2.0)
    potential = jnp.clip(4.0 * jax.random.uniform(arg_keys[4], (NODES,), jnp.float32) ** steps_of(arg_keys[4], (NODES,), ((0, 64),), -0.2, 0.2), 0.0, 4.0)
    cell_nodes = draw_cell_nodes(jax.random.fold_in(arg_keys[7], 71), 0)
    send_rows = draw_send_rows(jax.random.fold_in(arg_keys[7], 71), 0)
    return dict(start_block=start_block, resident=resident, cell_kernel=cell_kernel, cell_scale=cell_scale, potential=potential, cell_nodes=cell_nodes, send_rows=send_rows)


lower_edge = 0.0
cutoff_edge = 16.0
upper_edge = 96.0
epsilon = 1e-06

def chebyshev_terms(degree):
    half_width = (upper_edge - cutoff_edge) / 2.0
    centre = (upper_edge + cutoff_edge) / 2.0
    sigma_now = half_width / (lower_edge - centre)
    gamma_ratio = 2.0 / sigma_now
    lead_factor = sigma_now / half_width
    recurrence = []
    for _ in range(degree - 1):
        sigma_next = 1.0 / (gamma_ratio - sigma_now)
        recurrence.append((2.0 * sigma_next / half_width, sigma_now * sigma_next))
        sigma_now = sigma_next
    return (centre, lead_factor, recurrence)

def take_rows(values, indices):
    return values[indices]

def add_rows(target, indices, values):
    return target.at[indices].add(values)

def reference(start_block, resident, cell_kernel, cell_scale, potential, cell_nodes, send_rows):
    slab_count = SLABS
    band_count = FILTERED // ORB
    nodes_t = cell_nodes.reshape(slab_count, CELLS_DEV, CELL_NODES).transpose(0, 2, 1)
    plane_rows = send_rows.reshape(slab_count, PLANE)
    scale_grid = cell_scale.reshape(slab_count, CELLS_DEV)
    pot_grid = potential.reshape(slab_count, OWNED)
    kernel_wide = cell_kernel.astype(jnp.float32)
    centre, lead_factor, recurrence = chebyshev_terms(DEGREE)

    def apply_ham(vector):
        rounded = vector.astype(jnp.bfloat16)
        planes = jax.vmap(take_rows)(rounded, plane_rows)
        ghost_rows = jnp.concatenate([planes[1:], jnp.zeros_like(planes[:1])], 0)
        extended = jnp.concatenate([rounded, ghost_rows], 1)
        cell_block = jax.vmap(take_rows)(extended, nodes_t)
        products = jnp.einsum('ij,sjcw->sicw', kernel_wide, cell_block.astype(jnp.float32))
        products = products * scale_grid[:, None, :, None]
        summed = jax.vmap(add_rows)(jnp.zeros((slab_count, EXTENDED, ORB), jnp.float32), nodes_t, products)
        upper_part = summed[:, OWNED:]
        from_below = jnp.concatenate([jnp.zeros_like(upper_part[:1]), upper_part[:-1]], 0)
        own_part = jax.vmap(add_rows)(summed[:, :OWNED], plane_rows, from_below)
        return own_part + pot_grid[:, :, None] * vector

    def filter_block(orbital_block):
        former = orbital_block.astype(jnp.float32)
        current = lead_factor * (apply_ham(former) - centre * former)
        for lead_coeff, tail_coeff in recurrence:
            following = lead_coeff * (apply_ham(current) - centre * current) - tail_coeff * former
            former = current
            current = following
        return current
    blocks = start_block.reshape(slab_count, OWNED, band_count, ORB).transpose(2, 0, 1, 3)
    filtered_raw = lax.map(filter_block, blocks)
    filtered_raw = filtered_raw.transpose(1, 2, 0, 3).reshape(NODES, FILTERED)
    column_total = lax.optimization_barrier(jnp.sum(filtered_raw * filtered_raw, 0))
    inverse = lax.rsqrt(column_total + epsilon)
    filtered_block = (filtered_raw * inverse[None, :]).astype(jnp.bfloat16)
    filtered_low = filtered_raw.astype(jnp.bfloat16)
    margin = jnp.dot(resident.T, filtered_low, preferred_element_type=jnp.float32) * inverse[None, :]
    return (filtered_block, margin)
```

```python
import functools

import jax
import jax.numpy as jnp
from jax import lax
from jax.experimental import pallas as pl
from jax.experimental.pallas import tpu as pltpu
from jax.sharding import PartitionSpec as P

DEGREE = 8
EDGE = 7
ORB = 128
OWNED = 1014
PLANE = 169

lower_edge = 0.0
cutoff_edge = 16.0
upper_edge = 96.0
epsilon = 1e-06

NX = 13
XS = 112
NR = NX * XS
NRP = NR + 16
NRL = 1536
PL = 208
PLP = 256
MR = 392
KR = 448
KL = 384
OWNP = 1024

N_DOM = 64
N_ZH, N_X, N_Y = 2, 4, 8
N_ZL = 4

f32 = jnp.float32
bf16 = jnp.bfloat16
MESH = pl.DeviceIdType.MESH


def chebyshev_terms(degree):
    half_width = (upper_edge - cutoff_edge) / 2.0
    centre = (upper_edge + cutoff_edge) / 2.0
    sigma_now = half_width / (lower_edge - centre)
    gamma_ratio = 2.0 / sigma_now
    lead_factor = sigma_now / half_width
    recurrence = [(lead_factor, 0.0)]
    for _ in range(degree - 1):
        sigma_next = 1.0 / (gamma_ratio - sigma_now)
        recurrence.append((2.0 * sigma_next / half_width, sigma_now * sigma_next))
        sigma_now = sigma_next
    return (centre, recurrence)


CENTRE, TERMS = chebyshev_terms(DEGREE)


def mm(a, b):
    return jnp.dot(a, b, preferred_element_type=f32)


def mm_nt(a, b):
    return lax.dot_general(a, b, (((1,), (1,)), ((), ())), preferred_element_type=f32)


def mm_tn(a, b):
    return lax.dot_general(a, b, (((0,), (0,)), ((), ())), preferred_element_type=f32)


def iota(shape, dim):
    return lax.broadcasted_iota(jnp.int32, shape, dim)


def hot(cond):
    return jnp.where(cond, 1.0, 0.0).astype(bf16)


def pick(k, values):
    out = jnp.float32(values[0])
    for i in range(1, len(values)):
        out = jnp.where(k == i, jnp.float32(values[i]), out)
    return out


def kernel(
    start_ref, res_ref, ck_ref, scale_ref, pot_ref, cn_ref, cns_ref, sr_ref,
    out_ref, margin_ref,
    V, R, O, OG, part, potc, place, prow, Pm, PT, Q, st, kpad, K1, Kp, T, KgP, KttP, KgD,
    ET, F, W2, top_col, jbot_col, pot8, cnp, srp,
    Gs, cs, Gr, cr, Js, Jr, Us, Ur, RB, H2, LOW, CO, mpb, X1, M0, SF, SB, X2, N1s, N1r, N2s, N2r,
    g_send, g_recv, c_send, c_recv, j_sem, u_sem, r_send, r_recv, x1_send, x1_recv, x2_send, x2_recv,
    n1_send, n1_recv, n2_send, n2_recv,
):
    d = lax.axis_index("domain")
    band = lax.axis_index("band")
    zh = d // (N_X * N_Y)
    gx = (d // N_Y) % N_X
    gy = d % N_Y
    zl = band // 2
    core = band % 2
    sibling = zl * 2 + (1 - core)
    has_below = d > 0
    has_above = d < N_DOM - 1

    Gr[...] = jnp.zeros_like(Gr)
    cr[...] = jnp.zeros_like(cr)
    Jr[...] = jnp.full(Jr.shape, -3.0, f32)
    Ur[0:8, :] = jnp.full((8, PLP), -4.0, f32)
    Ur[8:16, :] = jnp.zeros((8, PLP), f32)

    barrier = pltpu.get_barrier_semaphore()

    def greet(dom, bnd):
        pl.semaphore_signal(barrier, inc=1, device_id=(dom, bnd), device_id_type=MESH)

    x_peers = [(zh * N_X + (gx + i) % N_X) * N_Y + gy for i in range(1, N_X)]
    x_from = x_peers
    yz_off = [(a, b) for a in range(N_ZH) for b in range(N_Y) if (a, b) != (0, 0)]
    yz_peers = [
        (((zh + a) % N_ZH) * N_X + gx) * N_Y + (gy + b) % N_Y for a, b in yz_off
    ]

    @pl.when(has_below)
    def _():
        greet(d - 1, band)

    @pl.when(has_above)
    def _():
        greet(d + 1, band)

    @pl.when(zl > 0)
    def _():
        greet(d, band - 2)

    @pl.when(zl < N_ZL - 1)
    def _():
        greet(d, band + 2)

    greet(d, sibling)
    for p in x_peers + yz_peers:
        greet(p, band)

    corner = [cns_ref[c, 0] for c in range(4)]
    right_x = [cns_ref[c, EDGE - 1] for c in range(4)]
    right_y = [cns_ref[c, EDGE * (EDGE - 1)] for c in range(4)]
    pos = []
    for c in range(4):
        in_x = sum([jnp.where(right_x[b] == corner[c], 1, 0) for b in range(4)])
        in_y = sum([jnp.where(right_y[b] == corner[c], 1, 0) for b in range(4)])
        pos.append(in_x + 2 * in_y)
    scale = []
    for p in range(4):
        s = jnp.float32(0.0)
        for c in range(4):
            s = s + jnp.where(pos[c] == p, scale_ref[c], 0.0)
        scale.append(s)

    cnp[...] = jnp.zeros_like(cnp)
    cnp[0:4, 0:343] = cn_ref[...]
    row8 = iota((8, KL), 0)
    full = jnp.zeros((8, KL), jnp.int32)
    for c in range(4):
        line = jnp.broadcast_to(cnp[c : c + 1, :], (8, KL))
        full = full + jnp.where((row8 & 3) == pos[c], line, 0)
    cn8 = jnp.where(row8 < 4, full >> 5, full & 31).astype(f32).astype(bf16)

    rr = iota((XS, KL), 0)
    ln = iota((XS, KL), 1)
    yy = rr >> 3
    zz = rr & 7
    k_base = jnp.where(
        (zz < EDGE) & (yy < NX), zz * 49 + jnp.where(yy > 6, yy - 6, yy) * 7, -1000
    )
    diff = k_base - ln
    l8 = iota((XS, 8), 1)
    y8 = iota((XS, 8), 0) >> 3
    z128 = iota((XS, 128), 0) & 7
    y128 = iota((XS, 128), 0) >> 3
    top_row = (z128 < EDGE) & (y128 < NX)
    own_row = (z128 < EDGE - 1) & (y128 < NX)
    weights = jnp.where(iota((8, 128), 0) < 4, 32.0, 1.0).astype(bf16)
    lane = iota((XS, 128), 1).astype(f32)
    for X in range(NX):
        x = X if X <= 6 else X - 6
        one = hot(diff == -x)
        Q[X * XS : (X + 1) * XS, :] = one
        a1 = mm_nt(one, cn8)
        cell = jnp.where(y8 > 6, 2, 0) + (1 if X > 6 else 0)
        a1 = jnp.where((l8 & 3) == cell, a1, 0.0).astype(bf16)
        pl_x = mm(a1, weights)
        place[X * XS : (X + 1) * XS, :] = jnp.where(top_row, pl_x, -1.0)
        own = jnp.where(own_row, pl_x, -1.0)
        for t in range(8):
            Pm[X * XS : (X + 1) * XS, t * 128 : (t + 1) * 128] = hot(own == lane + 128.0 * t)
    place[NR:NRP, :] = jnp.full((NRP - NR, 128), -1.0, f32)

    srp[...] = jnp.full(srp.shape, -5.0, f32)
    srp[0:1, 0:PLANE] = sr_ref[...].astype(f32)
    top_col[...] = jnp.full(top_col.shape, -1.0, f32)
    yrow = iota((16, 128), 0)
    lane16 = iota((16, 128), 1)
    ET[...] = jnp.zeros_like(ET)
    for X in range(NX):
        b0 = jnp.concatenate(
            [place[pl.ds(X * XS, 8, stride=8), :], place[pl.ds(X * XS + 64, 8, stride=8), :]], 0
        )
        b0 = jnp.where(yrow < NX, b0, -1.0)
        for t in range(2):
            ET[X * 16 : X * 16 + 16, t * 128 : (t + 1) * 128] = hot(
                b0 == srp[0:1, t * 128 : (t + 1) * 128]
            )
        t0 = jnp.concatenate(
            [place[pl.ds(X * XS + 6, 8, stride=8), :], place[pl.ds(X * XS + 70, 8, stride=8), :]],
            0,
        )
        top_col[X * 16 : X * 16 + 16, :] = jnp.where(yrow < NX, t0 - float(OWNED), -1.0)
    jm = iota((PLP, 128), 0).astype(f32).astype(bf16)
    p_row = iota((PLP, 128), 0)
    jb = mm(ET[...], jm)
    jbot_col[...] = jnp.where(((p_row & 15) < NX) & (p_row < PL), jb, -2.0)
    p_lane = iota((8, PLP), 1)
    p_ok = ((p_lane & 15) < NX) & (p_lane < PL)
    jr = mm_nt(iota((8, PLP), 1).astype(f32).astype(bf16), ET[...])
    Js[...] = jnp.where(p_ok, jr, -2.0)

    pr = iota((PLP, KL), 0)
    pln = iota((PLP, KL), 1)
    pX = pr >> 4
    pY = pr & 15
    p_in = (pX < NX) & (pY < NX)
    ox = jnp.where(pX > 6, pX - 6, pX)
    oy = jnp.where(pY > 6, pY - 6, pY)
    q_top = hot(p_in & (294 + oy * 7 + ox == pln))
    at = mm_nt(cn8, q_top)
    lX = p_lane >> 4
    lY = p_lane & 15
    l_cell = jnp.where(lX > 6, 1, 0) + jnp.where(lY > 6, 2, 0)
    r8 = iota((8, PLP), 0)
    at = jnp.where((r8 & 3) == l_cell, at, 0.0) * jnp.where(r8 < 4, 32.0, 1.0)
    top_line = jnp.sum(at, 0, keepdims=True) - float(OWNED)
    Us[0:8, :] = jnp.where(p_ok, jnp.broadcast_to(top_line, (8, PLP)), -1.0)
    srow = iota((8, PLP), 0)
    stile = jnp.zeros((8, PLP), f32)
    for c in range(4):
        stile = jnp.where(srow == c, scale[c], stile)
    Us[8:16, :] = stile

    RB[band, 1008:1024, :] = jnp.zeros((16, ORB), bf16)
    RB[band, 0:OWNED, :] = res_ref[...]

    ones = lambda cond: jnp.where(cond, 1, 0)
    count = (
        ones(has_below) + ones(has_above) + ones(zl > 0) + ones(zl < N_ZL - 1)
        + 1 + len(x_peers) + len(yz_peers)
    )
    pl.semaphore_wait(barrier, count)

    def remote(src, dst, ssem, rsem, dom, bnd):
        return pltpu.make_async_remote_copy(
            src_ref=src, dst_ref=dst, send_sem=ssem, recv_sem=rsem,
            device_id=(dom, bnd), device_id_type=MESH,
        )

    j_copy = remote(Js, Jr, j_sem.at[0], j_sem.at[1], d - 1, band)
    u_copy = remote(Us, Ur, u_sem.at[0], u_sem.at[1], d + 1, band)

    @pl.when(has_below)
    def _():
        j_copy.start()

    @pl.when(has_above)
    def _():
        u_copy.start()

    def block(src, to, s):
        return remote(RB.at[src], RB.at[src], r_send.at[s], r_recv.at[src], d, to)

    def send_own(start):
        def act(c):
            c.start() if start else c.wait_send()

        @pl.when(zl < N_ZL - 1)
        def _():
            act(block(band, band + 2, 0))

        @pl.when(zl > 0)
        def _():
            act(block(band, band - 2, 1))

        act(block(band, sibling, 2))

    def forward(dist, start):
        @pl.when(zl >= dist)
        def _():
            src = band - 2 * dist
            if start:
                block(src, sibling, 0).wait_recv()

            @pl.when(zl < N_ZL - 1)
            def _():
                c = block(src, band + 2, 3 * dist)
                c.start() if start else c.wait_send()

            c = block(src, sibling, 3 * dist + 1)
            c.start() if start else c.wait_send()

        @pl.when(zl + dist <= N_ZL - 1)
        def _():
            src = band + 2 * dist
            if start:
                block(src, sibling, 0).wait_recv()

            @pl.when(zl > 0)
            def _():
                c = block(src, band - 2, 9 + 3 * dist)
                c.start() if start else c.wait_send()

            c = block(src, sibling, 10 + 3 * dist)
            c.start() if start else c.wait_send()

    send_own(True)

    st[1008:1024, :] = jnp.zeros((16, ORB), bf16)
    st[0:OWNED, :] = start_ref[...]
    V[0, 0:NR, :] = mm(Pm[...], st[...])
    V[0, NR:NRP, :] = jnp.zeros((NRP - NR, ORB), f32)
    V[1, :, :] = jnp.zeros((NRP, ORB), f32)
    part[...] = jnp.zeros_like(part)
    zero8 = jnp.zeros((8, ORB), f32)
    for X in range(NX):
        R[X * 64 : X * 64 + 64, 0:128] = V[0, X * XS : X * XS + 64, :].astype(bf16)
        R[X * 64 : X * 64 + 64, 128:256] = V[0, X * XS + 48 : X * XS + 112, :].astype(bf16)

    kpad[...] = jnp.zeros_like(kpad)
    kpad[0:343, 0:343] = ck_ref[...]
    kmat = kpad[...]
    r56 = iota((56, KL), 0)
    k56 = jnp.where((r56 & 7) < 7, (r56 & 7) * 49 + (r56 >> 3) * 7, -1000) - iota((56, KL), 1)
    row_hot = jnp.concatenate([jnp.where(k56 == -x, 1.0, 0.0) for x in range(7)], 0).astype(bf16)
    r64 = iota((64, KL), 0)
    k64 = (
        jnp.where(((r64 & 7) < 7) & (r64 < 56), (r64 & 7) * 49 + (r64 >> 3) * 7, -1000)
        - iota((64, KL), 1)
    )
    col_hot = jnp.concatenate([hot(k64 == -x) for x in range(7)], 0)
    K1[...] = mm(row_hot, kmat).astype(bf16)
    Kp[...] = mm_nt(K1[...], col_hot).astype(bf16)
    r16 = iota((16, KL), 0)
    l16 = iota((16, KL), 1)
    for cy in range(2):
        y = r16 - 6 * cy
        kt = jnp.where((y >= 0) & (y < 7), 294 + y * 7, -1000) - l16
        t_hot = jnp.concatenate([hot(kt == -x) for x in range(7)], 0)
        T[cy] = mm_nt(mm(t_hot, kmat).astype(bf16), col_hot).astype(bf16)

    def down(k):
        return remote(
            Gs.at[k, pl.ds(0, PL)], Gr.at[k, pl.ds(0, PL)], g_send.at[k], g_recv.at[k], d - 1, band
        )

    def up(k):
        return remote(cs.at[k], cr.at[k, pl.ds(0, PL)], c_send.at[k], c_recv.at[k], d + 1, band)

    def send_planes(k, cur):
        Gs[k, PL:PLP, :] = jnp.zeros((PLP - PL, ORB), bf16)
        for X in range(NX):
            lo = V[cur, pl.ds(X * XS, 8, stride=8), :]
            hi = V[cur, pl.ds(X * XS + 64, 8, stride=8), :]
            Gs[k, X * 16 : X * 16 + 16, :] = jnp.concatenate([lo, hi], 0).astype(bf16)

        @pl.when(has_below)
        def _():
            down(k).start()

        c0 = mm(T[0], R[0:KR, 0:128]) * scale[0] + mm(T[1], R[0:KR, 128:256]) * scale[2]
        c1 = mm(T[0], R[384 : 384 + KR, 0:128]) * scale[1]
        c1 = c1 + mm(T[1], R[384 : 384 + KR, 128:256]) * scale[3]
        cs[k, 0:96, :] = c0[0:96].astype(bf16)
        cs[k, 96:112, :] = (c0[96:112] + c1[0:16]).astype(bf16)
        cs[k, 112:208, :] = c1[16:112].astype(bf16)

        @pl.when(has_above)
        def _():
            up(k).start()

    send_planes(0, 0)

    pot8[...] = jnp.zeros_like(pot8)
    pot = pot_ref[...]
    p_hi = pot.astype(bf16)
    rest = pot - p_hi.astype(f32)
    p_mid = rest.astype(bf16)
    p_lo = (rest - p_mid.astype(f32)).astype(bf16)
    pot8[0:1, 0:OWNED] = p_hi.astype(f32)
    pot8[1:2, 0:OWNED] = p_mid.astype(f32)
    pot8[2:3, 0:OWNED] = p_lo.astype(f32)
    pcol = mm_nt(Pm[...], pot8[...].astype(bf16)).astype(bf16)
    potc[...] = mm(pcol, jnp.ones((8, 128), bf16)) - CENTRE

    for c in range(4):
        cx, cy = c % 2, c // 2
        x = pX - 6 * cx
        y = pY - 6 * cy
        inside = (x >= 0) & (x < 7) & (y >= 0) & (y < 7)
        c_top = hot(inside & (294 + y * 7 + x == pln))
        KgP[c] = mm_nt(K1[...], c_top).astype(bf16)
        KttP[c] = mm_nt(mm(c_top, kmat).astype(bf16), c_top)

    lin = iota((8, NRL), 1)
    lin_x = jnp.floor((lin.astype(f32) + 0.5) * (1.0 / XS)).astype(jnp.int32)
    lin_r = lin - lin_x * XS
    lin_y = lin_r >> 3
    lin_z = lin_r & 7
    lin_cell = jnp.where(lin_x > 6, 1, 0) + jnp.where(lin_y > 6, 2, 0)
    lin_8 = iota((8, NRL), 0)
    Q[NR:NRL, :] = jnp.zeros((NRL - NR, KL), bf16)
    ar = mm_nt(cn8, Q[...])
    ar = jnp.where((lin_8 & 3) == lin_cell, ar, 0.0) * jnp.where(lin_8 < 4, 32.0, 1.0)
    ar = jnp.broadcast_to(jnp.sum(ar, 0, keepdims=True), (8, NRL))
    prow[...] = jnp.where((lin_x < NX) & (lin_y < NX) & (lin_z < EDGE - 1), ar, -1.0)
    n16 = iota((16, NRL), 0).astype(f32)

    def fill(i, carry):
        base = (i * 16).astype(f32)
        PT[pl.ds(pl.multiple_of(i * 16, 16), 16), :] = hot(prow[0:1, :] == n16 + base)
        return carry

    lax.fori_loop(0, OWNP // 16, fill, 0)

    @pl.when(has_above)
    def _():
        j_copy.wait_recv()

    @pl.when(has_below)
    def _():
        u_copy.wait_recv()

    tc = top_col[...]
    jc = jbot_col[...]
    m1 = jnp.concatenate([hot(tc == Jr[0:1, t * 128 : (t + 1) * 128]) for t in range(2)], 1)
    F[...] = jnp.concatenate([hot(jc == Ur[0:1, t * 128 : (t + 1) * 128]) for t in range(2)], 1)
    for c in range(4):
        KgD[c] = mm(KgP[c], m1).astype(bf16)
    w = jnp.zeros((PLP, PLP), f32)
    for c in range(4):
        w = w + KttP[c] * Ur[8 + c : 9 + c, :]
    w_hi = w.astype(bf16)
    w_lo = (w - w_hi.astype(f32)).astype(bf16)
    fm = F[...]
    W2[0] = mm_nt(mm(fm, w_hi).astype(bf16), fm).astype(bf16)
    W2[1] = mm_nt(mm(fm, w_lo).astype(bf16), fm).astype(bf16)

    mask8 = jnp.where(iota((8, ORB), 0) < EDGE - 1, 1.0, 0.0)

    def spread(ref_of, X, factor):
        lo, hi = None, None
        for cx in range(2):
            x = X - 6 * cx
            if 0 <= x < 7:
                a = ref_of(cx, 0, x).reshape(7, 8, ORB) * factor(cx, 0)
                b = ref_of(cx, 1, x).reshape(7, 8, ORB) * factor(cx, 1)
                lo = a if lo is None else lo + a
                hi = b if hi is None else hi + b
        return jnp.concatenate([lo[0:6], lo[6:7] + hi[0:1], hi[1:7]], 0)

    def bulk(k, cur):
        nxt = 1 - cur
        a = pick(k, [t[0] for t in TERMS])
        b = pick(k, [t[1] for t in TERMS])
        am = mask8 * a
        for cx in range(2):
            O[cx] = mm(Kp[...], R[384 * cx : 384 * cx + KR, :])
        for X in range(NX):
            rows = slice(X * XS, X * XS + 104)
            s = spread(
                lambda cx, cy, x: O[cx, x * 56 : x * 56 + 56, cy * 128 : (cy + 1) * 128],
                X,
                lambda cx, cy: scale[cx + 2 * cy],
            )
            v = V[cur, rows, :].reshape(NX, 8, ORB)
            u = V[nxt, rows, :].reshape(NX, 8, ORB)
            pc = potc[rows, :].reshape(NX, 8, ORB)
            new = (s + pc * v) * am[None] - b * u
            part[rows, :] = new.reshape(104, ORB)
        g = Gs[k]
        return (mm(W2[0], g) + mm(W2[1], g)) * a

    def finish(k, cur, plane, last):
        nxt = 1 - cur
        a = pick(k, [t[0] for t in TERMS])
        am = mask8 * a

        @pl.when(has_below)
        def _():
            up(k).wait_recv()

        e = plane + mm(F[...], cr[k]) * a
        for X in range(NX):
            lo = pl.ds(X * XS, 8, stride=8)
            hi = pl.ds(X * XS + 64, 8, stride=8)
            part[lo, :] = part[lo, :] + e[X * 16 : X * 16 + 8]
            part[hi, :] = part[hi, :] + e[X * 16 + 8 : X * 16 + 16]

        @pl.when(has_above)
        def _():
            down(k).wait_recv()

        for c in range(4):
            OG[c] = mm(KgD[c], Gr[k])
        sq = jnp.zeros((8, ORB), f32)
        for X in range(NX):
            rows = slice(X * XS, X * XS + 104)
            s = spread(
                lambda cx, cy, x: OG[cx + 2 * cy, x * 56 : x * 56 + 56, :],
                X,
                lambda cx, cy: (am * scale[cx + 2 * cy])[None],
            )
            new = part[rows, :].reshape(NX, 8, ORB) + s
            flat = new.reshape(104, ORB)
            if last:
                sq = sq + jnp.sum(new * new, 0)
                padded = jnp.concatenate([flat, zero8], 0)
                top = padded.astype(bf16)
                H2[X * XS : (X + 1) * XS, 0:128] = top
                H2[X * XS : (X + 1) * XS, 128:256] = (padded - top.astype(f32)).astype(bf16)
            else:
                V[nxt, rows, :] = flat
                R[X * 64 : X * 64 + 64, 0:128] = flat[0:64].astype(bf16)
                R[X * 64 : X * 64 + 64, 128:256] = jnp.concatenate(
                    [flat[48:104], zero8], 0
                ).astype(bf16)
        return sq

    def step(k, carry):
        cur = lax.rem(k, 2)
        plane = bulk(k, cur)

        @pl.when(k == 3)
        def _():
            forward(1, True)

        @pl.when(k == 5)
        def _():
            forward(2, True)

        finish(k, cur, plane, False)
        send_planes(k + 1, 1 - cur)
        return carry

    lax.fori_loop(0, DEGREE - 1, step, 0)
    final = DEGREE - 1
    plane = bulk(final, final % 2)
    forward(3, True)
    H2[NR:NRL, :] = jnp.zeros((NRL - NR, 256), bf16)
    sq = finish(final, final % 2, plane, True)

    N1s[...] = jnp.broadcast_to(jnp.sum(sq, 0, keepdims=True), (8, ORB))

    def n1(i):
        return remote(N1s, N1r.at[i], n1_send.at[i], n1_recv.at[i], x_peers[i], band)

    for i in range(3):
        n1(i).start()

    un = mm(PT[...], H2[...])
    LOW[...] = un[:, 0:128].astype(bf16)
    CO[...] = un[:, 0:128] + un[:, 128:256]

    for i in range(N_ZL):
        src = i * 2 + (1 - core)
        block(src, sibling, 0).wait_recv()

    def x1(i):
        return remote(mpb.at[i], X1.at[i], x1_send.at[i], x1_recv.at[i], x_peers[i], band)

    for i in range(4):
        tx = (gx + 1 + i) % N_X
        for h in range(N_ZH):
            m = mm_tn(RB[h * N_X + tx], LOW[...])
            if i < 3:
                mpb[i, h * 128 : (h + 1) * 128, :] = m.astype(bf16)
            else:
                M0[h * 128 : (h + 1) * 128, :] = m
        if i < 3:
            x1(i).start()

    for i in range(3):
        n1(i).wait_recv()
    N2s[...] = N1s[...] + N1r[0] + N1r[1] + N1r[2]

    def n2(i):
        return remote(N2s, N2r.at[i], n2_send.at[i], n2_recv.at[i], yz_peers[i], band)

    for i in range(15):
        n2(i).start()

    acc = M0[...]
    for i in range(3):
        x1(i).wait_recv()
        acc = acc + X1[i].astype(f32)
    SF[...] = acc
    SB[...] = acc.astype(bf16)

    def x2(i):
        a, b = yz_off[i]
        row = (((zh + a) % N_ZH) * N_Y + (gy + b) % N_Y) * 16
        return remote(
            SB.at[pl.ds(pl.multiple_of(row, 16), 16)], X2.at[i], x2_send.at[i], x2_recv.at[i],
            yz_peers[i], band,
        )

    for i in range(15):
        x2(i).start()

    total = N2s[...]
    for i in range(15):
        n2(i).wait_recv()
        total = total + N2r[i]
    inverse = lax.rsqrt(total[0:1, :] + epsilon)
    out_ref[...] = (CO[...] * inverse)[0:OWNED].astype(bf16)

    m = SF[pl.ds(pl.multiple_of((zh * N_Y + gy) * 16, 16), 16), :]
    for i in range(15):
        x2(i).wait_recv()
        m = m + X2[i].astype(f32)
    margin_ref[...] = m * inverse

    @pl.when(has_below)
    def _():
        j_copy.wait_send()

    @pl.when(has_above)
    def _():
        u_copy.wait_send()

    def sent(k, carry):
        @pl.when(has_below)
        def _():
            down(k).wait_send()

        @pl.when(has_above)
        def _():
            up(k).wait_send()

        return carry

    lax.fori_loop(0, DEGREE, sent, 0)
    send_own(False)
    for dist in range(1, N_ZL):
        forward(dist, False)
    for i in range(3):
        n1(i).wait_send()
        x1(i).wait_send()
    for i in range(15):
        n2(i).wait_send()
        x2(i).wait_send()


def per_device(start_block, resident, cell_kernel, cell_scale, potential, cell_nodes, send_rows):
    vm = lambda shape, t: pltpu.VMEM(shape, t)
    dma = lambda n: pltpu.SemaphoreType.DMA((n,))
    vmem = pl.BlockSpec(memory_space=pltpu.VMEM)
    smem = pl.BlockSpec(memory_space=pltpu.SMEM)
    scratch = [
        vm((2, NRP, ORB), f32),
        vm((832, 256), bf16),
        vm((2, MR, 256), f32),
        vm((4, MR, ORB), f32),
        vm((NRP, ORB), f32),
        vm((NR, ORB), f32),
        vm((NRP, ORB), f32),
        vm((8, NRL), f32),
        vm((NR, OWNP), bf16),
        vm((OWNP, NRL), bf16),
        vm((NRL, KL), bf16),
        vm((OWNP, ORB), bf16),
        vm((KL, KL), bf16),
        vm((MR, KL), bf16),
        vm((MR, KR), bf16),
        vm((2, 112, KR), bf16),
        vm((4, MR, PLP), bf16),
        vm((4, PLP, PLP), f32),
        vm((4, MR, PLP), bf16),
        vm((PLP, PLP), bf16),
        vm((PLP, PLP), bf16),
        vm((2, PLP, PLP), bf16),
        vm((PLP, ORB), f32),
        vm((PLP, ORB), f32),
        vm((8, OWNP), f32),
        vm((8, KL), jnp.int32),
        vm((8, PLP), f32),
        vm((DEGREE, PLP, ORB), bf16),
        vm((DEGREE, PL, ORB), bf16),
        vm((DEGREE, PLP, ORB), bf16),
        vm((DEGREE, PLP, ORB), bf16),
        vm((8, PLP), f32),
        vm((8, PLP), f32),
        vm((16, PLP), f32),
        vm((16, PLP), f32),
        vm((8, OWNP, ORB), bf16),
        vm((NRL, 256), bf16),
        vm((OWNP, ORB), bf16),
        vm((OWNP, ORB), f32),
        vm((3, 256, ORB), bf16),
        vm((3, 256, ORB), bf16),
        vm((256, ORB), f32),
        vm((256, ORB), f32),
        vm((256, ORB), bf16),
        vm((15, 16, ORB), bf16),
        vm((8, ORB), f32),
        vm((3, 8, ORB), f32),
        vm((8, ORB), f32),
        vm((15, 8, ORB), f32),
        dma(8), dma(8), dma(8), dma(8), dma(2), dma(2), dma(20), dma(8),
        dma(3), dma(3), dma(15), dma(15), dma(3), dma(3), dma(15), dma(15),
    ]
    return pl.pallas_call(
        kernel,
        out_shape=(
            jax.ShapeDtypeStruct((OWNED, ORB), bf16),
            jax.ShapeDtypeStruct((16, ORB), f32),
        ),
        in_specs=[vmem, vmem, vmem, smem, vmem, vmem, smem, vmem],
        out_specs=(vmem, vmem),
        scratch_shapes=scratch,
        compiler_params=pltpu.CompilerParams(
            collective_id=0, has_side_effects=True, vmem_limit_bytes=56 * 1024 * 1024
        ),
        cost_estimate=pl.CostEstimate(
            flops=4_000_000_000, bytes_accessed=1_000_000, transcendentals=128
        ),
    )(
        start_block, resident, cell_kernel, cell_scale, potential.reshape(1, OWNED), cell_nodes,
        cell_nodes, send_rows.reshape(1, PLANE),
    )


def solution(mesh):
    return jax.shard_map(
        per_device,
        mesh=mesh,
        in_specs=(
            P("domain", "band"),
            P("domain", "band"),
            P(),
            P("domain"),
            P("domain"),
            P("domain", None),
            P("domain"),
        ),
        out_specs=(P("domain", "band"), P("domain", "band")),
        check_vma=False,
    )
```

```python
import functools

import jax
import jax.numpy as jnp
from jax import lax
from jax.experimental import pallas as pl
from jax.experimental.pallas import tpu as pltpu
from jax.sharding import PartitionSpec as P

DEGREE = 8
EDGE = 7
ORB = 128
OWNED = 1014
PLANE = 169

lower_edge = 0.0
cutoff_edge = 16.0
upper_edge = 96.0
epsilon = 1e-06

NX = 13
XS = 112
NR = NX * XS
NRP = NR + 16
NRL = 1536
PL = 208
PLP = 256
MR = 392
KR = 448
KL = 384
OWNP = 1024

N_DOM = 64
N_ZH, N_X, N_Y = 2, 4, 8
N_ZL = 4

f32 = jnp.float32
bf16 = jnp.bfloat16
MESH = pl.DeviceIdType.MESH


def chebyshev_terms(degree):
    half_width = (upper_edge - cutoff_edge) / 2.0
    centre = (upper_edge + cutoff_edge) / 2.0
    sigma_now = half_width / (lower_edge - centre)
    gamma_ratio = 2.0 / sigma_now
    lead_factor = sigma_now / half_width
    recurrence = [(lead_factor, 0.0)]
    for _ in range(degree - 1):
        sigma_next = 1.0 / (gamma_ratio - sigma_now)
        recurrence.append((2.0 * sigma_next / half_width, sigma_now * sigma_next))
        sigma_now = sigma_next
    return (centre, recurrence)


CENTRE, TERMS = chebyshev_terms(DEGREE)


def mm(a, b):
    return jnp.dot(a, b, preferred_element_type=f32)


def mm_nt(a, b):
    return lax.dot_general(a, b, (((1,), (1,)), ((), ())), preferred_element_type=f32)


def mm_tn(a, b):
    return lax.dot_general(a, b, (((0,), (0,)), ((), ())), preferred_element_type=f32)


def iota(shape, dim):
    return lax.broadcasted_iota(jnp.int32, shape, dim)


def hot(cond):
    return jnp.where(cond, 1.0, 0.0).astype(bf16)


def pick(k, values):
    out = jnp.float32(values[0])
    for i in range(1, len(values)):
        out = jnp.where(k == i, jnp.float32(values[i]), out)
    return out


def kernel(
    start_ref, res_ref, ck_ref, scale_ref, pot_ref, cn_ref, cns_ref, sr_ref,
    out_ref, margin_ref,
    V, R, O, OG, part, potc, place, prow, Pm, PT, Q, st, kpad, K1, Kp, T, KgP, KttP, KgD,
    ET, F, W2, top_col, jbot_col, pot8, cnp, srp,
    R2, KgB, M1T, CR, Ps, Qs, Gs, cs, Gr, cr, Js, Jr, Us, Ur, RB, H2, LOW, CO, mpb, X1, M0, SF, SB, X2, N1s, N1r, N2s, N2r,
    g_send, g_recv, c_send, c_recv, j_sem, u_sem, r_send, r_recv, x1_send, x1_recv, x2_send, x2_recv,
    n1_send, n1_recv, n2_send, n2_recv,
):
    d = lax.axis_index("domain")
    band = lax.axis_index("band")
    zh = d // (N_X * N_Y)
    gx = (d // N_Y) % N_X
    gy = d % N_Y
    zl = band // 2
    core = band % 2
    sibling = zl * 2 + (1 - core)
    has_below = d > 0
    has_above = d < N_DOM - 1
    lower = d == N_DOM // N_ZH - 1
    upper = d == N_DOM // N_ZH

    Gr[...] = jnp.zeros_like(Gr)
    cr[...] = jnp.zeros_like(cr)
    Jr[...] = jnp.full(Jr.shape, -3.0, f32)
    Ur[0:8, :] = jnp.full((8, PLP), -4.0, f32)
    Ur[8:16, :] = jnp.zeros((8, PLP), f32)

    barrier = pltpu.get_barrier_semaphore()

    def greet(dom, bnd):
        pl.semaphore_signal(barrier, inc=1, device_id=(dom, bnd), device_id_type=MESH)

    x_peers = [(zh * N_X + (gx + i) % N_X) * N_Y + gy for i in range(1, N_X)]
    x_from = x_peers
    yz_off = [(a, b) for a in range(N_ZH) for b in range(N_Y) if (a, b) != (0, 0)]
    yz_peers = [
        (((zh + a) % N_ZH) * N_X + gx) * N_Y + (gy + b) % N_Y for a, b in yz_off
    ]

    @pl.when(has_below)
    def _():
        greet(d - 1, band)

    @pl.when(has_above)
    def _():
        greet(d + 1, band)

    @pl.when(zl > 0)
    def _():
        greet(d, band - 2)

    @pl.when(zl < N_ZL - 1)
    def _():
        greet(d, band + 2)

    greet(d, sibling)
    for p in x_peers + yz_peers:
        greet(p, band)

    corner = [cns_ref[c, 0] for c in range(4)]
    right_x = [cns_ref[c, EDGE - 1] for c in range(4)]
    right_y = [cns_ref[c, EDGE * (EDGE - 1)] for c in range(4)]
    pos = []
    for c in range(4):
        in_x = sum([jnp.where(right_x[b] == corner[c], 1, 0) for b in range(4)])
        in_y = sum([jnp.where(right_y[b] == corner[c], 1, 0) for b in range(4)])
        pos.append(in_x + 2 * in_y)
    scale = []
    for p in range(4):
        s = jnp.float32(0.0)
        for c in range(4):
            s = s + jnp.where(pos[c] == p, scale_ref[c], 0.0)
        scale.append(s)

    cnp[...] = jnp.zeros_like(cnp)
    cnp[0:4, 0:343] = cn_ref[...]
    row8 = iota((8, KL), 0)
    full = jnp.zeros((8, KL), jnp.int32)
    for c in range(4):
        line = jnp.broadcast_to(cnp[c : c + 1, :], (8, KL))
        full = full + jnp.where((row8 & 3) == pos[c], line, 0)
    cn8 = jnp.where(row8 < 4, full >> 5, full & 31).astype(f32).astype(bf16)

    rr = iota((XS, KL), 0)
    ln = iota((XS, KL), 1)
    yy = rr >> 3
    zz = rr & 7
    k_base = jnp.where(
        (zz < EDGE) & (yy < NX), zz * 49 + jnp.where(yy > 6, yy - 6, yy) * 7, -1000
    )
    diff = k_base - ln
    l8 = iota((XS, 8), 1)
    y8 = iota((XS, 8), 0) >> 3
    z128 = iota((XS, 128), 0) & 7
    y128 = iota((XS, 128), 0) >> 3
    top_row = (z128 < EDGE) & (y128 < NX)
    own_row = (z128 < EDGE - 1) & (y128 < NX)
    weights = jnp.where(iota((8, 128), 0) < 4, 32.0, 1.0).astype(bf16)
    lane = iota((XS, 128), 1).astype(f32)
    for X in range(NX):
        x = X if X <= 6 else X - 6
        one = hot(diff == -x)
        Q[X * XS : (X + 1) * XS, :] = one
        a1 = mm_nt(one, cn8)
        cell = jnp.where(y8 > 6, 2, 0) + (1 if X > 6 else 0)
        a1 = jnp.where((l8 & 3) == cell, a1, 0.0).astype(bf16)
        pl_x = mm(a1, weights)
        place[X * XS : (X + 1) * XS, :] = jnp.where(top_row, pl_x, -1.0)
        own = jnp.where(own_row, pl_x, -1.0)
        for t in range(8):
            Pm[X * XS : (X + 1) * XS, t * 128 : (t + 1) * 128] = hot(own == lane + 128.0 * t)
    place[NR:NRP, :] = jnp.full((NRP - NR, 128), -1.0, f32)

    srp[...] = jnp.full(srp.shape, -5.0, f32)
    srp[0:1, 0:PLANE] = sr_ref[...].astype(f32)
    top_col[...] = jnp.full(top_col.shape, -1.0, f32)
    yrow = iota((16, 128), 0)
    lane16 = iota((16, 128), 1)
    ET[...] = jnp.zeros_like(ET)
    for X in range(NX):
        b0 = jnp.concatenate(
            [place[pl.ds(X * XS, 8, stride=8), :], place[pl.ds(X * XS + 64, 8, stride=8), :]], 0
        )
        b0 = jnp.where(yrow < NX, b0, -1.0)
        for t in range(2):
            ET[X * 16 : X * 16 + 16, t * 128 : (t + 1) * 128] = hot(
                b0 == srp[0:1, t * 128 : (t + 1) * 128]
            )
        t0 = jnp.concatenate(
            [place[pl.ds(X * XS + 6, 8, stride=8), :], place[pl.ds(X * XS + 70, 8, stride=8), :]],
            0,
        )
        top_col[X * 16 : X * 16 + 16, :] = jnp.where(yrow < NX, t0 - float(OWNED), -1.0)
    jm = iota((PLP, 128), 0).astype(f32).astype(bf16)
    p_row = iota((PLP, 128), 0)
    jb = mm(ET[...], jm)
    jbot_col[...] = jnp.where(((p_row & 15) < NX) & (p_row < PL), jb, -2.0)
    p_lane = iota((8, PLP), 1)
    p_ok = ((p_lane & 15) < NX) & (p_lane < PL)
    jr = mm_nt(iota((8, PLP), 1).astype(f32).astype(bf16), ET[...])
    Js[...] = jnp.where(p_ok, jr, -2.0)

    pr = iota((PLP, KL), 0)
    pln = iota((PLP, KL), 1)
    pX = pr >> 4
    pY = pr & 15
    p_in = (pX < NX) & (pY < NX)
    ox = jnp.where(pX > 6, pX - 6, pX)
    oy = jnp.where(pY > 6, pY - 6, pY)
    q_top = hot(p_in & (294 + oy * 7 + ox == pln))
    at = mm_nt(cn8, q_top)
    lX = p_lane >> 4
    lY = p_lane & 15
    l_cell = jnp.where(lX > 6, 1, 0) + jnp.where(lY > 6, 2, 0)
    r8 = iota((8, PLP), 0)
    at = jnp.where((r8 & 3) == l_cell, at, 0.0) * jnp.where(r8 < 4, 32.0, 1.0)
    top_line = jnp.sum(at, 0, keepdims=True) - float(OWNED)
    Us[0:8, :] = jnp.where(p_ok, jnp.broadcast_to(top_line, (8, PLP)), -1.0)
    srow = iota((8, PLP), 0)
    stile = jnp.zeros((8, PLP), f32)
    for c in range(4):
        stile = jnp.where(srow == c, scale[c], stile)
    Us[8:16, :] = stile

    RB[band, 1008:1024, :] = jnp.zeros((16, ORB), bf16)
    RB[band, 0:OWNED, :] = res_ref[...]

    def remote(src, dst, ssem, rsem, dom, bnd):
        return pltpu.make_async_remote_copy(
            src_ref=src, dst_ref=dst, send_sem=ssem, recv_sem=rsem,
            device_id=(dom, bnd), device_id_type=MESH,
        )

    j_copy = remote(Js, Jr, j_sem.at[0], j_sem.at[1], d - 1, band)
    u_copy = remote(Us, Ur, u_sem.at[0], u_sem.at[1], d + 1, band)

    def block(src, to, s):
        return remote(RB.at[src], RB.at[src], r_send.at[s], r_recv.at[src], d, to)

    def send_own(start):
        def act(c):
            c.start() if start else c.wait_send()

        @pl.when(zl < N_ZL - 1)
        def _():
            act(block(band, band + 2, 0))

        @pl.when(zl > 0)
        def _():
            act(block(band, band - 2, 1))

        act(block(band, sibling, 2))

    def forward(dist, start):
        @pl.when(zl >= dist)
        def _():
            src = band - 2 * dist
            if start:
                block(src, sibling, 0).wait_recv()

            @pl.when(zl < N_ZL - 1)
            def _():
                c = block(src, band + 2, 3 * dist)
                c.start() if start else c.wait_send()

            c = block(src, sibling, 3 * dist + 1)
            c.start() if start else c.wait_send()

        @pl.when(zl + dist <= N_ZL - 1)
        def _():
            src = band + 2 * dist
            if start:
                block(src, sibling, 0).wait_recv()

            @pl.when(zl > 0)
            def _():
                c = block(src, band - 2, 9 + 3 * dist)
                c.start() if start else c.wait_send()

            c = block(src, sibling, 10 + 3 * dist)
            c.start() if start else c.wait_send()

    st[1008:1024, :] = jnp.zeros((16, ORB), bf16)
    st[0:OWNED, :] = start_ref[...]
    V[0, 0:NR, :] = mm(Pm[...], st[...])
    V[0, NR:NRP, :] = jnp.zeros((NRP - NR, ORB), f32)
    V[1, :, :] = jnp.zeros((NRP, ORB), f32)
    part[...] = jnp.zeros_like(part)
    zero8 = jnp.zeros((8, ORB), f32)
    for X in range(NX):
        R[X * 64 : X * 64 + 64, 0:128] = V[0, X * XS : X * XS + 64, :].astype(bf16)
        R[X * 64 : X * 64 + 64, 128:256] = V[0, X * XS + 48 : X * XS + 112, :].astype(bf16)

    kpad[...] = jnp.zeros_like(kpad)
    kpad[0:343, 0:343] = ck_ref[...]
    kmat = kpad[...]
    r56 = iota((56, KL), 0)
    k56 = jnp.where((r56 & 7) < 7, (r56 & 7) * 49 + (r56 >> 3) * 7, -1000) - iota((56, KL), 1)
    row_hot = jnp.concatenate([jnp.where(k56 == -x, 1.0, 0.0) for x in range(7)], 0).astype(bf16)
    r64 = iota((64, KL), 0)
    k64 = (
        jnp.where(((r64 & 7) < 7) & (r64 < 56), (r64 & 7) * 49 + (r64 >> 3) * 7, -1000)
        - iota((64, KL), 1)
    )
    col_hot = jnp.concatenate([hot(k64 == -x) for x in range(7)], 0)
    K1[...] = mm(row_hot, kmat).astype(bf16)
    Kp[...] = mm_nt(K1[...], col_hot).astype(bf16)
    r16 = iota((16, KL), 0)
    l16 = iota((16, KL), 1)
    for cy in range(2):
        y = r16 - 6 * cy
        kt = jnp.where((y >= 0) & (y < 7), 294 + y * 7, -1000) - l16
        t_hot = jnp.concatenate([hot(kt == -x) for x in range(7)], 0)
        T[cy] = mm_nt(mm(t_hot, kmat).astype(bf16), col_hot).astype(bf16)

    def down(k, src):
        return remote(
            src.at[k, pl.ds(0, PL)], Gr.at[k, pl.ds(0, PL)], g_send.at[k], g_recv.at[k], d - 1, band
        )

    def up(k, src):
        return remote(
            src.at[k, pl.ds(0, PL)], cr.at[k, pl.ds(0, PL)], c_send.at[k], c_recv.at[k], d + 1, band
        )

    def lowest_plane(v, out, k):
        for X in range(NX):
            lo = v[pl.ds(X * XS, 8, stride=8), :]
            hi = v[pl.ds(X * XS + 64, 8, stride=8), :]
            out[k, X * 16 : X * 16 + 16, :] = jnp.concatenate([lo, hi], 0).astype(bf16)

    def top_sums(r, sc):
        c0 = mm(T[0], r[0:KR, 0:128]) * sc[0] + mm(T[1], r[0:KR, 128:256]) * sc[2]
        c1 = mm(T[0], r[384 : 384 + KR, 0:128]) * sc[1]
        c1 = c1 + mm(T[1], r[384 : 384 + KR, 128:256]) * sc[3]
        return ((0, 96, c0[0:96]), (96, 112, c0[96:112] + c1[0:16]), (112, 208, c1[16:112]))

    def prepare_down(k, cur):
        Gs[k, PL:PLP, :] = jnp.zeros((PLP - PL, ORB), bf16)
        lowest_plane(V.at[cur], Gs, k)

    def prepare_up(k):
        cs[k, PL:PLP, :] = jnp.zeros((PLP - PL, ORB), bf16)
        for lo, hi, value in top_sums(R, scale):
            cs[k, lo:hi, :] = value.astype(bf16)

    def send_planes(k, cur):
        prepare_down(k, cur)

        @pl.when(has_below & jnp.logical_not(upper))
        def _():
            down(k, Gs).start()

        prepare_up(k)

        @pl.when(has_above & jnp.logical_not(lower))
        def _():
            up(k, cs).start()

    prepare_down(0, 0)
    prepare_up(0)

    ones = lambda cond: jnp.where(cond, 1, 0)
    count = (
        ones(has_below) + ones(has_above) + ones(zl > 0) + ones(zl < N_ZL - 1)
        + 1 + len(x_peers) + len(yz_peers)
    )
    pl.semaphore_wait(barrier, count)

    @pl.when(has_below)
    def _():
        down(0, Gs).start()

    @pl.when(has_above)
    def _():
        up(0, cs).start()

    @pl.when(has_below)
    def _():
        j_copy.start()

    @pl.when(has_above)
    def _():
        u_copy.start()

    send_own(True)

    pot8[...] = jnp.zeros_like(pot8)
    pot = pot_ref[...]
    p_hi = pot.astype(bf16)
    rest = pot - p_hi.astype(f32)
    p_mid = rest.astype(bf16)
    p_lo = (rest - p_mid.astype(f32)).astype(bf16)
    pot8[0:1, 0:OWNED] = p_hi.astype(f32)
    pot8[1:2, 0:OWNED] = p_mid.astype(f32)
    pot8[2:3, 0:OWNED] = p_lo.astype(f32)
    pcol = mm_nt(Pm[...], pot8[...].astype(bf16)).astype(bf16)
    potc[...] = mm(pcol, jnp.ones((8, 128), bf16)) - CENTRE

    for c in range(4):
        cx, cy = c % 2, c // 2
        x = pX - 6 * cx
        y = pY - 6 * cy
        inside = (x >= 0) & (x < 7) & (y >= 0) & (y < 7)
        c_top = hot(inside & (294 + y * 7 + x == pln))
        KgP[c] = mm_nt(K1[...], c_top).astype(bf16)
        KttP[c] = mm_nt(mm(c_top, kmat).astype(bf16), c_top)

    lin = iota((8, NRL), 1)
    lin_x = jnp.floor((lin.astype(f32) + 0.5) * (1.0 / XS)).astype(jnp.int32)
    lin_r = lin - lin_x * XS
    lin_y = lin_r >> 3
    lin_z = lin_r & 7
    lin_cell = jnp.where(lin_x > 6, 1, 0) + jnp.where(lin_y > 6, 2, 0)
    lin_8 = iota((8, NRL), 0)
    Q[NR:NRL, :] = jnp.zeros((NRL - NR, KL), bf16)
    ar = mm_nt(cn8, Q[...])
    ar = jnp.where((lin_8 & 3) == lin_cell, ar, 0.0) * jnp.where(lin_8 < 4, 32.0, 1.0)
    ar = jnp.broadcast_to(jnp.sum(ar, 0, keepdims=True), (8, NRL))
    prow[...] = jnp.where((lin_x < NX) & (lin_y < NX) & (lin_z < EDGE - 1), ar, -1.0)
    n16 = iota((16, NRL), 0).astype(f32)

    def fill(i, carry):
        base = (i * 16).astype(f32)
        PT[pl.ds(pl.multiple_of(i * 16, 16), 16), :] = hot(prow[0:1, :] == n16 + base)
        return carry

    lax.fori_loop(0, OWNP // 16, fill, 0)

    @pl.when(has_above)
    def _():
        j_copy.wait_recv()

    @pl.when(has_below)
    def _():
        u_copy.wait_recv()

    tc = top_col[...]
    jc = jbot_col[...]
    m1 = jnp.concatenate([hot(tc == Jr[0:1, t * 128 : (t + 1) * 128]) for t in range(2)], 1)
    F[...] = jnp.concatenate([hot(jc == Ur[0:1, t * 128 : (t + 1) * 128]) for t in range(2)], 1)
    for c in range(4):
        KgD[c] = mm(KgP[c], m1).astype(bf16)
    w = jnp.zeros((PLP, PLP), f32)
    for c in range(4):
        w = w + KttP[c] * Ur[8 + c : 9 + c, :]
    w_hi = w.astype(bf16)
    w_lo = (w - w_hi.astype(f32)).astype(bf16)
    fm = F[...]
    @pl.when(lower)
    def _():
        eye = hot(iota((PLP, PLP), 0) == iota((PLP, PLP), 1))
        M1T[...] = mm_nt(eye, m1).astype(bf16)

    @pl.when(upper)
    def _():
        for c in range(4):
            KgB[c] = mm_nt(KgP[c], F[...]).astype(bf16)

    W2[0] = mm_nt(mm(fm, w_hi).astype(bf16), fm).astype(bf16)
    W2[1] = mm_nt(mm(fm, w_lo).astype(bf16), fm).astype(bf16)

    mask8 = jnp.where(iota((8, ORB), 0) < EDGE - 1, 1.0, 0.0)

    def spread(ref_of, X, factor):
        lo, hi = None, None
        for cx in range(2):
            x = X - 6 * cx
            if 0 <= x < 7:
                a = ref_of(cx, 0, x).reshape(7, 8, ORB) * factor(cx, 0)
                b = ref_of(cx, 1, x).reshape(7, 8, ORB) * factor(cx, 1)
                lo = a if lo is None else lo + a
                hi = b if hi is None else hi + b
        return jnp.concatenate([lo[0:6], lo[6:7] + hi[0:1], hi[1:7]], 0)

    def bulk(k, cur):
        nxt = 1 - cur
        a = pick(k, [t[0] for t in TERMS])
        b = pick(k, [t[1] for t in TERMS])
        am = mask8 * a
        for cx in range(2):
            O[cx] = mm(Kp[...], R[384 * cx : 384 * cx + KR, :])
        for X in range(NX):
            rows = slice(X * XS, X * XS + 104)
            s = spread(
                lambda cx, cy, x: O[cx, x * 56 : x * 56 + 56, cy * 128 : (cy + 1) * 128],
                X,
                lambda cx, cy: scale[cx + 2 * cy],
            )
            v = V[cur, rows, :].reshape(NX, 8, ORB)
            u = V[nxt, rows, :].reshape(NX, 8, ORB)
            pc = potc[rows, :].reshape(NX, 8, ORB)
            new = (s + pc * v) * am[None] - b * u
            part[rows, :] = new.reshape(104, ORB)
        g = Gs[k]
        return (mm(W2[0], g) + mm(W2[1], g)) * a

    def add_plane(v, e):
        for X in range(NX):
            lo = pl.ds(X * XS, 8, stride=8)
            hi = pl.ds(X * XS + 64, 8, stride=8)
            v[lo, :] = v[lo, :] + e[X * 16 : X * 16 + 8]
            v[hi, :] = v[hi, :] + e[X * 16 + 8 : X * 16 + 16]

    def to_operand(r, X, flat):
        r[X * 64 : X * 64 + 64, 0:128] = flat[0:64].astype(bf16)
        r[X * 64 : X * 64 + 64, 128:256] = jnp.concatenate([flat[48:104], zero8], 0).astype(bf16)

    def ghost(X, am, sc):
        return spread(
            lambda cx, cy, x: OG[cx + 2 * cy, x * 56 : x * 56 + 56, :],
            X,
            lambda cx, cy: (am * sc[cx + 2 * cy])[None],
        )

    def ahead(k):
        am = mask8 * pick(k - 1, [t[0] for t in TERMS])
        sb = [Ur[8 + c : 9 + c, 0:128] for c in range(4)]
        for c in range(4):
            OG[c] = mm(KgB[c], Gs[k - 1])
        for X in range(NX):
            to_operand(R2, X, ghost(X, am, sb).reshape(104, ORB))
        for lo, hi, value in top_sums(R2, sb):
            CR[lo:hi, :] = value

    def finish(k, cur, plane, last):
        nxt = 1 - cur
        a = pick(k, [t[0] for t in TERMS])
        am = mask8 * a

        @pl.when(upper)
        def _():
            add_plane(part, plane)

        @pl.when(jnp.logical_not(upper))
        def _():
            @pl.when(has_below)
            def _():
                up(k, cs).wait_recv()

            add_plane(part, plane + mm(F[...], cr[k]) * a)

        if not last:

            @pl.when(lower)
            def _():
                for X in range(NX):
                    to_operand(R2, X, part[X * XS : X * XS + 104, :])
                for lo, hi, value in top_sums(R2, scale):
                    Ps[k + 1, lo:hi, :] = value.astype(bf16)
                up(k + 1, Ps).start()

        @pl.when(has_above)
        def _():
            down(k, Gs).wait_recv()

        @pl.when(lower & (k >= 1))
        def _():
            before = pick(k - 1, [t[0] for t in TERMS])
            Gr[k] = (Gr[k].astype(f32) + mm(M1T[...], cs[k - 1]) * before).astype(bf16)

        for c in range(4):
            OG[c] = mm(KgD[c], Gr[k])
        for X in range(NX):
            rows = slice(X * XS, X * XS + 104)
            new = part[rows, :].reshape(NX, 8, ORB) + ghost(X, am, scale)
            flat = new.reshape(104, ORB)
            V[nxt, rows, :] = flat
            if not last:
                to_operand(R, X, flat)

        @pl.when(upper)
        def _():
            if not last:
                lowest_plane(V.at[nxt], Qs, k + 1)
                down(k + 1, Qs).start()
            up(k, cs).wait_recv()

            @pl.when(k >= 1)
            def _():
                cr[k, 0:PL, :] = (cr[k, 0:PL, :].astype(f32) + CR[...]).astype(bf16)

            add_plane(V.at[nxt], mm(F[...], cr[k]) * a)
            if not last:
                for X in range(NX):
                    to_operand(R, X, V[nxt, X * XS : X * XS + 104, :])

        if not last:
            return None
        sq = jnp.zeros((8, ORB), f32)
        for X in range(NX):
            padded = V[nxt, X * XS : (X + 1) * XS, :]
            cube = padded.reshape(NX + 1, 8, ORB)
            sq = sq + jnp.sum(cube * cube, 0)
            top = padded.astype(bf16)
            H2[X * XS : (X + 1) * XS, 0:128] = top
            H2[X * XS : (X + 1) * XS, 128:256] = (padded - top.astype(f32)).astype(bf16)
        return sq

    def step(k, carry):
        cur = lax.rem(k, 2)
        plane = bulk(k, cur)

        @pl.when(upper & (k >= 1))
        def _():
            ahead(k)

        @pl.when(k == 3)
        def _():
            forward(1, True)

        @pl.when(k == 5)
        def _():
            forward(2, True)

        finish(k, cur, plane, False)
        send_planes(k + 1, 1 - cur)
        return carry

    lax.fori_loop(0, DEGREE - 1, step, 0)
    final = DEGREE - 1
    plane = bulk(final, final % 2)

    @pl.when(upper)
    def _():
        ahead(final)

    forward(3, True)
    H2[NR:NRL, :] = jnp.zeros((NRL - NR, 256), bf16)
    sq = finish(final, final % 2, plane, True)

    N1s[...] = jnp.broadcast_to(jnp.sum(sq, 0, keepdims=True), (8, ORB))

    def n1(i):
        return remote(N1s, N1r.at[i], n1_send.at[i], n1_recv.at[i], x_peers[i], band)

    for i in range(3):
        n1(i).start()

    un = mm(PT[...], H2[...])
    LOW[...] = un[:, 0:128].astype(bf16)
    CO[...] = un[:, 0:128] + un[:, 128:256]

    for i in range(N_ZL):
        src = i * 2 + (1 - core)
        block(src, sibling, 0).wait_recv()

    def x1(i):
        return remote(mpb.at[i], X1.at[i], x1_send.at[i], x1_recv.at[i], x_peers[i], band)

    for i in range(4):
        tx = (gx + 1 + i) % N_X
        for h in range(N_ZH):
            m = mm_tn(RB[h * N_X + tx], LOW[...])
            if i < 3:
                mpb[i, h * 128 : (h + 1) * 128, :] = m.astype(bf16)
            else:
                M0[h * 128 : (h + 1) * 128, :] = m
        if i < 3:
            x1(i).start()

    for i in range(3):
        n1(i).wait_recv()
    N2s[...] = N1s[...] + N1r[0] + N1r[1] + N1r[2]

    def n2(i):
        return remote(N2s, N2r.at[i], n2_send.at[i], n2_recv.at[i], yz_peers[i], band)

    for i in range(15):
        n2(i).start()

    acc = M0[...]
    for i in range(3):
        x1(i).wait_recv()
        acc = acc + X1[i].astype(f32)
    SF[...] = acc
    SB[...] = acc.astype(bf16)

    def x2(i):
        a, b = yz_off[i]
        row = (((zh + a) % N_ZH) * N_Y + (gy + b) % N_Y) * 16
        return remote(
            SB.at[pl.ds(pl.multiple_of(row, 16), 16)], X2.at[i], x2_send.at[i], x2_recv.at[i],
            yz_peers[i], band,
        )

    for i in range(15):
        x2(i).start()

    total = N2s[...]
    for i in range(15):
        n2(i).wait_recv()
        total = total + N2r[i]
    inverse = lax.rsqrt(total[0:1, :] + epsilon)
    out_ref[...] = (CO[...] * inverse)[0:OWNED].astype(bf16)

    m = SF[pl.ds(pl.multiple_of((zh * N_Y + gy) * 16, 16), 16), :]
    for i in range(15):
        x2(i).wait_recv()
        m = m + X2[i].astype(f32)
    margin_ref[...] = m * inverse

    @pl.when(has_below)
    def _():
        j_copy.wait_send()

    @pl.when(has_above)
    def _():
        u_copy.wait_send()

    def sent(k, carry):
        @pl.when(has_below)
        def _():
            down(k, Gs).wait_send()

        @pl.when(has_above)
        def _():
            up(k, cs).wait_send()

        return carry

    lax.fori_loop(0, DEGREE, sent, 0)
    send_own(False)
    for dist in range(1, N_ZL):
        forward(dist, False)
    for i in range(3):
        n1(i).wait_send()
        x1(i).wait_send()
    for i in range(15):
        n2(i).wait_send()
        x2(i).wait_send()


def per_device(start_block, resident, cell_kernel, cell_scale, potential, cell_nodes, send_rows):
    vm = lambda shape, t: pltpu.VMEM(shape, t)
    dma = lambda n: pltpu.SemaphoreType.DMA((n,))
    vmem = pl.BlockSpec(memory_space=pltpu.VMEM)
    smem = pl.BlockSpec(memory_space=pltpu.SMEM)
    scratch = [
        vm((2, NRP, ORB), f32),
        vm((832, 256), bf16),
        vm((2, MR, 256), f32),
        vm((4, MR, ORB), f32),
        vm((NRP, ORB), f32),
        vm((NR, ORB), f32),
        vm((NRP, ORB), f32),
        vm((8, NRL), f32),
        vm((NR, OWNP), bf16),
        vm((OWNP, NRL), bf16),
        vm((NRL, KL), bf16),
        vm((OWNP, ORB), bf16),
        vm((KL, KL), bf16),
        vm((MR, KL), bf16),
        vm((MR, KR), bf16),
        vm((2, 112, KR), bf16),
        vm((4, MR, PLP), bf16),
        vm((4, PLP, PLP), f32),
        vm((4, MR, PLP), bf16),
        vm((PLP, PLP), bf16),
        vm((PLP, PLP), bf16),
        vm((2, PLP, PLP), bf16),
        vm((PLP, ORB), f32),
        vm((PLP, ORB), f32),
        vm((8, OWNP), f32),
        vm((8, KL), jnp.int32),
        vm((8, PLP), f32),
        vm((832, 256), bf16),
        vm((4, MR, PLP), bf16),
        vm((PLP, PLP), bf16),
        vm((PL, ORB), f32),
        vm((DEGREE, PL, ORB), bf16),
        vm((DEGREE, PL, ORB), bf16),
        vm((DEGREE, PLP, ORB), bf16),
        vm((DEGREE, PLP, ORB), bf16),
        vm((DEGREE, PLP, ORB), bf16),
        vm((DEGREE, PLP, ORB), bf16),
        vm((8, PLP), f32),
        vm((8, PLP), f32),
        vm((16, PLP), f32),
        vm((16, PLP), f32),
        vm((8, OWNP, ORB), bf16),
        vm((NRL, 256), bf16),
        vm((OWNP, ORB), bf16),
        vm((OWNP, ORB), f32),
        vm((3, 256, ORB), bf16),
        vm((3, 256, ORB), bf16),
        vm((256, ORB), f32),
        vm((256, ORB), f32),
        vm((256, ORB), bf16),
        vm((15, 16, ORB), bf16),
        vm((8, ORB), f32),
        vm((3, 8, ORB), f32),
        vm((8, ORB), f32),
        vm((15, 8, ORB), f32),
        dma(8), dma(8), dma(8), dma(8), dma(2), dma(2), dma(20), dma(8),
        dma(3), dma(3), dma(15), dma(15), dma(3), dma(3), dma(15), dma(15),
    ]
    return pl.pallas_call(
        kernel,
        out_shape=(
            jax.ShapeDtypeStruct((OWNED, ORB), bf16),
            jax.ShapeDtypeStruct((16, ORB), f32),
        ),
        in_specs=[vmem, vmem, vmem, smem, vmem, vmem, smem, vmem],
        out_specs=(vmem, vmem),
        scratch_shapes=scratch,
        compiler_params=pltpu.CompilerParams(
            collective_id=0, has_side_effects=True, vmem_limit_bytes=56 * 1024 * 1024
        ),
        cost_estimate=pl.CostEstimate(
            flops=4_000_000_000, bytes_accessed=1_000_000, transcendentals=128
        ),
    )(
        start_block, resident, cell_kernel, cell_scale, potential.reshape(1, OWNED), cell_nodes,
        cell_nodes, send_rows.reshape(1, PLANE),
    )


def solution(mesh):
    return jax.shard_map(
        per_device,
        mesh=mesh,
        in_specs=(
            P("domain", "band"),
            P("domain", "band"),
            P(),
            P("domain"),
            P("domain"),
            P("domain", None),
            P("domain"),
        ),
        out_specs=(P("domain", "band"), P("domain", "band")),
        check_vma=False,
    )
```

```python
import functools

import jax
import jax.numpy as jnp
from jax import lax
from jax.experimental import pallas as pl
from jax.experimental.pallas import tpu as pltpu
from jax.sharding import PartitionSpec as P

DEGREE = 8
EDGE = 7
ORB = 128
OWNED = 1014
PLANE = 169

lower_edge = 0.0
cutoff_edge = 16.0
upper_edge = 96.0
epsilon = 1e-06

NX = 13
XS = 112
NR = NX * XS
NRP = NR + 16
NRL = 1536
PL = 208
PLP = 256
MR = 392
KR = 448
KL = 384
OWNP = 1024

N_DOM = 64
N_ZH, N_X, N_Y = 2, 4, 8
N_ZL = 4

f32 = jnp.float32
bf16 = jnp.bfloat16
MESH = pl.DeviceIdType.MESH


def chebyshev_terms(degree):
    half_width = (upper_edge - cutoff_edge) / 2.0
    centre = (upper_edge + cutoff_edge) / 2.0
    sigma_now = half_width / (lower_edge - centre)
    gamma_ratio = 2.0 / sigma_now
    lead_factor = sigma_now / half_width
    recurrence = [(lead_factor, 0.0)]
    for _ in range(degree - 1):
        sigma_next = 1.0 / (gamma_ratio - sigma_now)
        recurrence.append((2.0 * sigma_next / half_width, sigma_now * sigma_next))
        sigma_now = sigma_next
    return (centre, recurrence)


CENTRE, TERMS = chebyshev_terms(DEGREE)


def mm(a, b):
    return jnp.dot(a, b, preferred_element_type=f32)


def mm_nt(a, b):
    return lax.dot_general(a, b, (((1,), (1,)), ((), ())), preferred_element_type=f32)


def mm_tn(a, b):
    return lax.dot_general(a, b, (((0,), (0,)), ((), ())), preferred_element_type=f32)


def iota(shape, dim):
    return lax.broadcasted_iota(jnp.int32, shape, dim)


def hot(cond):
    return jnp.where(cond, 1.0, 0.0).astype(bf16)


def pick(k, values):
    out = jnp.float32(values[0])
    for i in range(1, len(values)):
        out = jnp.where(k == i, jnp.float32(values[i]), out)
    return out


def kernel(
    start_hbm, res_hbm, ck_hbm, scale_hbm, pot_hbm, cn_hbm, sr_hbm,
    out_ref, margin_ref,
    start_ref, res_ref, ck_ref, scale_ref, pot_ref, cn_ref, cns_ref, sr_ref, OUT,
    V, R, O, OG, part, potc, place, prow, Pm, PT, Q, st, kpad, K1, Kp, T, KgP, KttP, KgD,
    ET, F, W2, top_col, jbot_col, pot8, cnp, srp,
    RBT, R2, KgB, M1T, D2, CR, CR2, Ps, Qs, Gs, cs, Gr, cr, Js, Jr, Us, Ur, RB, H2, LOW, CO, mpb, X1, M0, SF, SB, X2, N1s, N1r, N2s, N2r,
    g_send, g_recv, c_send, c_recv, j_sem, u_sem, r_send, r_recv, x1_send, x1_recv, x2_send, x2_recv,
    n1_send, n1_recv, n2_send, n2_recv, in_sem, out_sem,
):
    d = lax.axis_index("domain")
    band = lax.axis_index("band")
    zh = d // (N_X * N_Y)
    gx = (d // N_Y) % N_X
    gy = d % N_Y
    zl = band // 2
    core = band % 2
    sibling = zl * 2 + (1 - core)
    has_below = d > 0
    has_above = d < N_DOM - 1
    mid = N_DOM // N_ZH
    end_y = has_above & (d % N_Y == N_Y - 1)
    first_y = has_below & (d % N_Y == 0)
    up_early = end_y | (d == mid - 2)
    up_mend = first_y | (d == mid - 1)
    down_early = first_y | (d == mid + 1)
    down_mend = end_y | (d == mid)

    given = [
        (cn_hbm, cns_ref), (cn_hbm, cn_ref), (scale_hbm, scale_ref), (sr_hbm, sr_ref),
        (start_hbm, start_ref), (ck_hbm, ck_ref), (res_hbm, res_ref), (pot_hbm, pot_ref),
    ]
    given = [pltpu.make_async_copy(a, b, in_sem.at[i]) for i, (a, b) in enumerate(given)]
    for c in given:
        c.start()

    Gr[...] = jnp.zeros_like(Gr)
    cr[...] = jnp.zeros_like(cr)
    Jr[...] = jnp.full(Jr.shape, -3.0, f32)
    Ur[0:8, :] = jnp.full((8, PLP), -4.0, f32)
    Ur[8:16, :] = jnp.zeros((8, PLP), f32)

    barrier = pltpu.get_barrier_semaphore()

    def greet(dom, bnd):
        pl.semaphore_signal(barrier, inc=1, device_id=(dom, bnd), device_id_type=MESH)

    x_peers = [(zh * N_X + (gx + i) % N_X) * N_Y + gy for i in range(1, N_X)]
    x_from = x_peers
    yz_off = [(a, b) for a in range(N_ZH) for b in range(N_Y) if (a, b) != (0, 0)]
    yz_peers = [
        (((zh + a) % N_ZH) * N_X + gx) * N_Y + (gy + b) % N_Y for a, b in yz_off
    ]

    for p in yz_peers[::-1] + x_peers:
        greet(p, band)

    @pl.when(has_below)
    def _():
        greet(d - 1, band)

    @pl.when(has_above)
    def _():
        greet(d + 1, band)

    @pl.when(zl > 0)
    def _():
        greet(d, band - 2)

    @pl.when(zl < N_ZL - 1)
    def _():
        greet(d, band + 2)

    greet(d, sibling)

    for c in given[0:3]:
        c.wait()
    corner = [cns_ref[c, 0] for c in range(4)]
    right_x = [cns_ref[c, EDGE - 1] for c in range(4)]
    right_y = [cns_ref[c, EDGE * (EDGE - 1)] for c in range(4)]
    pos = []
    for c in range(4):
        in_x = sum([jnp.where(right_x[b] == corner[c], 1, 0) for b in range(4)])
        in_y = sum([jnp.where(right_y[b] == corner[c], 1, 0) for b in range(4)])
        pos.append(in_x + 2 * in_y)
    scale = []
    for p in range(4):
        s = jnp.float32(0.0)
        for c in range(4):
            s = s + jnp.where(pos[c] == p, scale_ref[c], 0.0)
        scale.append(s)

    cnp[...] = jnp.zeros_like(cnp)
    cnp[0:4, 0:343] = cn_ref[...]
    row8 = iota((8, KL), 0)
    full = jnp.zeros((8, KL), jnp.int32)
    for c in range(4):
        line = jnp.broadcast_to(cnp[c : c + 1, :], (8, KL))
        full = full + jnp.where((row8 & 3) == pos[c], line, 0)
    cn8 = jnp.where(row8 < 4, full >> 5, full & 31).astype(f32).astype(bf16)

    rr = iota((XS, KL), 0)
    ln = iota((XS, KL), 1)
    yy = rr >> 3
    zz = rr & 7
    k_base = jnp.where(
        (zz < EDGE) & (yy < NX), zz * 49 + jnp.where(yy > 6, yy - 6, yy) * 7, -1000
    )
    diff = k_base - ln
    l8 = iota((XS, 8), 1)
    y8 = iota((XS, 8), 0) >> 3
    z128 = iota((XS, 128), 0) & 7
    y128 = iota((XS, 128), 0) >> 3
    top_row = (z128 < EDGE) & (y128 < NX)
    own_row = (z128 < EDGE - 1) & (y128 < NX)
    weights = jnp.where(iota((8, 128), 0) < 4, 32.0, 1.0).astype(bf16)
    lane = iota((XS, 128), 1).astype(f32)
    for X in range(NX):
        x = X if X <= 6 else X - 6
        one = hot(diff == -x)
        Q[X * XS : (X + 1) * XS, :] = one
        a1 = mm_nt(one, cn8)
        cell = jnp.where(y8 > 6, 2, 0) + (1 if X > 6 else 0)
        a1 = jnp.where((l8 & 3) == cell, a1, 0.0).astype(bf16)
        pl_x = mm(a1, weights)
        place[X * XS : (X + 1) * XS, :] = jnp.where(top_row, pl_x, -1.0)
        own = jnp.where(own_row, pl_x, -1.0)
        for t in range(8):
            Pm[X * XS : (X + 1) * XS, t * 128 : (t + 1) * 128] = hot(own == lane + 128.0 * t)
    place[NR:NRP, :] = jnp.full((NRP - NR, 128), -1.0, f32)

    given[3].wait()
    srp[...] = jnp.full(srp.shape, -5.0, f32)
    srp[0:1, 0:PLANE] = sr_ref[...].astype(f32)
    top_col[...] = jnp.full(top_col.shape, -1.0, f32)
    yrow = iota((16, 128), 0)
    lane16 = iota((16, 128), 1)
    ET[...] = jnp.zeros_like(ET)
    for X in range(NX):
        b0 = jnp.concatenate(
            [place[pl.ds(X * XS, 8, stride=8), :], place[pl.ds(X * XS + 64, 8, stride=8), :]], 0
        )
        b0 = jnp.where(yrow < NX, b0, -1.0)
        for t in range(2):
            ET[X * 16 : X * 16 + 16, t * 128 : (t + 1) * 128] = hot(
                b0 == srp[0:1, t * 128 : (t + 1) * 128]
            )
        t0 = jnp.concatenate(
            [place[pl.ds(X * XS + 6, 8, stride=8), :], place[pl.ds(X * XS + 54, 8, stride=8), :]],
            0,
        )
        top_col[X * 16 : X * 16 + 16, :] = jnp.where((yrow & 7) < EDGE, t0 - float(OWNED), -1.0)
    jm = iota((PLP, 128), 0).astype(f32).astype(bf16)
    p_row = iota((PLP, 128), 0)
    jb = mm(ET[...], jm)
    jbot_col[...] = jnp.where(((p_row & 15) < NX) & (p_row < PL), jb, -2.0)
    p_lane = iota((8, PLP), 1)
    p_ok = ((p_lane & 15) < NX) & (p_lane < PL)
    jr = mm_nt(iota((8, PLP), 1).astype(f32).astype(bf16), ET[...])
    Js[...] = jnp.where(p_ok, jr, -2.0)

    pr = iota((PLP, KL), 0)
    pln = iota((PLP, KL), 1)
    pX = pr >> 4
    pY = pr & 15
    ty = pr & 7
    tcy = (pr >> 3) & 1
    t_in = (pX < NX) & (ty < EDGE)
    ox = jnp.where(pX > 6, pX - 6, pX)
    q_top = hot(t_in & (294 + ty * 7 + ox == pln))
    at = mm_nt(cn8, q_top)
    lX = p_lane >> 4
    l_cell = jnp.where(lX > 6, 1, 0) + ((p_lane >> 3) & 1) * 2
    t_ok = ((p_lane & 7) < EDGE) & (p_lane < PL)
    r8 = iota((8, PLP), 0)
    at = jnp.where((r8 & 3) == l_cell, at, 0.0) * jnp.where(r8 < 4, 32.0, 1.0)
    top_line = jnp.sum(at, 0, keepdims=True) - float(OWNED)
    Us[0:8, :] = jnp.where(t_ok, jnp.broadcast_to(top_line, (8, PLP)), -1.0)
    srow = iota((8, PLP), 0)
    stile = jnp.zeros((8, PLP), f32)
    for c in range(4):
        stile = jnp.where(srow == c, scale[c], stile)
    Us[8:16, :] = stile

    given[6].wait()
    RB[band, 1008:1024, :] = jnp.zeros((16, ORB), bf16)
    RB[band, 0:OWNED, :] = res_ref[...]

    def remote(src, dst, ssem, rsem, dom, bnd):
        return pltpu.make_async_remote_copy(
            src_ref=src, dst_ref=dst, send_sem=ssem, recv_sem=rsem,
            device_id=(dom, bnd), device_id_type=MESH,
        )

    j_copy = remote(Js, Jr, j_sem.at[0], j_sem.at[1], d - 1, band)
    u_copy = remote(Us, Ur, u_sem.at[0], u_sem.at[1], d + 1, band)

    def turn(dist):
        if dist == 0:
            block(sibling, sibling, 0).wait_recv()
            RBT[band] = RB[band].T
            RBT[sibling] = RB[sibling].T
            return

        def both(src):
            other = src + 1 - 2 * core
            block(other, sibling, 0).wait_recv()
            RBT[src] = RB[src].T
            RBT[other] = RB[other].T

        @pl.when(zl >= dist)
        def _():
            both(band - 2 * dist)

        @pl.when(zl + dist <= N_ZL - 1)
        def _():
            both(band + 2 * dist)

    def block(src, to, s):
        return remote(RB.at[src], RB.at[src], r_send.at[s], r_recv.at[src], d, to)

    def send_own(start):
        def act(c):
            c.start() if start else c.wait_send()

        @pl.when(zl < N_ZL - 1)
        def _():
            act(block(band, band + 2, 0))

        @pl.when(zl > 0)
        def _():
            act(block(band, band - 2, 1))

        act(block(band, sibling, 2))

    def forward(dist, start):
        @pl.when(zl >= dist)
        def _():
            src = band - 2 * dist
            if start:
                block(src, sibling, 0).wait_recv()

            @pl.when(zl < N_ZL - 1)
            def _():
                c = block(src, band + 2, 3 * dist)
                c.start() if start else c.wait_send()

            c = block(src, sibling, 3 * dist + 1)
            c.start() if start else c.wait_send()

        @pl.when(zl + dist <= N_ZL - 1)
        def _():
            src = band + 2 * dist
            if start:
                block(src, sibling, 0).wait_recv()

            @pl.when(zl > 0)
            def _():
                c = block(src, band - 2, 9 + 3 * dist)
                c.start() if start else c.wait_send()

            c = block(src, sibling, 10 + 3 * dist)
            c.start() if start else c.wait_send()

    given[4].wait()
    st[1008:1024, :] = jnp.zeros((16, ORB), bf16)
    st[0:OWNED, :] = start_ref[...]
    V[0, 0:NR, :] = mm(Pm[...], st[...])
    V[0, NR:NRP, :] = jnp.zeros((NRP - NR, ORB), f32)
    V[1, :, :] = jnp.zeros((NRP, ORB), f32)
    part[...] = jnp.zeros_like(part)
    zero8 = jnp.zeros((8, ORB), f32)
    for X in range(NX):
        R[X * 64 : X * 64 + 64, 0:128] = V[0, X * XS : X * XS + 64, :].astype(bf16)
        R[X * 64 : X * 64 + 64, 128:256] = V[0, X * XS + 48 : X * XS + 112, :].astype(bf16)

    given[5].wait()
    kpad[...] = jnp.zeros_like(kpad)
    kpad[0:343, 0:343] = ck_ref[...]
    kmat = kpad[...]
    r56 = iota((56, KL), 0)
    k56 = jnp.where((r56 & 7) < 7, (r56 & 7) * 49 + (r56 >> 3) * 7, -1000) - iota((56, KL), 1)
    row_hot = jnp.concatenate([jnp.where(k56 == -x, 1.0, 0.0) for x in range(7)], 0).astype(bf16)
    r64 = iota((64, KL), 0)
    k64 = (
        jnp.where(((r64 & 7) < 7) & (r64 < 56), (r64 & 7) * 49 + (r64 >> 3) * 7, -1000)
        - iota((64, KL), 1)
    )
    col_hot = jnp.concatenate([hot(k64 == -x) for x in range(7)], 0)
    K1[...] = mm(row_hot, kmat).astype(bf16)
    Kp[...] = mm_nt(K1[...], col_hot).astype(bf16)
    r8k = iota((8, KL), 0)
    l8k = iota((8, KL), 1)
    kt = jnp.where(r8k < EDGE, 294 + r8k * 7, -1000) - l8k
    kb = jnp.where(r8k < EDGE, r8k * 7, -1000) - l8k
    none8 = jnp.zeros((8, KL), f32)
    t_hot = jnp.concatenate([jnp.where(kt == -x, 1.0, 0.0) for x in range(7)] + [none8], 0).astype(bf16)
    b_hot = jnp.concatenate([jnp.where(kb == -x, 1.0, 0.0) for x in range(7)] + [none8], 0).astype(bf16)
    top_k = mm(t_hot, kmat).astype(bf16)
    T[...] = mm_nt(top_k, col_hot)[0:56].astype(bf16)

    def down(k, src):
        return remote(
            src.at[k, pl.ds(0, PL)], Gr.at[k, pl.ds(0, PL)], g_send.at[k], g_recv.at[k], d - 1, band
        )

    def up(k, src):
        return remote(
            src.at[k, pl.ds(0, PL)], cr.at[k, pl.ds(0, PL)], c_send.at[k], c_recv.at[k], d + 1, band
        )

    def lowest_plane(v, out, k, more=None):
        for X in range(NX):
            lo = v[pl.ds(X * XS, 8, stride=8), :]
            hi = v[pl.ds(X * XS + 64, 8, stride=8), :]
            both = jnp.concatenate([lo, hi], 0)
            if more is not None:
                both = both + more[X * 16 : X * 16 + 16]
            out[k, X * 16 : X * 16 + 16, :] = both.astype(bf16)

    def top_sums(r, sc):
        parts = [mm(T[...], r[384 * cx : 384 * cx + KR, :]) for cx in range(2)]
        out = []
        for X in range(NX):
            tiles = []
            for cy in range(2):
                t = None
                for cx in range(2):
                    x = X - 6 * cx
                    if 0 <= x < 7:
                        p = parts[cx][x * 8 : x * 8 + 8, cy * 128 : (cy + 1) * 128] * sc[cx + 2 * cy]
                        t = p if t is None else t + p
                tiles.append(t)
            out.append((X * 16, X * 16 + 16, jnp.concatenate(tiles, 0)))
        return out

    def prepare_down(k, cur):
        Gs[k, PL:PLP, :] = jnp.zeros((PLP - PL, ORB), bf16)
        lowest_plane(V.at[cur], Gs, k)

    def prepare_up(k):
        cs[k, PL:PLP, :] = jnp.zeros((PLP - PL, ORB), bf16)
        for lo, hi, value in top_sums(R, scale):
            cs[k, lo:hi, :] = value.astype(bf16)

    def to_operand(r, X, flat):
        r[X * 64 : X * 64 + 64, 0:128] = flat[0:64].astype(bf16)
        r[X * 64 : X * 64 + 64, 128:256] = jnp.concatenate([flat[48:104], zero8], 0).astype(bf16)

    def send_planes(k, cur):
        prepare_down(k, cur)

        @pl.when(has_below & jnp.logical_not(down_early))
        def _():
            down(k, Gs).start()

        for X in range(NX):
            to_operand(R, X, V[cur, X * XS : X * XS + 104, :])
        prepare_up(k)

        @pl.when(has_above & jnp.logical_not(up_early))
        def _():
            up(k, cs).start()

    prepare_down(0, 0)
    prepare_up(0)

    ones = lambda cond: jnp.where(cond, 1, 0)
    count = (
        ones(has_below) + ones(has_above) + ones(zl > 0) + ones(zl < N_ZL - 1)
        + 1 + len(x_peers) + len(yz_peers)
    )
    pl.semaphore_wait(barrier, count)

    @pl.when(has_below)
    def _():
        down(0, Gs).start()

    @pl.when(has_above)
    def _():
        up(0, cs).start()

    @pl.when(has_below)
    def _():
        j_copy.start()

    @pl.when(has_above)
    def _():
        u_copy.start()

    send_own(True)

    given[7].wait()
    pot8[...] = jnp.zeros_like(pot8)
    pot = pot_ref[...]
    p_hi = pot.astype(bf16)
    rest = pot - p_hi.astype(f32)
    p_mid = rest.astype(bf16)
    p_lo = (rest - p_mid.astype(f32)).astype(bf16)
    pot8[0:1, 0:OWNED] = p_hi.astype(f32)
    pot8[1:2, 0:OWNED] = p_mid.astype(f32)
    pot8[2:3, 0:OWNED] = p_lo.astype(f32)
    pcol = mm_nt(Pm[...], pot8[...].astype(bf16)).astype(bf16)
    potc[...] = mm(pcol, jnp.ones((8, 128), bf16)) - CENTRE

    q_l = iota((PLP, 64), 1)
    q_p = iota((PLP, 64), 0)
    q_in = ((q_l & 7) < EDGE) & (q_l < 56)

    def in_top(c):
        cx, cy = c % 2, c // 2
        y_ok = (((q_p >> 3) & 1) == cy) & ((q_p & 7) == (q_l & 7))
        return hot(((q_p >> 4) - 6 * cx == (q_l >> 3)) & y_ok & q_in)

    def in_bottom(c):
        cx, cy = c % 2, c // 2
        return hot(((q_p >> 4) - 6 * cx == (q_l >> 3)) & ((q_p & 15) - 6 * cy == (q_l & 7)) & q_in)

    k_tt = mm_nt(top_k, t_hot).astype(bf16)
    k_g = mm_nt(K1[...], t_hot).astype(bf16)
    for c in range(4):
        e_top = in_top(c)
        KgP[c] = mm_nt(k_g, e_top).astype(bf16)
        KttP[c] = mm_nt(mm(e_top, k_tt).astype(bf16), e_top)

    lin = iota((8, NRL), 1)
    lin_x = jnp.floor((lin.astype(f32) + 0.5) * (1.0 / XS)).astype(jnp.int32)
    lin_r = lin - lin_x * XS
    lin_y = lin_r >> 3
    lin_z = lin_r & 7
    lin_cell = jnp.where(lin_x > 6, 1, 0) + jnp.where(lin_y > 6, 2, 0)
    lin_8 = iota((8, NRL), 0)
    Q[NR:NRL, :] = jnp.zeros((NRL - NR, KL), bf16)
    ar = mm_nt(cn8, Q[...])
    ar = jnp.where((lin_8 & 3) == lin_cell, ar, 0.0) * jnp.where(lin_8 < 4, 32.0, 1.0)
    ar = jnp.broadcast_to(jnp.sum(ar, 0, keepdims=True), (8, NRL))
    prow[...] = jnp.where((lin_x < NX) & (lin_y < NX) & (lin_z < EDGE - 1), ar, -1.0)
    n16 = iota((16, NRL), 0).astype(f32)

    def fill(i, carry):
        base = (i * 16).astype(f32)
        PT[pl.ds(pl.multiple_of(i * 16, 16), 16), :] = hot(prow[0:1, :] == n16 + base)
        return carry


    mask8 = jnp.where(iota((8, ORB), 0) < EDGE - 1, 1.0, 0.0)

    def spread(ref_of, X, factor):
        lo, hi = None, None
        for cx in range(2):
            x = X - 6 * cx
            if 0 <= x < 7:
                a = ref_of(cx, 0, x).reshape(7, 8, ORB) * factor(cx, 0)
                b = ref_of(cx, 1, x).reshape(7, 8, ORB) * factor(cx, 1)
                lo = a if lo is None else lo + a
                hi = b if hi is None else hi + b
        return jnp.concatenate([lo[0:6], lo[6:7] + hi[0:1], hi[1:7]], 0)

    def bulk(k, cur):
        nxt = 1 - cur
        a = pick(k, [t[0] for t in TERMS])
        b = pick(k, [t[1] for t in TERMS])
        am = mask8 * a
        for cx in range(2):
            O[cx] = mm(Kp[...], R[384 * cx : 384 * cx + KR, :])
        for X in range(NX):
            rows = slice(X * XS, X * XS + 104)
            s = spread(
                lambda cx, cy, x: O[cx, x * 56 : x * 56 + 56, cy * 128 : (cy + 1) * 128],
                X,
                lambda cx, cy: scale[cx + 2 * cy],
            )
            v = V[cur, rows, :].reshape(NX, 8, ORB)
            u = V[nxt, rows, :].reshape(NX, 8, ORB)
            pc = potc[rows, :].reshape(NX, 8, ORB)
            new = (s + pc * v) * am[None] - b * u
            part[rows, :] = new.reshape(104, ORB)

    bulk(0, 0)

    @pl.when(has_above)
    def _():
        j_copy.wait_recv()

    @pl.when(has_below)
    def _():
        u_copy.wait_recv()

    tc = top_col[...]
    jc = jbot_col[...]
    m1 = jnp.concatenate([hot(tc == Jr[0:1, t * 128 : (t + 1) * 128]) for t in range(2)], 1)
    F[...] = jnp.concatenate([hot(jc == Ur[0:1, t * 128 : (t + 1) * 128]) for t in range(2)], 1)
    for c in range(4):
        KgD[c] = mm(KgP[c], m1).astype(bf16)
    w = jnp.zeros((PLP, PLP), f32)
    for c in range(4):
        w = w + KttP[c] * Ur[8 + c : 9 + c, :]
    w_hi = w.astype(bf16)
    w_lo = (w - w_hi.astype(f32)).astype(bf16)
    fm = F[...]
    @pl.when(down_mend)
    def _():
        eye = hot(iota((PLP, PLP), 0) == iota((PLP, PLP), 1))
        M1T[...] = mm_nt(eye, m1).astype(bf16)

    @pl.when(up_mend)
    def _():
        for c in range(4):
            KgB[c] = mm_nt(KgP[c], F[...]).astype(bf16)

    w = mm_nt(mm(fm, w_hi).astype(bf16), fm) + mm_nt(mm(fm, w_lo).astype(bf16), fm)
    w_hi = w.astype(bf16)
    W2[0] = w_hi
    W2[1] = (w - w_hi.astype(f32)).astype(bf16)

    def plane_to_plane(rows_top, onward):
        total = jnp.zeros((PLP, PLP), f32)
        if rows_top:
            block_k = mm_nt(top_k, b_hot).astype(bf16)
        else:
            block_k = mm_nt(mm(b_hot, kmat).astype(bf16), t_hot).astype(bf16)
        for c in range(4):
            one, two = (in_top(c), in_bottom(c)) if rows_top else (in_bottom(c), in_top(c))
            total = total + mm_nt(mm(one, block_k).astype(bf16), two) * scale[c]
        hi = total.astype(bf16)
        lo = (total - hi.astype(f32)).astype(bf16)
        total = mm(hi, onward) + mm(lo, onward)
        hi = total.astype(bf16)
        D2[0] = hi
        D2[1] = (total - hi.astype(f32)).astype(bf16)

    @pl.when(up_early)
    def _():
        plane_to_plane(True, F[...])

    @pl.when(down_early)
    def _():
        plane_to_plane(False, m1)

    def add_plane(v, e):
        for X in range(NX):
            lo = pl.ds(X * XS, 8, stride=8)
            hi = pl.ds(X * XS + 64, 8, stride=8)
            v[lo, :] = v[lo, :] + e[X * 16 : X * 16 + 8]
            v[hi, :] = v[hi, :] + e[X * 16 + 8 : X * 16 + 16]

    def ghost(X, am, sc):
        return spread(
            lambda cx, cy, x: OG[cx + 2 * cy, x * 56 : x * 56 + 56, :],
            X,
            lambda cx, cy: (am * sc[cx + 2 * cy])[None],
        )

    def ahead(k):
        am = mask8 * pick(k - 1, [t[0] for t in TERMS])
        sb = [Ur[8 + c : 9 + c, 0:128] for c in range(4)]
        for c in range(4):
            OG[c] = mm(KgB[c], Gs[k - 1])
        for X in range(NX):
            to_operand(R2, X, ghost(X, am, sb).reshape(104, ORB))
        for lo, hi, value in top_sums(R2, sb):
            CR[lax.rem(k, 2), lo:hi, :] = value

    def mend_sums(k):
        cr[k, 0:PL, :] = (cr[k, 0:PL, :].astype(f32) + CR[lax.rem(k, 2)]).astype(bf16)

    def mend_plane(k):
        before = pick(k - 1, [t[0] for t in TERMS])
        Gr[k] = (Gr[k].astype(f32) + mm(M1T[...], cs[k - 1]) * before).astype(bf16)

    def early(k, last):
        a = pick(k, [t[0] for t in TERMS])
        g = Gs[k]
        add_plane(part, (mm(W2[0], g) + mm(W2[1], g)) * a)
        if last:
            return

        @pl.when(up_early)
        def _():
            for X in range(NX):
                to_operand(R2, X, part[X * XS : X * XS + 104, :])
            for lo, hi, value in top_sums(R2, scale):
                CR2[lo:hi, :] = value

            @pl.when(has_below)
            def _():
                up(k, cs).wait_recv()

            @pl.when(up_mend & (k >= 1))
            def _():
                mend_sums(k)

            more = (mm(D2[0], cr[k]) + mm(D2[1], cr[k])) * a
            Ps[k + 1] = (CR2[...] + more[0:PL]).astype(bf16)
            up(k + 1, Ps).start()

        @pl.when(down_early)
        def _():
            @pl.when(has_above)
            def _():
                down(k, Gs).wait_recv()

            @pl.when(down_mend & (k >= 1))
            def _():
                mend_plane(k)

            more = (mm(D2[0], Gr[k]) + mm(D2[1], Gr[k])) * a
            lowest_plane(part, Qs, k + 1, more)
            down(k + 1, Qs).start()

    def finish(k, cur, last):
        nxt = 1 - cur
        a = pick(k, [t[0] for t in TERMS])
        am = mask8 * a
        rest_down = has_above if last else has_above & jnp.logical_not(down_early)
        rest_up = has_below if last else has_below & jnp.logical_not(up_early)

        @pl.when(rest_down)
        def _():
            down(k, Gs).wait_recv()

        @pl.when(rest_down & down_mend & (k >= 1))
        def _():
            mend_plane(k)

        for c in range(4):
            OG[c] = mm(KgD[c], Gr[k])
        for X in range(NX):
            rows = slice(X * XS, X * XS + 104)
            new = part[rows, :].reshape(NX, 8, ORB) + ghost(X, am, scale)
            V[nxt, rows, :] = new.reshape(104, ORB)

        @pl.when(rest_up)
        def _():
            up(k, cs).wait_recv()

        @pl.when(rest_up & up_mend & (k >= 1))
        def _():
            mend_sums(k)

        add_plane(V.at[nxt], mm(F[...], cr[k]) * a)
        if not last:
            return None
        sq = jnp.zeros((8, ORB), f32)
        for X in range(NX):
            padded = V[nxt, X * XS : (X + 1) * XS, :]
            cube = padded.reshape(NX + 1, 8, ORB)
            sq = sq + jnp.sum(cube * cube, 0)
            top = padded.astype(bf16)
            H2[X * XS : (X + 1) * XS, 0:128] = top
            H2[X * XS : (X + 1) * XS, 128:256] = (padded - top.astype(f32)).astype(bf16)
        return sq

    def step(k, carry):
        cur = lax.rem(k, 2)
        early(k, False)

        @pl.when(up_mend)
        def _():
            ahead(k + 1)

        for dist in range(1, N_ZL - 1):

            @pl.when(k == 2 * dist + 1)
            def _(dist=dist):
                forward(dist, True)

        for dist in range(2):

            @pl.when(k == 4 * dist + 2)
            def _(dist=dist):
                turn(dist)

        lax.fori_loop(k * 10, jnp.minimum(k * 10 + 10, OWNP // 16), fill, 0)
        finish(k, cur, False)
        send_planes(k + 1, 1 - cur)
        bulk(k + 1, 1 - cur)
        return carry

    lax.fori_loop(0, DEGREE - 1, step, 0)
    final = DEGREE - 1
    early(final, True)
    forward(3, True)
    turn(2)
    H2[NR:NRL, :] = jnp.zeros((NRL - NR, 256), bf16)
    sq = finish(final, final % 2, True)

    N1s[...] = jnp.broadcast_to(jnp.sum(sq, 0, keepdims=True), (8, ORB))

    def n1(i):
        return remote(N1s, N1r.at[i], n1_send.at[i], n1_recv.at[i], x_peers[i], band)

    for i in range(3):
        n1(i).start()

    turn(3)
    un = mm(PT[...], H2[...])
    LOW[...] = un[:, 0:128].astype(bf16)
    CO[...] = un[:, 0:128] + un[:, 128:256]

    def x1(i):
        return remote(mpb.at[i], X1.at[i], x1_send.at[i], x1_recv.at[i], x_peers[i], band)

    for i in range(4):
        tx = (gx + 1 + i) % N_X
        for h in range(N_ZH):
            m = mm(RBT[h * N_X + tx], LOW[...])
            if i < 3:
                mpb[i, h * 128 : (h + 1) * 128, :] = m.astype(bf16)
            else:
                M0[h * 128 : (h + 1) * 128, :] = m
        if i < 3:
            x1(i).start()

    for i in range(3):
        n1(i).wait_recv()
    N2s[...] = N1s[...] + N1r[0] + N1r[1] + N1r[2]

    def n2(i):
        return remote(N2s, N2r.at[i], n2_send.at[i], n2_recv.at[i], yz_peers[i], band)

    for i in range(15):
        n2(i).start()

    acc = M0[...]
    for i in range(3):
        x1(i).wait_recv()
        acc = acc + X1[i].astype(f32)
    SF[...] = acc
    SB[...] = acc.astype(bf16)

    def x2(i):
        a, b = yz_off[i]
        row = (((zh + a) % N_ZH) * N_Y + (gy + b) % N_Y) * 16
        return remote(
            SB.at[pl.ds(pl.multiple_of(row, 16), 16)], X2.at[i], x2_send.at[i], x2_recv.at[i],
            yz_peers[i], band,
        )

    for i in range(15):
        x2(i).start()

    total = N2s[...]
    for i in range(15):
        n2(i).wait_recv()
        total = total + N2r[i]
    inverse = lax.rsqrt(total[0:1, :] + epsilon)
    OUT[...] = (CO[...] * inverse)[0:OWNED].astype(bf16)
    out_copy = pltpu.make_async_copy(OUT, out_ref, out_sem.at[0])
    out_copy.start()

    m = SF[pl.ds(pl.multiple_of((zh * N_Y + gy) * 16, 16), 16), :]
    for i in range(15):
        x2(i).wait_recv()
        m = m + X2[i].astype(f32)
    margin_ref[...] = m * inverse
    out_copy.wait()

    @pl.when(has_below)
    def _():
        j_copy.wait_send()

    @pl.when(has_above)
    def _():
        u_copy.wait_send()

    def sent(k, carry):
        @pl.when(has_below)
        def _():
            down(k, Gs).wait_send()

        @pl.when(has_above)
        def _():
            up(k, cs).wait_send()

        return carry

    lax.fori_loop(0, DEGREE, sent, 0)
    send_own(False)
    for dist in range(1, N_ZL):
        forward(dist, False)
    for i in range(3):
        n1(i).wait_send()
        x1(i).wait_send()
    for i in range(15):
        n2(i).wait_send()
        x2(i).wait_send()


def per_device(start_block, resident, cell_kernel, cell_scale, potential, cell_nodes, send_rows):
    vm = lambda shape, t: pltpu.VMEM(shape, t)
    dma = lambda n: pltpu.SemaphoreType.DMA((n,))
    vmem = pl.BlockSpec(memory_space=pltpu.VMEM)
    scratch = [
        vm((OWNED, ORB), bf16),
        vm((OWNED, ORB), bf16),
        vm((343, 343), bf16),
        pltpu.SMEM((4,), f32),
        vm((1, OWNED), f32),
        vm((4, 343), jnp.int32),
        pltpu.SMEM((4, 343), jnp.int32),
        vm((1, PLANE), jnp.int32),
        vm((OWNED, ORB), bf16),
        vm((2, NRP, ORB), f32),
        vm((832, 256), bf16),
        vm((2, MR, 256), f32),
        vm((4, MR, ORB), f32),
        vm((NRP, ORB), f32),
        vm((NR, ORB), f32),
        vm((NRP, ORB), f32),
        vm((8, NRL), f32),
        vm((NR, OWNP), bf16),
        vm((OWNP, NRL), bf16),
        vm((NRL, KL), bf16),
        vm((OWNP, ORB), bf16),
        vm((KL, KL), bf16),
        vm((MR, KL), bf16),
        vm((MR, KR), bf16),
        vm((56, KR), bf16),
        vm((4, MR, PLP), bf16),
        vm((4, PLP, PLP), f32),
        vm((4, MR, PLP), bf16),
        vm((PLP, PLP), bf16),
        vm((PLP, PLP), bf16),
        vm((2, PLP, PLP), bf16),
        vm((PLP, ORB), f32),
        vm((PLP, ORB), f32),
        vm((8, OWNP), f32),
        vm((8, KL), jnp.int32),
        vm((8, PLP), f32),
        vm((8, ORB, OWNP), bf16),
        vm((832, 256), bf16),
        vm((4, MR, PLP), bf16),
        vm((PLP, PLP), bf16),
        vm((2, PLP, PLP), bf16),
        vm((2, PL, ORB), f32),
        vm((PL, ORB), f32),
        vm((DEGREE, PL, ORB), bf16),
        vm((DEGREE, PL, ORB), bf16),
        vm((DEGREE, PLP, ORB), bf16),
        vm((DEGREE, PLP, ORB), bf16),
        vm((DEGREE, PLP, ORB), bf16),
        vm((DEGREE, PLP, ORB), bf16),
        vm((8, PLP), f32),
        vm((8, PLP), f32),
        vm((16, PLP), f32),
        vm((16, PLP), f32),
        vm((8, OWNP, ORB), bf16),
        vm((NRL, 256), bf16),
        vm((OWNP, ORB), bf16),
        vm((OWNP, ORB), f32),
        vm((3, 256, ORB), bf16),
        vm((3, 256, ORB), bf16),
        vm((256, ORB), f32),
        vm((256, ORB), f32),
        vm((256, ORB), bf16),
        vm((15, 16, ORB), bf16),
        vm((8, ORB), f32),
        vm((3, 8, ORB), f32),
        vm((8, ORB), f32),
        vm((15, 8, ORB), f32),
        dma(8), dma(8), dma(8), dma(8), dma(2), dma(2), dma(20), dma(8),
        dma(3), dma(3), dma(15), dma(15), dma(3), dma(3), dma(15), dma(15), dma(8), dma(1),
    ]
    return pl.pallas_call(
        kernel,
        out_shape=(
            jax.ShapeDtypeStruct((OWNED, ORB), bf16),
            jax.ShapeDtypeStruct((16, ORB), f32),
        ),
        in_specs=[pl.BlockSpec(memory_space=pl.ANY)] * 7,
        out_specs=(pl.BlockSpec(memory_space=pl.ANY), vmem),
        scratch_shapes=scratch,
        compiler_params=pltpu.CompilerParams(
            collective_id=0, has_side_effects=True, vmem_limit_bytes=56 * 1024 * 1024
        ),
        cost_estimate=pl.CostEstimate(
            flops=4_000_000_000, bytes_accessed=1_000_000, transcendentals=128
        ),
    )(
        start_block, resident, cell_kernel, cell_scale, potential.reshape(1, OWNED), cell_nodes,
        send_rows.reshape(1, PLANE),
    )


def solution(mesh):
    return jax.shard_map(
        per_device,
        mesh=mesh,
        in_specs=(
            P("domain", "band"),
            P("domain", "band"),
            P(),
            P("domain"),
            P("domain"),
            P("domain", None),
            P("domain"),
        ),
        out_specs=(P("domain", "band"), P("domain", "band")),
        check_vma=False,
    )
```

```python
import functools

import jax
import jax.numpy as jnp
from jax import lax
from jax.experimental import pallas as pl
from jax.experimental.pallas import tpu as pltpu
from jax.sharding import PartitionSpec as P

DEGREE = 8
EDGE = 7
ORB = 128
OWNED = 1014
PLANE = 169

lower_edge = 0.0
cutoff_edge = 16.0
upper_edge = 96.0
epsilon = 1e-06

NX = 13
XS = 112
NR = NX * XS
NRP = NR + 16
NRL = 1536
PL = 208
PLP = 256
MR = 392
KR = 448
KL = 384
OWNP = 1024

N_DOM = 64
N_ZH, N_X, N_Y = 2, 4, 8
N_ZL = 4

f32 = jnp.float32
bf16 = jnp.bfloat16
MESH = pl.DeviceIdType.MESH


def chebyshev_terms(degree):
    half_width = (upper_edge - cutoff_edge) / 2.0
    centre = (upper_edge + cutoff_edge) / 2.0
    sigma_now = half_width / (lower_edge - centre)
    gamma_ratio = 2.0 / sigma_now
    lead_factor = sigma_now / half_width
    recurrence = [(lead_factor, 0.0)]
    for _ in range(degree - 1):
        sigma_next = 1.0 / (gamma_ratio - sigma_now)
        recurrence.append((2.0 * sigma_next / half_width, sigma_now * sigma_next))
        sigma_now = sigma_next
    return (centre, recurrence)


CENTRE, TERMS = chebyshev_terms(DEGREE)


def mm(a, b):
    return jnp.dot(a, b, preferred_element_type=f32)


def mm_nt(a, b):
    return lax.dot_general(a, b, (((1,), (1,)), ((), ())), preferred_element_type=f32)


def mm_tn(a, b):
    return lax.dot_general(a, b, (((0,), (0,)), ((), ())), preferred_element_type=f32)


def iota(shape, dim):
    return lax.broadcasted_iota(jnp.int32, shape, dim)


def hot(cond):
    return jnp.where(cond, 1.0, 0.0).astype(bf16)


def pick(k, values):
    out = jnp.float32(values[0])
    for i in range(1, len(values)):
        out = jnp.where(k == i, jnp.float32(values[i]), out)
    return out


def kernel(
    start_hbm, res_hbm, ck_hbm, scale_hbm, pot_hbm, cn_hbm, sr_hbm,
    out_ref, margin_ref,
    start_ref, res_ref, ck_ref, scale_ref, pot_ref, cn_ref, cns_ref, sr_ref, OUT,
    V, R, O, OG, part, potc, place, prow, Pm, PT, Q, st, kpad, K1, Kp, T, KgP, KttP, KgD,
    ET, F, W2, top_col, jbot_col, pot8, cnp, srp,
    RBT, R2, KgB, M1, WT, M1T, D2, CR, CR2, Ps, Qs, Gs, cs, Gr, cr, Js, Jr, Us, Ur, RB, H2, LOW, CO, mpb, X1, M0, SF, SB, X2, SZ, X3, N1s, N1r, N2s, N2r, N3s, N3r,
    g_send, g_recv, c_send, c_recv, j_sem, u_sem, r_send, r_recv, x1_send, x1_recv, x2_send, x2_recv,
    n1_send, n1_recv, n2_send, n2_recv, n3_sem, x3_sem, in_sem, out_sem,
):
    d = lax.axis_index("domain")
    band = lax.axis_index("band")
    zh = d // (N_X * N_Y)
    gx = (d // N_Y) % N_X
    gy = d % N_Y
    zl = band // 2
    core = band % 2
    sibling = zl * 2 + (1 - core)
    has_below = d > 0
    has_above = d < N_DOM - 1
    mid = N_DOM // N_ZH
    end_y = has_above & (d % N_Y == N_Y - 1)
    first_y = has_below & (d % N_Y == 0)
    up_early = end_y | (d == mid - 2)
    up_mend = first_y | (d == mid - 1)
    down_early = first_y | (d == mid + 1)
    down_mend = end_y | (d == mid)

    given = [
        (cn_hbm, cns_ref), (cn_hbm, cn_ref), (scale_hbm, scale_ref), (sr_hbm, sr_ref),
        (start_hbm, start_ref), (ck_hbm, ck_ref), (res_hbm, res_ref), (pot_hbm, pot_ref),
    ]
    given = [pltpu.make_async_copy(a, b, in_sem.at[i]) for i, (a, b) in enumerate(given)]
    for c in given:
        c.start()

    Gr[...] = jnp.zeros_like(Gr)
    cr[...] = jnp.zeros_like(cr)
    Jr[...] = jnp.full(Jr.shape, -3.0, f32)
    Ur[0:8, :] = jnp.full((8, PLP), -4.0, f32)
    Ur[8:16, :] = jnp.zeros((8, PLP), f32)

    barrier = pltpu.get_barrier_semaphore()

    def greet(dom, bnd):
        pl.semaphore_signal(barrier, inc=1, device_id=(dom, bnd), device_id_type=MESH)

    x_peers = [(zh * N_X + (gx + i) % N_X) * N_Y + gy for i in range(1, N_X)]
    y_peers = [(zh * N_X + gx) * N_Y + (gy + i) % N_Y for i in range(1, N_Y)]
    z_peer = ((1 - zh) * N_X + gx) * N_Y + gy
    for p in [z_peer] + y_peers + x_peers:
        greet(p, band)

    @pl.when(has_below)
    def _():
        greet(d - 1, band)

    @pl.when(has_above)
    def _():
        greet(d + 1, band)

    @pl.when(zl > 0)
    def _():
        greet(d, band - 2)

    @pl.when(zl < N_ZL - 1)
    def _():
        greet(d, band + 2)

    greet(d, sibling)

    for c in given[0:3]:
        c.wait()
    corner = [cns_ref[c, 0] for c in range(4)]
    right_x = [cns_ref[c, EDGE - 1] for c in range(4)]
    right_y = [cns_ref[c, EDGE * (EDGE - 1)] for c in range(4)]
    pos = []
    for c in range(4):
        in_x = sum([jnp.where(right_x[b] == corner[c], 1, 0) for b in range(4)])
        in_y = sum([jnp.where(right_y[b] == corner[c], 1, 0) for b in range(4)])
        pos.append(in_x + 2 * in_y)
    scale = []
    for p in range(4):
        s = jnp.float32(0.0)
        for c in range(4):
            s = s + jnp.where(pos[c] == p, scale_ref[c], 0.0)
        scale.append(s)

    cnp[...] = jnp.zeros_like(cnp)
    cnp[0:4, 0:343] = cn_ref[...]
    row8 = iota((8, KL), 0)
    full = jnp.zeros((8, KL), jnp.int32)
    for c in range(4):
        line = jnp.broadcast_to(cnp[c : c + 1, :], (8, KL))
        full = full + jnp.where((row8 & 3) == pos[c], line, 0)
    cn8 = jnp.where(row8 < 4, full >> 5, full & 31).astype(f32).astype(bf16)

    rr = iota((XS, KL), 0)
    ln = iota((XS, KL), 1)
    yy = rr >> 3
    zz = rr & 7
    k_base = jnp.where(
        (zz < EDGE) & (yy < NX), zz * 49 + jnp.where(yy > 6, yy - 6, yy) * 7, -1000
    )
    diff = k_base - ln
    l8 = iota((XS, 8), 1)
    y8 = iota((XS, 8), 0) >> 3
    z128 = iota((XS, 128), 0) & 7
    y128 = iota((XS, 128), 0) >> 3
    top_row = (z128 < EDGE) & (y128 < NX)
    own_row = (z128 < EDGE - 1) & (y128 < NX)
    weights = jnp.where(iota((8, 128), 0) < 4, 32.0, 1.0).astype(bf16)
    lane = iota((XS, 128), 1).astype(f32)
    for X in range(NX):
        x = X if X <= 6 else X - 6
        one = hot(diff == -x)
        Q[X * XS : (X + 1) * XS, :] = one
        a1 = mm_nt(one, cn8)
        cell = jnp.where(y8 > 6, 2, 0) + (1 if X > 6 else 0)
        a1 = jnp.where((l8 & 3) == cell, a1, 0.0).astype(bf16)
        pl_x = mm(a1, weights)
        place[X * XS : (X + 1) * XS, :] = jnp.where(top_row, pl_x, -1.0)
        own = jnp.where(own_row, pl_x, -1.0)
        for t in range(8):
            Pm[X * XS : (X + 1) * XS, t * 128 : (t + 1) * 128] = hot(own == lane + 128.0 * t)
    place[NR:NRP, :] = jnp.full((NRP - NR, 128), -1.0, f32)

    given[3].wait()
    srp[...] = jnp.full(srp.shape, -5.0, f32)
    srp[0:1, 0:PLANE] = sr_ref[...].astype(f32)
    top_col[...] = jnp.full(top_col.shape, -1.0, f32)
    yrow = iota((16, 128), 0)
    lane16 = iota((16, 128), 1)
    ET[...] = jnp.zeros_like(ET)
    for X in range(NX):
        b0 = jnp.concatenate(
            [place[pl.ds(X * XS, 8, stride=8), :], place[pl.ds(X * XS + 64, 8, stride=8), :]], 0
        )
        b0 = jnp.where(yrow < NX, b0, -1.0)
        for t in range(2):
            ET[X * 16 : X * 16 + 16, t * 128 : (t + 1) * 128] = hot(
                b0 == srp[0:1, t * 128 : (t + 1) * 128]
            )
        t0 = jnp.concatenate(
            [place[pl.ds(X * XS + 6, 8, stride=8), :], place[pl.ds(X * XS + 54, 8, stride=8), :]],
            0,
        )
        top_col[X * 16 : X * 16 + 16, :] = jnp.where((yrow & 7) < EDGE, t0 - float(OWNED), -1.0)
    jm = iota((PLP, 128), 0).astype(f32).astype(bf16)
    p_row = iota((PLP, 128), 0)
    jb = mm(ET[...], jm)
    jbot_col[...] = jnp.where(((p_row & 15) < NX) & (p_row < PL), jb, -2.0)
    p_lane = iota((8, PLP), 1)
    p_ok = ((p_lane & 15) < NX) & (p_lane < PL)
    jr = mm_nt(iota((8, PLP), 1).astype(f32).astype(bf16), ET[...])
    Js[...] = jnp.where(p_ok, jr, -2.0)

    pr = iota((PLP, KL), 0)
    pln = iota((PLP, KL), 1)
    pX = pr >> 4
    pY = pr & 15
    ty = pr & 7
    tcy = (pr >> 3) & 1
    t_in = (pX < NX) & (ty < EDGE)
    ox = jnp.where(pX > 6, pX - 6, pX)
    q_top = hot(t_in & (294 + ty * 7 + ox == pln))
    at = mm_nt(cn8, q_top)
    lX = p_lane >> 4
    l_cell = jnp.where(lX > 6, 1, 0) + ((p_lane >> 3) & 1) * 2
    t_ok = ((p_lane & 7) < EDGE) & (p_lane < PL)
    r8 = iota((8, PLP), 0)
    at = jnp.where((r8 & 3) == l_cell, at, 0.0) * jnp.where(r8 < 4, 32.0, 1.0)
    top_line = jnp.sum(at, 0, keepdims=True) - float(OWNED)
    Us[0:8, :] = jnp.where(t_ok, jnp.broadcast_to(top_line, (8, PLP)), -1.0)
    srow = iota((8, PLP), 0)
    stile = jnp.zeros((8, PLP), f32)
    for c in range(4):
        stile = jnp.where(srow == c, scale[c], stile)
    Us[8:16, :] = stile

    given[6].wait()
    RB[band, 1008:1024, :] = jnp.zeros((16, ORB), bf16)
    RB[band, 0:OWNED, :] = res_ref[...]

    def remote(src, dst, ssem, rsem, dom, bnd):
        return pltpu.make_async_remote_copy(
            src_ref=src, dst_ref=dst, send_sem=ssem, recv_sem=rsem,
            device_id=(dom, bnd), device_id_type=MESH,
        )

    j_copy = remote(Js, Jr, j_sem.at[0], j_sem.at[1], d - 1, band)
    u_copy = remote(Us, Ur, u_sem.at[0], u_sem.at[1], d + 1, band)

    def turn(dist):
        if dist == 0:
            block(sibling, sibling, 0).wait_recv()
            RBT[band] = RB[band].T
            RBT[sibling] = RB[sibling].T
            return

        def both(src):
            other = src + 1 - 2 * core
            block(other, sibling, 0).wait_recv()
            RBT[src] = RB[src].T
            RBT[other] = RB[other].T

        @pl.when(zl >= dist)
        def _():
            both(band - 2 * dist)

        @pl.when(zl + dist <= N_ZL - 1)
        def _():
            both(band + 2 * dist)

    def block(src, to, s):
        return remote(RB.at[src], RB.at[src], r_send.at[s], r_recv.at[src], d, to)

    def send_own(start):
        def act(c):
            c.start() if start else c.wait_send()

        @pl.when(zl < N_ZL - 1)
        def _():
            act(block(band, band + 2, 0))

        @pl.when(zl > 0)
        def _():
            act(block(band, band - 2, 1))

        act(block(band, sibling, 2))

    def forward(dist, start):
        @pl.when(zl >= dist)
        def _():
            src = band - 2 * dist
            if start:
                block(src, sibling, 0).wait_recv()

            @pl.when(zl < N_ZL - 1)
            def _():
                c = block(src, band + 2, 3 * dist)
                c.start() if start else c.wait_send()

            c = block(src, sibling, 3 * dist + 1)
            c.start() if start else c.wait_send()

        @pl.when(zl + dist <= N_ZL - 1)
        def _():
            src = band + 2 * dist
            if start:
                block(src, sibling, 0).wait_recv()

            @pl.when(zl > 0)
            def _():
                c = block(src, band - 2, 9 + 3 * dist)
                c.start() if start else c.wait_send()

            c = block(src, sibling, 10 + 3 * dist)
            c.start() if start else c.wait_send()

    given[4].wait()
    st[1008:1024, :] = jnp.zeros((16, ORB), bf16)
    st[0:OWNED, :] = start_ref[...]
    V[0, 0:NR, :] = mm(Pm[...], st[...])
    V[0, NR:NRP, :] = jnp.zeros((NRP - NR, ORB), f32)
    V[1, :, :] = jnp.zeros((NRP, ORB), f32)
    part[...] = jnp.zeros_like(part)
    zero8 = jnp.zeros((8, ORB), f32)
    for X in range(NX):
        R[X * 64 : X * 64 + 64, 0:128] = V[0, X * XS : X * XS + 64, :].astype(bf16)
        R[X * 64 : X * 64 + 64, 128:256] = V[0, X * XS + 48 : X * XS + 112, :].astype(bf16)

    given[5].wait()
    kpad[...] = jnp.zeros_like(kpad)
    kpad[0:343, 0:343] = ck_ref[...]
    kmat = kpad[...]
    r56 = iota((56, KL), 0)
    k56 = jnp.where((r56 & 7) < 7, (r56 & 7) * 49 + (r56 >> 3) * 7, -1000) - iota((56, KL), 1)
    row_hot = jnp.concatenate([jnp.where(k56 == -x, 1.0, 0.0) for x in range(7)], 0).astype(bf16)
    r64 = iota((64, KL), 0)
    k64 = (
        jnp.where(((r64 & 7) < 7) & (r64 < 56), (r64 & 7) * 49 + (r64 >> 3) * 7, -1000)
        - iota((64, KL), 1)
    )
    col_hot = jnp.concatenate([hot(k64 == -x) for x in range(7)], 0)
    K1[...] = mm(row_hot, kmat).astype(bf16)
    Kp[...] = mm_nt(K1[...], col_hot).astype(bf16)
    r8k = iota((8, KL), 0)
    l8k = iota((8, KL), 1)
    kt = jnp.where(r8k < EDGE, 294 + r8k * 7, -1000) - l8k
    kb = jnp.where(r8k < EDGE, r8k * 7, -1000) - l8k
    none8 = jnp.zeros((8, KL), f32)
    t_hot = jnp.concatenate([jnp.where(kt == -x, 1.0, 0.0) for x in range(7)] + [none8], 0).astype(bf16)
    b_hot = jnp.concatenate([jnp.where(kb == -x, 1.0, 0.0) for x in range(7)] + [none8], 0).astype(bf16)
    top_k = mm(t_hot, kmat).astype(bf16)
    T[...] = mm_nt(top_k, col_hot)[0:56].astype(bf16)

    def down(k, src):
        return remote(
            src.at[k, pl.ds(0, PL)], Gr.at[k, pl.ds(0, PL)], g_send.at[k], g_recv.at[k], d - 1, band
        )

    def up(k, src):
        return remote(
            src.at[k, pl.ds(0, PL)], cr.at[k, pl.ds(0, PL)], c_send.at[k], c_recv.at[k], d + 1, band
        )

    def lowest_plane(v, out, k, more=None):
        for X in range(NX):
            lo = v[pl.ds(X * XS, 8, stride=8), :]
            hi = v[pl.ds(X * XS + 64, 8, stride=8), :]
            both = jnp.concatenate([lo, hi], 0)
            if more is not None:
                both = both + more[X * 16 : X * 16 + 16]
            out[k, X * 16 : X * 16 + 16, :] = both.astype(bf16)

    def top_sums(r, sc):
        parts = [mm(T[...], r[384 * cx : 384 * cx + KR, :]) for cx in range(2)]
        out = []
        for X in range(NX):
            tiles = []
            for cy in range(2):
                t = None
                for cx in range(2):
                    x = X - 6 * cx
                    if 0 <= x < 7:
                        p = parts[cx][x * 8 : x * 8 + 8, cy * 128 : (cy + 1) * 128] * sc[cx + 2 * cy]
                        t = p if t is None else t + p
                tiles.append(t)
            out.append((X * 16, X * 16 + 16, jnp.concatenate(tiles, 0)))
        return out

    def prepare_down(k, cur):
        Gs[k, PL:PLP, :] = jnp.zeros((PLP - PL, ORB), bf16)
        lowest_plane(V.at[cur], Gs, k)

    def prepare_up(k):
        cs[k, PL:PLP, :] = jnp.zeros((PLP - PL, ORB), bf16)
        for lo, hi, value in top_sums(R, scale):
            cs[k, lo:hi, :] = value.astype(bf16)

    def to_operand(r, X, flat):
        r[X * 64 : X * 64 + 64, 0:128] = flat[0:64].astype(bf16)
        r[X * 64 : X * 64 + 64, 128:256] = jnp.concatenate([flat[48:104], zero8], 0).astype(bf16)

    def send_planes(k, cur):
        prepare_down(k, cur)

        @pl.when(has_below & jnp.logical_not(down_early))
        def _():
            down(k, Gs).start()

        for X in range(NX):
            to_operand(R, X, V[cur, X * XS : X * XS + 104, :])
        prepare_up(k)

        @pl.when(has_above & jnp.logical_not(up_early))
        def _():
            up(k, cs).start()

    prepare_down(0, 0)
    prepare_up(0)

    ones = lambda cond: jnp.where(cond, 1, 0)
    count = (
        ones(has_below) + ones(has_above) + ones(zl > 0) + ones(zl < N_ZL - 1)
        + 2 + len(x_peers) + len(y_peers)
    )
    pl.semaphore_wait(barrier, count)

    @pl.when(has_below)
    def _():
        j_copy.start()

    @pl.when(has_above)
    def _():
        u_copy.start()

    @pl.when(has_below)
    def _():
        down(0, Gs).start()

    @pl.when(has_above)
    def _():
        up(0, cs).start()

    send_own(True)

    given[7].wait()
    pot8[...] = jnp.zeros_like(pot8)
    pot = pot_ref[...]
    p_hi = pot.astype(bf16)
    rest = pot - p_hi.astype(f32)
    p_mid = rest.astype(bf16)
    p_lo = (rest - p_mid.astype(f32)).astype(bf16)
    pot8[0:1, 0:OWNED] = p_hi.astype(f32)
    pot8[1:2, 0:OWNED] = p_mid.astype(f32)
    pot8[2:3, 0:OWNED] = p_lo.astype(f32)
    pcol = mm_nt(Pm[...], pot8[...].astype(bf16)).astype(bf16)
    potc[...] = mm(pcol, jnp.ones((8, 128), bf16)) - CENTRE

    q_l = iota((PLP, 64), 1)
    q_p = iota((PLP, 64), 0)
    q_in = ((q_l & 7) < EDGE) & (q_l < 56)

    def in_top(c):
        cx, cy = c % 2, c // 2
        y_ok = (((q_p >> 3) & 1) == cy) & ((q_p & 7) == (q_l & 7))
        return hot(((q_p >> 4) - 6 * cx == (q_l >> 3)) & y_ok & q_in)

    def in_bottom(c):
        cx, cy = c % 2, c // 2
        return hot(((q_p >> 4) - 6 * cx == (q_l >> 3)) & ((q_p & 15) - 6 * cy == (q_l & 7)) & q_in)

    k_tt = mm_nt(top_k, t_hot).astype(bf16)
    k_g = mm_nt(K1[...], t_hot).astype(bf16)
    for c in range(4):
        e_top = in_top(c)
        KgP[c] = mm_nt(k_g, e_top).astype(bf16)
        KttP[c] = mm_nt(mm(e_top, k_tt).astype(bf16), e_top)

    lin = iota((8, NRL), 1)
    lin_x = jnp.floor((lin.astype(f32) + 0.5) * (1.0 / XS)).astype(jnp.int32)
    lin_r = lin - lin_x * XS
    lin_y = lin_r >> 3
    lin_z = lin_r & 7
    lin_cell = jnp.where(lin_x > 6, 1, 0) + jnp.where(lin_y > 6, 2, 0)
    lin_8 = iota((8, NRL), 0)
    Q[NR:NRL, :] = jnp.zeros((NRL - NR, KL), bf16)
    ar = mm_nt(cn8, Q[...])
    ar = jnp.where((lin_8 & 3) == lin_cell, ar, 0.0) * jnp.where(lin_8 < 4, 32.0, 1.0)
    ar = jnp.broadcast_to(jnp.sum(ar, 0, keepdims=True), (8, NRL))
    prow[...] = jnp.where((lin_x < NX) & (lin_y < NX) & (lin_z < EDGE - 1), ar, -1.0)
    n16 = iota((16, NRL), 0).astype(f32)

    def fill(i, carry):
        base = (i * 16).astype(f32)
        PT[pl.ds(pl.multiple_of(i * 16, 16), 16), :] = hot(prow[0:1, :] == n16 + base)
        return carry


    mask8 = jnp.where(iota((8, ORB), 0) < EDGE - 1, 1.0, 0.0)

    def spread(ref_of, X, factor):
        lo, hi = None, None
        for cx in range(2):
            x = X - 6 * cx
            if 0 <= x < 7:
                a = ref_of(cx, 0, x).reshape(7, 8, ORB) * factor(cx, 0)
                b = ref_of(cx, 1, x).reshape(7, 8, ORB) * factor(cx, 1)
                lo = a if lo is None else lo + a
                hi = b if hi is None else hi + b
        return jnp.concatenate([lo[0:6], lo[6:7] + hi[0:1], hi[1:7]], 0)

    def bulk(k, cur):
        nxt = 1 - cur
        a = pick(k, [t[0] for t in TERMS])
        b = pick(k, [t[1] for t in TERMS])
        am = mask8 * a
        for cx in range(2):
            O[cx] = mm(Kp[...], R[384 * cx : 384 * cx + KR, :])
        for X in range(NX):
            rows = slice(X * XS, X * XS + 104)
            s = spread(
                lambda cx, cy, x: O[cx, x * 56 : x * 56 + 56, cy * 128 : (cy + 1) * 128],
                X,
                lambda cx, cy: scale[cx + 2 * cy],
            )
            v = V[cur, rows, :].reshape(NX, 8, ORB)
            u = V[nxt, rows, :].reshape(NX, 8, ORB)
            pc = potc[rows, :].reshape(NX, 8, ORB)
            new = (s + pc * v) * am[None] - b * u
            part[rows, :] = new.reshape(104, ORB)

    bulk(0, 0)

    def halves(v):
        hi = v.astype(bf16)
        return hi, (v - hi.astype(f32)).astype(bf16)

    def plane_to_plane(rows_top, onward):
        total = jnp.zeros((PLP, PLP), f32)
        if rows_top:
            block_k = mm_nt(top_k, b_hot).astype(bf16)
        else:
            block_k = mm_nt(mm(b_hot, kmat).astype(bf16), t_hot).astype(bf16)
        for c in range(4):
            one, two = (in_top(c), in_bottom(c)) if rows_top else (in_bottom(c), in_top(c))
            total = total + mm_nt(mm(one, block_k).astype(bf16), two) * scale[c]
        hi = total.astype(bf16)
        lo = (total - hi.astype(f32)).astype(bf16)
        total = mm(hi, onward) + mm(lo, onward)
        hi = total.astype(bf16)
        D2[0] = hi
        D2[1] = (total - hi.astype(f32)).astype(bf16)

    def add_plane(v, e):
        for X in range(NX):
            lo = pl.ds(X * XS, 8, stride=8)
            hi = pl.ds(X * XS + 64, 8, stride=8)
            v[lo, :] = v[lo, :] + e[X * 16 : X * 16 + 8]
            v[hi, :] = v[hi, :] + e[X * 16 + 8 : X * 16 + 16]

    def ghost(X, am, sc):
        return spread(
            lambda cx, cy, x: OG[cx + 2 * cy, x * 56 : x * 56 + 56, :],
            X,
            lambda cx, cy: (am * sc[cx + 2 * cy])[None],
        )

    def ahead(k):
        am = mask8 * pick(k - 1, [t[0] for t in TERMS])
        sb = [Ur[8 + c : 9 + c, 0:128] for c in range(4)]
        for c in range(4):
            OG[c] = mm(KgB[c], Gs[k - 1])
        for X in range(NX):
            to_operand(R2, X, ghost(X, am, sb).reshape(104, ORB))
        for lo, hi, value in top_sums(R2, sb):
            CR[lax.rem(k, 2), lo:hi, :] = value

    def mend_sums(k):
        cr[k, 0:PL, :] = (cr[k, 0:PL, :].astype(f32) + CR[lax.rem(k, 2)]).astype(bf16)

    def mend_plane(k):
        before = pick(k - 1, [t[0] for t in TERMS])

        @pl.when((k != 1) | (d != mid - 1))
        def _():
            Gr[k] = (Gr[k].astype(f32) + mm(M1T[...], cs[k - 1]) * before).astype(bf16)

        @pl.when((k == 1) & (d == mid - 1))
        def _():
            own = mm(M1[...], Gr[0]).astype(bf16)
            sums = cs[0].astype(f32) + mm(WT[0], own) + mm(WT[1], own)
            Gr[k] = (Gr[k].astype(f32) + mm(M1T[...], sums.astype(bf16)) * before).astype(bf16)

    def early_up(k):
        a = pick(k, [t[0] for t in TERMS])
        g = Gs[k]
        add_plane(part, (mm(W2[0], g) + mm(W2[1], g)) * a)

        @pl.when(up_early & (k < DEGREE - 1))
        def _():
            for X in range(NX):
                to_operand(R2, X, part[X * XS : X * XS + 104, :])
            for lo, hi, value in top_sums(R2, scale):
                CR2[lo:hi, :] = value

            @pl.when(has_below)
            def _():
                up(k, cs).wait_recv()

            @pl.when(up_mend & (k >= 1))
            def _():
                mend_sums(k)

            more = (mm(D2[0], cr[k]) + mm(D2[1], cr[k])) * a
            Ps[k + 1] = (CR2[...] + more[0:PL]).astype(bf16)
            up(k + 1, Ps).start()

    def early_down(k):
        a = pick(k, [t[0] for t in TERMS])

        @pl.when(has_above)
        def _():
            down(k, Gs).wait_recv()

        @pl.when(down_mend & (k >= 1))
        def _():
            mend_plane(k)

        more = (mm(D2[0], Gr[k]) + mm(D2[1], Gr[k])) * a
        lowest_plane(part, Qs, k + 1, more)
        down(k + 1, Qs).start()

    def finish(k, cur, last):
        nxt = 1 - cur
        a = pick(k, [t[0] for t in TERMS])
        am = mask8 * a
        rest_down = has_above if last else has_above & jnp.logical_not(down_early)
        rest_up = has_below if last else has_below & jnp.logical_not(up_early)

        @pl.when(rest_down)
        def _():
            down(k, Gs).wait_recv()

        @pl.when(rest_down & down_mend & (k >= 1))
        def _():
            mend_plane(k)

        for c in range(4):
            OG[c] = mm(KgD[c], Gr[k])
        for X in range(NX):
            rows = slice(X * XS, X * XS + 104)
            new = part[rows, :].reshape(NX, 8, ORB) + ghost(X, am, scale)
            V[nxt, rows, :] = new.reshape(104, ORB)

        @pl.when(rest_up)
        def _():
            up(k, cs).wait_recv()

        @pl.when(rest_up & up_mend & (k >= 1))
        def _():
            mend_sums(k)

        add_plane(V.at[nxt], mm(F[...], cr[k]) * a)
        if not last:
            return None
        sq = jnp.zeros((8, ORB), f32)
        for X in range(NX):
            padded = V[nxt, X * XS : (X + 1) * XS, :]
            cube = padded.reshape(NX + 1, 8, ORB)
            sq = sq + jnp.sum(cube * cube, 0)
            top = padded.astype(bf16)
            H2[X * XS : (X + 1) * XS, 0:128] = top
            H2[X * XS : (X + 1) * XS, 128:256] = (padded - top.astype(f32)).astype(bf16)
        return sq

    @pl.when(has_above)
    def _():
        j_copy.wait_recv()

    tc = top_col[...]
    M1[...] = jnp.concatenate([hot(tc == Jr[0:1, t * 128 : (t + 1) * 128]) for t in range(2)], 1)

    @pl.when(down_early)
    def _():
        plane_to_plane(False, M1[...])

    @pl.when(d == mid)
    def _():
        early_down(0)

    @pl.when(has_below)
    def _():
        u_copy.wait_recv()

    jc = jbot_col[...]
    F[...] = jnp.concatenate([hot(jc == Ur[0:1, t * 128 : (t + 1) * 128]) for t in range(2)], 1)

    @pl.when(up_early)
    def _():
        plane_to_plane(True, F[...])

    w = jnp.zeros((PLP, PLP), f32)
    for c in range(4):
        w = w + KttP[c] * Ur[8 + c : 9 + c, :]
    fm = F[...]
    w_hi, w_lo = halves(w)
    w = mm_nt(mm(fm, w_hi).astype(bf16), fm) + mm_nt(mm(fm, w_lo).astype(bf16), fm)
    W2[0], W2[1] = halves(w)
    early_up(0)

    @pl.when(down_early & (d != mid))
    def _():
        early_down(0)

    for c in range(4):
        KgD[c] = mm(KgP[c], M1[...]).astype(bf16)

    @pl.when(down_mend)
    def _():
        eye = hot(iota((PLP, PLP), 0) == iota((PLP, PLP), 1))
        M1T[...] = mm_nt(eye, M1[...]).astype(bf16)

    @pl.when(d == mid - 1)
    def _():
        total = KttP[0] * scale[0]
        for c in range(1, 4):
            total = total + KttP[c] * scale[c]
        WT[0], WT[1] = halves(total)

    @pl.when(up_mend)
    def _():
        for c in range(4):
            KgB[c] = mm_nt(KgP[c], F[...]).astype(bf16)

    def step(k, carry):
        cur = lax.rem(k, 2)
        @pl.when(up_mend)
        def _():
            ahead(k + 1)

        for dist in range(1, N_ZL - 1):

            @pl.when(k == 2 * dist + 1)
            def _(dist=dist):
                forward(dist, True)

        for dist in range(2):

            @pl.when(k == 4 * dist + 2)
            def _(dist=dist):
                turn(dist)

        lax.fori_loop(k * 10, jnp.minimum(k * 10 + 10, OWNP // 16), fill, 0)
        finish(k, cur, False)
        send_planes(k + 1, 1 - cur)
        bulk(k + 1, 1 - cur)
        early_up(k + 1)

        @pl.when(down_early & (k + 1 < DEGREE - 1))
        def _():
            early_down(k + 1)

        return carry

    lax.fori_loop(0, DEGREE - 1, step, 0)
    final = DEGREE - 1
    forward(3, True)
    turn(2)
    turn(3)
    H2[NR:NRL, :] = jnp.zeros((NRL - NR, 256), bf16)
    sq = finish(final, final % 2, True)

    N1s[...] = jnp.broadcast_to(jnp.sum(sq, 0, keepdims=True), (8, ORB))

    def n1(i):
        return remote(N1s, N1r.at[i], n1_send.at[i], n1_recv.at[i], x_peers[i], band)

    for i in range(3):
        n1(i).start()

    CO[...] = mm(PT[...], H2[...])
    LOW[...] = CO[:, 0:128].astype(bf16)

    def x1(i, h):
        j = i * N_ZH + h
        return remote(mpb.at[j], X1.at[j], x1_send.at[j], x1_recv.at[j], x_peers[i], band)

    for i in (1, 0, 2, 3):
        tx = (gx + 1 + i) % N_X
        for h in range(N_ZH):
            m = mm(RBT[h * N_X + tx], LOW[...])
            if i < 3:
                mpb[i * N_ZH + h] = m.astype(bf16)
                x1(i, h).start()
            else:
                M0[h] = m

    for i in range(3):
        n1(i).wait_recv()
    N2s[...] = N1s[...] + N1r[0] + N1r[1] + N1r[2]

    def n2(i):
        return remote(N2s, N2r.at[i], n2_send.at[i], n2_recv.at[i], y_peers[i], band)

    for i in range(7):
        n2(i).start()

    for i in range(3):
        for h in range(N_ZH):
            x1(i, h).wait_recv()
    for h in range(N_ZH):
        acc = M0[h]
        for i in range(3):
            acc = acc + X1[i * N_ZH + h].astype(f32)
        for y in range(N_Y):
            to = y * 32 + h * 16
            SF[to : to + 16, :] = acc[y * 16 : y * 16 + 16]
            SB[to : to + 16, :] = acc[y * 16 : y * 16 + 16].astype(bf16)

    def x2(i):
        row = ((gy + 1 + i) % N_Y) * 32
        return remote(
            SB.at[pl.ds(pl.multiple_of(row, 32), 32)], X2.at[i], x2_send.at[i], x2_recv.at[i],
            y_peers[i], band,
        )

    for i in (3, 2, 4, 1, 5, 0, 6):
        x2(i).start()

    total = N2s[...]
    for i in range(7):
        n2(i).wait_recv()
        total = total + N2r[i]
    N3s[...] = total
    n3 = remote(N3s, N3r, n3_sem.at[0], n3_sem.at[1], z_peer, band)
    n3.start()

    m = SF[pl.ds(pl.multiple_of(gy * 32, 32), 32), :]
    for i in range(7):
        x2(i).wait_recv()
        m = m + X2[i].astype(f32)
    SZ[...] = m
    x3 = remote(
        SZ.at[pl.ds(pl.multiple_of((1 - zh) * 16, 16), 16)], X3, x3_sem.at[0], x3_sem.at[1], z_peer, band
    )
    x3.start()

    n3.wait_recv()
    inverse = lax.rsqrt((N3s[...] + N3r[...])[0:1, :] + epsilon)
    OUT[...] = ((CO[:, 0:128] + CO[:, 128:256]) * inverse)[0:OWNED].astype(bf16)
    out_copy = pltpu.make_async_copy(OUT, out_ref, out_sem.at[0])
    out_copy.start()
    x3.wait_recv()
    margin_ref[...] = (SZ[pl.ds(pl.multiple_of(zh * 16, 16), 16), :] + X3[...]) * inverse
    out_copy.wait()
    n3.wait_send()
    x3.wait_send()

    @pl.when(has_below)
    def _():
        j_copy.wait_send()

    @pl.when(has_above)
    def _():
        u_copy.wait_send()

    def sent(k, carry):
        @pl.when(has_below)
        def _():
            down(k, Gs).wait_send()

        @pl.when(has_above)
        def _():
            up(k, cs).wait_send()

        return carry

    lax.fori_loop(0, DEGREE, sent, 0)
    send_own(False)
    for dist in range(1, N_ZL):
        forward(dist, False)
    for i in range(3):
        n1(i).wait_send()
        for h in range(N_ZH):
            x1(i, h).wait_send()
    for i in range(7):
        n2(i).wait_send()
        x2(i).wait_send()


def per_device(start_block, resident, cell_kernel, cell_scale, potential, cell_nodes, send_rows):
    vm = lambda shape, t: pltpu.VMEM(shape, t)
    dma = lambda n: pltpu.SemaphoreType.DMA((n,))
    vmem = pl.BlockSpec(memory_space=pltpu.VMEM)
    scratch = [
        vm((OWNED, ORB), bf16),
        vm((OWNED, ORB), bf16),
        vm((343, 343), bf16),
        pltpu.SMEM((4,), f32),
        vm((1, OWNED), f32),
        vm((4, 343), jnp.int32),
        pltpu.SMEM((4, 343), jnp.int32),
        vm((1, PLANE), jnp.int32),
        vm((OWNED, ORB), bf16),
        vm((2, NRP, ORB), f32),
        vm((832, 256), bf16),
        vm((2, MR, 256), f32),
        vm((4, MR, ORB), f32),
        vm((NRP, ORB), f32),
        vm((NR, ORB), f32),
        vm((NRP, ORB), f32),
        vm((8, NRL), f32),
        vm((NR, OWNP), bf16),
        vm((OWNP, NRL), bf16),
        vm((NRL, KL), bf16),
        vm((OWNP, ORB), bf16),
        vm((KL, KL), bf16),
        vm((MR, KL), bf16),
        vm((MR, KR), bf16),
        vm((56, KR), bf16),
        vm((4, MR, PLP), bf16),
        vm((4, PLP, PLP), f32),
        vm((4, MR, PLP), bf16),
        vm((PLP, PLP), bf16),
        vm((PLP, PLP), bf16),
        vm((2, PLP, PLP), bf16),
        vm((PLP, ORB), f32),
        vm((PLP, ORB), f32),
        vm((8, OWNP), f32),
        vm((8, KL), jnp.int32),
        vm((8, PLP), f32),
        vm((8, ORB, OWNP), bf16),
        vm((832, 256), bf16),
        vm((4, MR, PLP), bf16),
        vm((PLP, PLP), bf16),
        vm((2, PLP, PLP), bf16),
        vm((PLP, PLP), bf16),
        vm((2, PLP, PLP), bf16),
        vm((2, PL, ORB), f32),
        vm((PL, ORB), f32),
        vm((DEGREE, PL, ORB), bf16),
        vm((DEGREE, PL, ORB), bf16),
        vm((DEGREE, PLP, ORB), bf16),
        vm((DEGREE, PLP, ORB), bf16),
        vm((DEGREE, PLP, ORB), bf16),
        vm((DEGREE, PLP, ORB), bf16),
        vm((8, PLP), f32),
        vm((8, PLP), f32),
        vm((16, PLP), f32),
        vm((16, PLP), f32),
        vm((8, OWNP, ORB), bf16),
        vm((NRL, 256), bf16),
        vm((OWNP, ORB), bf16),
        vm((OWNP, 256), f32),
        vm((6, 128, ORB), bf16),
        vm((6, 128, ORB), bf16),
        vm((2, 128, ORB), f32),
        vm((256, ORB), f32),
        vm((256, ORB), bf16),
        vm((7, 32, ORB), bf16),
        vm((32, ORB), f32),
        vm((16, ORB), f32),
        vm((8, ORB), f32),
        vm((3, 8, ORB), f32),
        vm((8, ORB), f32),
        vm((7, 8, ORB), f32),
        vm((8, ORB), f32),
        vm((8, ORB), f32),
        dma(8), dma(8), dma(8), dma(8), dma(2), dma(2), dma(20), dma(8),
        dma(6), dma(6), dma(7), dma(7), dma(3), dma(3), dma(7), dma(7), dma(2), dma(2), dma(8), dma(1),
    ]
    return pl.pallas_call(
        kernel,
        out_shape=(
            jax.ShapeDtypeStruct((OWNED, ORB), bf16),
            jax.ShapeDtypeStruct((16, ORB), f32),
        ),
        in_specs=[pl.BlockSpec(memory_space=pl.ANY)] * 7,
        out_specs=(pl.BlockSpec(memory_space=pl.ANY), vmem),
        scratch_shapes=scratch,
        compiler_params=pltpu.CompilerParams(
            collective_id=0, has_side_effects=True, vmem_limit_bytes=56 * 1024 * 1024
        ),
        cost_estimate=pl.CostEstimate(
            flops=4_000_000_000, bytes_accessed=1_000_000, transcendentals=128
        ),
    )(
        start_block, resident, cell_kernel, cell_scale, potential.reshape(1, OWNED), cell_nodes,
        send_rows.reshape(1, PLANE),
    )


def solution(mesh):
    return jax.shard_map(
        per_device,
        mesh=mesh,
        in_specs=(
            P("domain", "band"),
            P("domain", "band"),
            P(),
            P("domain"),
            P("domain"),
            P("domain", None),
            P("domain"),
        ),
        out_specs=(P("domain", "band"), P("domain", "band")),
        check_vma=False,
    )
```

```python
import functools

import jax
import jax.numpy as jnp
from jax import lax
from jax.experimental import pallas as pl
from jax.experimental.pallas import tpu as pltpu
from jax.sharding import PartitionSpec as P

DEGREE = 8
EDGE = 7
ORB = 128
OWNED = 1014
PLANE = 169

lower_edge = 0.0
cutoff_edge = 16.0
upper_edge = 96.0
epsilon = 1e-06

NX = 13
XS = 112
NR = NX * XS
NRP = NR + 16
NRL = 1536
PL = 208
PLP = 256
MR = 392
KR = 448
KL = 384
OWNP = 1024

N_DOM = 64
N_ZH, N_X, N_Y = 2, 4, 8
N_ZL = 4

f32 = jnp.float32
bf16 = jnp.bfloat16
MESH = pl.DeviceIdType.MESH


def chebyshev_terms(degree):
    half_width = (upper_edge - cutoff_edge) / 2.0
    centre = (upper_edge + cutoff_edge) / 2.0
    sigma_now = half_width / (lower_edge - centre)
    gamma_ratio = 2.0 / sigma_now
    lead_factor = sigma_now / half_width
    recurrence = [(lead_factor, 0.0)]
    for _ in range(degree - 1):
        sigma_next = 1.0 / (gamma_ratio - sigma_now)
        recurrence.append((2.0 * sigma_next / half_width, sigma_now * sigma_next))
        sigma_now = sigma_next
    return (centre, recurrence)


CENTRE, TERMS = chebyshev_terms(DEGREE)


def mm(a, b):
    return jnp.dot(a, b, preferred_element_type=f32)


def mm_nt(a, b):
    return lax.dot_general(a, b, (((1,), (1,)), ((), ())), preferred_element_type=f32)


def mm_tn(a, b):
    return lax.dot_general(a, b, (((0,), (0,)), ((), ())), preferred_element_type=f32)


def iota(shape, dim):
    return lax.broadcasted_iota(jnp.int32, shape, dim)


def hot(cond):
    return jnp.where(cond, 1.0, 0.0).astype(bf16)


def pick(k, values):
    out = jnp.float32(values[0])
    for i in range(1, len(values)):
        out = jnp.where(k == i, jnp.float32(values[i]), out)
    return out


def kernel(
    start_hbm, res_hbm, ck_hbm, scale_hbm, pot_hbm, cn_hbm, sr_hbm,
    out_ref, margin_ref,
    start_ref, res_ref, ck_ref, scale_ref, pot_ref, cn_ref, cns_ref, sr_ref, OUT,
    V, R, O, OG, part, potc, place, prow, Pm, PT, Q, st, kpad, K1, Kp, T, KgP, KttP, KgD,
    ET, F, W2, top_col, jbot_col, pot8, cnp, srp,
    RBT, R2, KgB, M1, WT, M1T, D2, CR, CR2, Ps, Qs, Gs, cs, Gr, cr, Js, Jr, Us, Ur, RB, H2, LOW, CO, mpb, X1, M0, SF, SB, X2, N1s, N1r, N2s, N2r,
    g_send, g_recv, c_send, c_recv, j_sem, u_sem, r_send, r_recv, x1_send, x1_recv, x2_send, x2_recv,
    n1_send, n1_recv, n2_send, n2_recv, hello, in_sem, out_sem,
):
    d = lax.axis_index("domain")
    band = lax.axis_index("band")
    zh = d // (N_X * N_Y)
    gx = (d // N_Y) % N_X
    gy = d % N_Y
    zl = band // 2
    core = band % 2
    sibling = zl * 2 + (1 - core)
    has_below = d > 0
    has_above = d < N_DOM - 1
    mid = N_DOM // N_ZH
    end_y = has_above & (d % N_Y == N_Y - 1)
    first_y = has_below & (d % N_Y == 0)
    up_early = end_y | (d == mid - 2)
    up_mend = first_y | (d == mid - 1)
    down_early = first_y | (d == mid + 1)
    down_mend = end_y | (d == mid)

    given = [
        (cn_hbm, cns_ref), (cn_hbm, cn_ref), (scale_hbm, scale_ref), (sr_hbm, sr_ref),
        (start_hbm, start_ref), (ck_hbm, ck_ref), (res_hbm, res_ref), (pot_hbm, pot_ref),
    ]
    given = [pltpu.make_async_copy(a, b, in_sem.at[i]) for i, (a, b) in enumerate(given)]
    for c in given:
        c.start()

    Gr[...] = jnp.zeros_like(Gr)
    cr[...] = jnp.zeros_like(cr)
    Jr[...] = jnp.full(Jr.shape, -3.0, f32)
    Ur[0:8, :] = jnp.full((8, PLP), -4.0, f32)
    Ur[8:16, :] = jnp.zeros((8, PLP), f32)

    barrier = pltpu.get_barrier_semaphore()

    def greet(dom, bnd):
        pl.semaphore_signal(barrier, inc=1, device_id=(dom, bnd), device_id_type=MESH)

    x_peers = [(zh * N_X + (gx + i) % N_X) * N_Y + gy for i in range(1, N_X)]
    y_peers = [(zh * N_X + gx) * N_Y + (gy + i) % N_Y for i in range(1, N_Y)]
    z_peer = ((1 - zh) * N_X + gx) * N_Y + gy
    for p in [z_peer] + y_peers + x_peers:
        greet(p, band)

    @pl.when(has_below)
    def _():
        greet(d - 1, band)

    @pl.when(has_above)
    def _():
        greet(d + 1, band)

    @pl.when(zl > 0)
    def _():
        greet(d, band - 2)

    @pl.when(zl < N_ZL - 1)
    def _():
        greet(d, band + 2)

    greet(d, sibling)

    for c in given[0:3]:
        c.wait()
    corner = [cns_ref[c, 0] for c in range(4)]
    right_x = [cns_ref[c, EDGE - 1] for c in range(4)]
    right_y = [cns_ref[c, EDGE * (EDGE - 1)] for c in range(4)]
    pos = []
    for c in range(4):
        in_x = sum([jnp.where(right_x[b] == corner[c], 1, 0) for b in range(4)])
        in_y = sum([jnp.where(right_y[b] == corner[c], 1, 0) for b in range(4)])
        pos.append(in_x + 2 * in_y)
    scale = []
    for p in range(4):
        s = jnp.float32(0.0)
        for c in range(4):
            s = s + jnp.where(pos[c] == p, scale_ref[c], 0.0)
        scale.append(s)

    cnp[...] = jnp.zeros_like(cnp)
    cnp[0:4, 0:343] = cn_ref[...]
    row8 = iota((8, KL), 0)
    full = jnp.zeros((8, KL), jnp.int32)
    for c in range(4):
        line = jnp.broadcast_to(cnp[c : c + 1, :], (8, KL))
        full = full + jnp.where((row8 & 3) == pos[c], line, 0)
    cn8 = jnp.where(row8 < 4, full >> 5, full & 31).astype(f32).astype(bf16)

    rr = iota((XS, KL), 0)
    ln = iota((XS, KL), 1)
    yy = rr >> 3
    zz = rr & 7
    k_base = jnp.where(
        (zz < EDGE) & (yy < NX), zz * 49 + jnp.where(yy > 6, yy - 6, yy) * 7, -1000
    )
    diff = k_base - ln
    l8 = iota((XS, 8), 1)
    y8 = iota((XS, 8), 0) >> 3
    z128 = iota((XS, 128), 0) & 7
    y128 = iota((XS, 128), 0) >> 3
    top_row = (z128 < EDGE) & (y128 < NX)
    own_row = (z128 < EDGE - 1) & (y128 < NX)
    weights = jnp.where(iota((8, 128), 0) < 4, 32.0, 1.0).astype(bf16)
    lane = iota((XS, 128), 1).astype(f32)
    for X in range(NX):
        x = X if X <= 6 else X - 6
        one = hot(diff == -x)
        Q[X * XS : (X + 1) * XS, :] = one
        a1 = mm_nt(one, cn8)
        cell = jnp.where(y8 > 6, 2, 0) + (1 if X > 6 else 0)
        a1 = jnp.where((l8 & 3) == cell, a1, 0.0).astype(bf16)
        pl_x = mm(a1, weights)
        place[X * XS : (X + 1) * XS, :] = jnp.where(top_row, pl_x, -1.0)
        own = jnp.where(own_row, pl_x, -1.0)
        for t in range(8):
            Pm[X * XS : (X + 1) * XS, t * 128 : (t + 1) * 128] = hot(own == lane + 128.0 * t)
    place[NR:NRP, :] = jnp.full((NRP - NR, 128), -1.0, f32)

    given[3].wait()
    srp[...] = jnp.full(srp.shape, -5.0, f32)
    srp[0:1, 0:PLANE] = sr_ref[...].astype(f32)
    top_col[...] = jnp.full(top_col.shape, -1.0, f32)
    yrow = iota((16, 128), 0)
    lane16 = iota((16, 128), 1)
    ET[...] = jnp.zeros_like(ET)
    for X in range(NX):
        b0 = jnp.concatenate(
            [place[pl.ds(X * XS, 8, stride=8), :], place[pl.ds(X * XS + 64, 8, stride=8), :]], 0
        )
        b0 = jnp.where(yrow < NX, b0, -1.0)
        for t in range(2):
            ET[X * 16 : X * 16 + 16, t * 128 : (t + 1) * 128] = hot(
                b0 == srp[0:1, t * 128 : (t + 1) * 128]
            )
        t0 = jnp.concatenate(
            [place[pl.ds(X * XS + 6, 8, stride=8), :], place[pl.ds(X * XS + 54, 8, stride=8), :]],
            0,
        )
        top_col[X * 16 : X * 16 + 16, :] = jnp.where((yrow & 7) < EDGE, t0 - float(OWNED), -1.0)
    jm = iota((PLP, 128), 0).astype(f32).astype(bf16)
    p_row = iota((PLP, 128), 0)
    jb = mm(ET[...], jm)
    jbot_col[...] = jnp.where(((p_row & 15) < NX) & (p_row < PL), jb, -2.0)
    p_lane = iota((8, PLP), 1)
    p_ok = ((p_lane & 15) < NX) & (p_lane < PL)
    jr = mm_nt(iota((8, PLP), 1).astype(f32).astype(bf16), ET[...])
    Js[...] = jnp.where(p_ok, jr, -2.0)

    pr = iota((PLP, KL), 0)
    pln = iota((PLP, KL), 1)
    pX = pr >> 4
    pY = pr & 15
    ty = pr & 7
    tcy = (pr >> 3) & 1
    t_in = (pX < NX) & (ty < EDGE)
    ox = jnp.where(pX > 6, pX - 6, pX)
    q_top = hot(t_in & (294 + ty * 7 + ox == pln))
    at = mm_nt(cn8, q_top)
    lX = p_lane >> 4
    l_cell = jnp.where(lX > 6, 1, 0) + ((p_lane >> 3) & 1) * 2
    t_ok = ((p_lane & 7) < EDGE) & (p_lane < PL)
    r8 = iota((8, PLP), 0)
    at = jnp.where((r8 & 3) == l_cell, at, 0.0) * jnp.where(r8 < 4, 32.0, 1.0)
    top_line = jnp.sum(at, 0, keepdims=True) - float(OWNED)
    Us[0:8, :] = jnp.where(t_ok, jnp.broadcast_to(top_line, (8, PLP)), -1.0)
    srow = iota((8, PLP), 0)
    stile = jnp.zeros((8, PLP), f32)
    for c in range(4):
        stile = jnp.where(srow == c, scale[c], stile)
    Us[8:16, :] = stile

    given[6].wait()
    RB[band, 1008:1024, :] = jnp.zeros((16, ORB), bf16)
    RB[band, 0:OWNED, :] = res_ref[...]

    def remote(src, dst, ssem, rsem, dom, bnd):
        return pltpu.make_async_remote_copy(
            src_ref=src, dst_ref=dst, send_sem=ssem, recv_sem=rsem,
            device_id=(dom, bnd), device_id_type=MESH,
        )

    j_copy = remote(Js, Jr, j_sem.at[0], j_sem.at[1], d - 1, band)
    u_copy = remote(Us, Ur, u_sem.at[0], u_sem.at[1], d + 1, band)

    def turn(dist):
        if dist == 0:
            block(sibling, sibling, 0).wait_recv()
            RBT[band] = RB[band].T
            RBT[sibling] = RB[sibling].T
            return

        def both(src):
            other = src + 1 - 2 * core
            block(other, sibling, 0).wait_recv()
            RBT[src] = RB[src].T
            RBT[other] = RB[other].T

        @pl.when(zl >= dist)
        def _():
            both(band - 2 * dist)

        @pl.when(zl + dist <= N_ZL - 1)
        def _():
            both(band + 2 * dist)

    def block(src, to, s):
        return remote(RB.at[src], RB.at[src], r_send.at[s], r_recv.at[src], d, to)

    def send_own(start):
        def act(c):
            c.start() if start else c.wait_send()

        @pl.when(zl < N_ZL - 1)
        def _():
            act(block(band, band + 2, 0))

        @pl.when(zl > 0)
        def _():
            act(block(band, band - 2, 1))

        act(block(band, sibling, 2))

    def forward(dist, start):
        @pl.when(zl >= dist)
        def _():
            src = band - 2 * dist
            if start:
                block(src, sibling, 0).wait_recv()

            @pl.when(zl < N_ZL - 1)
            def _():
                c = block(src, band + 2, 3 * dist)
                c.start() if start else c.wait_send()

            c = block(src, sibling, 3 * dist + 1)
            c.start() if start else c.wait_send()

        @pl.when(zl + dist <= N_ZL - 1)
        def _():
            src = band + 2 * dist
            if start:
                block(src, sibling, 0).wait_recv()

            @pl.when(zl > 0)
            def _():
                c = block(src, band - 2, 9 + 3 * dist)
                c.start() if start else c.wait_send()

            c = block(src, sibling, 10 + 3 * dist)
            c.start() if start else c.wait_send()

    given[4].wait()
    st[1008:1024, :] = jnp.zeros((16, ORB), bf16)
    st[0:OWNED, :] = start_ref[...]
    V[0, 0:NR, :] = mm(Pm[...], st[...])
    V[0, NR:NRP, :] = jnp.zeros((NRP - NR, ORB), f32)
    V[1, :, :] = jnp.zeros((NRP, ORB), f32)
    part[...] = jnp.zeros_like(part)
    zero8 = jnp.zeros((8, ORB), f32)
    for X in range(NX):
        R[X * 64 : X * 64 + 64, 0:128] = V[0, X * XS : X * XS + 64, :].astype(bf16)
        R[X * 64 : X * 64 + 64, 128:256] = V[0, X * XS + 48 : X * XS + 112, :].astype(bf16)

    given[5].wait()
    kpad[...] = jnp.zeros_like(kpad)
    kpad[0:343, 0:343] = ck_ref[...]
    kmat = kpad[...]
    r56 = iota((56, KL), 0)
    k56 = jnp.where((r56 & 7) < 7, (r56 & 7) * 49 + (r56 >> 3) * 7, -1000) - iota((56, KL), 1)
    row_hot = jnp.concatenate([jnp.where(k56 == -x, 1.0, 0.0) for x in range(7)], 0).astype(bf16)
    r64 = iota((64, KL), 0)
    k64 = (
        jnp.where(((r64 & 7) < 7) & (r64 < 56), (r64 & 7) * 49 + (r64 >> 3) * 7, -1000)
        - iota((64, KL), 1)
    )
    col_hot = jnp.concatenate([hot(k64 == -x) for x in range(7)], 0)
    K1[...] = mm(row_hot, kmat).astype(bf16)
    Kp[...] = mm_nt(K1[...], col_hot).astype(bf16)
    r8k = iota((8, KL), 0)
    l8k = iota((8, KL), 1)
    kt = jnp.where(r8k < EDGE, 294 + r8k * 7, -1000) - l8k
    kb = jnp.where(r8k < EDGE, r8k * 7, -1000) - l8k
    none8 = jnp.zeros((8, KL), f32)
    t_hot = jnp.concatenate([jnp.where(kt == -x, 1.0, 0.0) for x in range(7)] + [none8], 0).astype(bf16)
    b_hot = jnp.concatenate([jnp.where(kb == -x, 1.0, 0.0) for x in range(7)] + [none8], 0).astype(bf16)
    top_k = mm(t_hot, kmat).astype(bf16)
    T[...] = mm_nt(top_k, col_hot)[0:56].astype(bf16)

    def down(k, src):
        return remote(
            src.at[k, pl.ds(0, PL)], Gr.at[k, pl.ds(0, PL)], g_send.at[k], g_recv.at[k], d - 1, band
        )

    def up(k, src):
        return remote(
            src.at[k, pl.ds(0, PL)], cr.at[k, pl.ds(0, PL)], c_send.at[k], c_recv.at[k], d + 1, band
        )

    def lowest_plane(v, out, k, more=None):
        for X in range(NX):
            lo = v[pl.ds(X * XS, 8, stride=8), :]
            hi = v[pl.ds(X * XS + 64, 8, stride=8), :]
            both = jnp.concatenate([lo, hi], 0)
            if more is not None:
                both = both + more[X * 16 : X * 16 + 16]
            out[k, X * 16 : X * 16 + 16, :] = both.astype(bf16)

    def top_sums(r, sc):
        parts = [mm(T[...], r[384 * cx : 384 * cx + KR, :]) for cx in range(2)]
        out = []
        for X in range(NX):
            tiles = []
            for cy in range(2):
                t = None
                for cx in range(2):
                    x = X - 6 * cx
                    if 0 <= x < 7:
                        p = parts[cx][x * 8 : x * 8 + 8, cy * 128 : (cy + 1) * 128] * sc[cx + 2 * cy]
                        t = p if t is None else t + p
                tiles.append(t)
            out.append((X * 16, X * 16 + 16, jnp.concatenate(tiles, 0)))
        return out

    def prepare_down(k, cur):
        Gs[k, PL:PLP, :] = jnp.zeros((PLP - PL, ORB), bf16)
        lowest_plane(V.at[cur], Gs, k)

    def prepare_up(k):
        cs[k, PL:PLP, :] = jnp.zeros((PLP - PL, ORB), bf16)
        for lo, hi, value in top_sums(R, scale):
            cs[k, lo:hi, :] = value.astype(bf16)

    def to_operand(r, X, flat):
        r[X * 64 : X * 64 + 64, 0:128] = flat[0:64].astype(bf16)
        r[X * 64 : X * 64 + 64, 128:256] = jnp.concatenate([flat[48:104], zero8], 0).astype(bf16)

    def send_planes(k, cur):
        prepare_down(k, cur)

        @pl.when(has_below & jnp.logical_not(down_early))
        def _():
            down(k, Gs).start()

        for X in range(NX):
            to_operand(R, X, V[cur, X * XS : X * XS + 104, :])
        prepare_up(k)

        @pl.when(has_above & jnp.logical_not(up_early))
        def _():
            up(k, cs).start()

    prepare_down(0, 0)
    prepare_up(0)

    ones = lambda cond: jnp.where(cond, 1, 0)
    count = (
        ones(has_below) + ones(has_above) + ones(zl > 0) + ones(zl < N_ZL - 1)
        + 2 + len(x_peers) + len(y_peers)
    )
    pl.semaphore_wait(barrier, count)

    for p in y_peers:
        pl.semaphore_signal(hello, inc=1, device_id=(p, band), device_id_type=MESH)

    @pl.when(has_below)
    def _():
        j_copy.start()

    @pl.when(has_above)
    def _():
        u_copy.start()

    @pl.when(has_below)
    def _():
        down(0, Gs).start()

    @pl.when(has_above)
    def _():
        up(0, cs).start()

    send_own(True)

    given[7].wait()
    pot8[...] = jnp.zeros_like(pot8)
    pot = pot_ref[...]
    p_hi = pot.astype(bf16)
    rest = pot - p_hi.astype(f32)
    p_mid = rest.astype(bf16)
    p_lo = (rest - p_mid.astype(f32)).astype(bf16)
    pot8[0:1, 0:OWNED] = p_hi.astype(f32)
    pot8[1:2, 0:OWNED] = p_mid.astype(f32)
    pot8[2:3, 0:OWNED] = p_lo.astype(f32)
    pcol = mm_nt(Pm[...], pot8[...].astype(bf16)).astype(bf16)
    potc[...] = mm(pcol, jnp.ones((8, 128), bf16)) - CENTRE

    q_l = iota((PLP, 64), 1)
    q_p = iota((PLP, 64), 0)
    q_in = ((q_l & 7) < EDGE) & (q_l < 56)

    def in_top(c):
        cx, cy = c % 2, c // 2
        y_ok = (((q_p >> 3) & 1) == cy) & ((q_p & 7) == (q_l & 7))
        return hot(((q_p >> 4) - 6 * cx == (q_l >> 3)) & y_ok & q_in)

    def in_bottom(c):
        cx, cy = c % 2, c // 2
        return hot(((q_p >> 4) - 6 * cx == (q_l >> 3)) & ((q_p & 15) - 6 * cy == (q_l & 7)) & q_in)

    k_tt = mm_nt(top_k, t_hot).astype(bf16)
    k_g = mm_nt(K1[...], t_hot).astype(bf16)
    for c in range(4):
        e_top = in_top(c)
        KgP[c] = mm_nt(k_g, e_top).astype(bf16)
        KttP[c] = mm_nt(mm(e_top, k_tt).astype(bf16), e_top)

    lin = iota((8, NRL), 1)
    lin_x = jnp.floor((lin.astype(f32) + 0.5) * (1.0 / XS)).astype(jnp.int32)
    lin_r = lin - lin_x * XS
    lin_y = lin_r >> 3
    lin_z = lin_r & 7
    lin_cell = jnp.where(lin_x > 6, 1, 0) + jnp.where(lin_y > 6, 2, 0)
    lin_8 = iota((8, NRL), 0)
    Q[NR:NRL, :] = jnp.zeros((NRL - NR, KL), bf16)
    ar = mm_nt(cn8, Q[...])
    ar = jnp.where((lin_8 & 3) == lin_cell, ar, 0.0) * jnp.where(lin_8 < 4, 32.0, 1.0)
    ar = jnp.broadcast_to(jnp.sum(ar, 0, keepdims=True), (8, NRL))
    prow[...] = jnp.where((lin_x < NX) & (lin_y < NX) & (lin_z < EDGE - 1), ar, -1.0)
    n16 = iota((16, NRL), 0).astype(f32)

    def fill(i, carry):
        base = (i * 16).astype(f32)
        PT[pl.ds(pl.multiple_of(i * 16, 16), 16), :] = hot(prow[0:1, :] == n16 + base)
        return carry


    mask8 = jnp.where(iota((8, ORB), 0) < EDGE - 1, 1.0, 0.0)

    def spread(ref_of, X, factor):
        lo, hi = None, None
        for cx in range(2):
            x = X - 6 * cx
            if 0 <= x < 7:
                a = ref_of(cx, 0, x).reshape(7, 8, ORB) * factor(cx, 0)
                b = ref_of(cx, 1, x).reshape(7, 8, ORB) * factor(cx, 1)
                lo = a if lo is None else lo + a
                hi = b if hi is None else hi + b
        return jnp.concatenate([lo[0:6], lo[6:7] + hi[0:1], hi[1:7]], 0)

    def bulk(k, cur):
        nxt = 1 - cur
        a = pick(k, [t[0] for t in TERMS])
        b = pick(k, [t[1] for t in TERMS])
        am = mask8 * a
        for cx in range(2):
            O[cx] = mm(Kp[...], R[384 * cx : 384 * cx + KR, :])
        for X in range(NX):
            rows = slice(X * XS, X * XS + 104)
            s = spread(
                lambda cx, cy, x: O[cx, x * 56 : x * 56 + 56, cy * 128 : (cy + 1) * 128],
                X,
                lambda cx, cy: scale[cx + 2 * cy],
            )
            v = V[cur, rows, :].reshape(NX, 8, ORB)
            u = V[nxt, rows, :].reshape(NX, 8, ORB)
            pc = potc[rows, :].reshape(NX, 8, ORB)
            new = (s + pc * v) * am[None] - b * u
            part[rows, :] = new.reshape(104, ORB)

    bulk(0, 0)

    def halves(v):
        hi = v.astype(bf16)
        return hi, (v - hi.astype(f32)).astype(bf16)

    def plane_to_plane(rows_top, onward):
        total = jnp.zeros((PLP, PLP), f32)
        if rows_top:
            block_k = mm_nt(top_k, b_hot).astype(bf16)
        else:
            block_k = mm_nt(mm(b_hot, kmat).astype(bf16), t_hot).astype(bf16)
        for c in range(4):
            one, two = (in_top(c), in_bottom(c)) if rows_top else (in_bottom(c), in_top(c))
            total = total + mm_nt(mm(one, block_k).astype(bf16), two) * scale[c]
        hi = total.astype(bf16)
        lo = (total - hi.astype(f32)).astype(bf16)
        total = mm(hi, onward) + mm(lo, onward)
        hi = total.astype(bf16)
        D2[0] = hi
        D2[1] = (total - hi.astype(f32)).astype(bf16)

    def add_plane(v, e):
        for X in range(NX):
            lo = pl.ds(X * XS, 8, stride=8)
            hi = pl.ds(X * XS + 64, 8, stride=8)
            v[lo, :] = v[lo, :] + e[X * 16 : X * 16 + 8]
            v[hi, :] = v[hi, :] + e[X * 16 + 8 : X * 16 + 16]

    def ghost(X, am, sc):
        return spread(
            lambda cx, cy, x: OG[cx + 2 * cy, x * 56 : x * 56 + 56, :],
            X,
            lambda cx, cy: (am * sc[cx + 2 * cy])[None],
        )

    def ahead(k):
        am = mask8 * pick(k - 1, [t[0] for t in TERMS])
        sb = [Ur[8 + c : 9 + c, 0:128] for c in range(4)]
        for c in range(4):
            OG[c] = mm(KgB[c], Gs[k - 1])
        for X in range(NX):
            to_operand(R2, X, ghost(X, am, sb).reshape(104, ORB))
        for lo, hi, value in top_sums(R2, sb):
            CR[lax.rem(k, 2), lo:hi, :] = value

    def mend_sums(k):
        cr[k, 0:PL, :] = (cr[k, 0:PL, :].astype(f32) + CR[lax.rem(k, 2)]).astype(bf16)

    def mend_plane(k):
        before = pick(k - 1, [t[0] for t in TERMS])

        @pl.when((k != 1) | (d != mid - 1))
        def _():
            Gr[k] = (Gr[k].astype(f32) + mm(M1T[...], cs[k - 1]) * before).astype(bf16)

        @pl.when((k == 1) & (d == mid - 1))
        def _():
            own = mm(M1[...], Gr[0]).astype(bf16)
            sums = cs[0].astype(f32) + mm(WT[0], own) + mm(WT[1], own)
            Gr[k] = (Gr[k].astype(f32) + mm(M1T[...], sums.astype(bf16)) * before).astype(bf16)

    def early_up(k):
        a = pick(k, [t[0] for t in TERMS])
        g = Gs[k]
        add_plane(part, (mm(W2[0], g) + mm(W2[1], g)) * a)

        @pl.when(up_early & (k < DEGREE - 1))
        def _():
            for X in range(NX):
                to_operand(R2, X, part[X * XS : X * XS + 104, :])
            for lo, hi, value in top_sums(R2, scale):
                CR2[lo:hi, :] = value

            @pl.when(has_below)
            def _():
                up(k, cs).wait_recv()

            @pl.when(up_mend & (k >= 1))
            def _():
                mend_sums(k)

            more = (mm(D2[0], cr[k]) + mm(D2[1], cr[k])) * a
            Ps[k + 1] = (CR2[...] + more[0:PL]).astype(bf16)
            up(k + 1, Ps).start()

    def early_down(k):
        a = pick(k, [t[0] for t in TERMS])

        @pl.when(has_above)
        def _():
            down(k, Gs).wait_recv()

        @pl.when(down_mend & (k >= 1))
        def _():
            mend_plane(k)

        more = (mm(D2[0], Gr[k]) + mm(D2[1], Gr[k])) * a
        lowest_plane(part, Qs, k + 1, more)
        down(k + 1, Qs).start()

    def finish(k, cur, last):
        nxt = 1 - cur
        a = pick(k, [t[0] for t in TERMS])
        am = mask8 * a
        rest_down = has_above if last else has_above & jnp.logical_not(down_early)
        rest_up = has_below if last else has_below & jnp.logical_not(up_early)

        @pl.when(rest_down)
        def _():
            down(k, Gs).wait_recv()

        @pl.when(rest_down & down_mend & (k >= 1))
        def _():
            mend_plane(k)

        for c in range(4):
            OG[c] = mm(KgD[c], Gr[k])
        for X in range(NX):
            rows = slice(X * XS, X * XS + 104)
            new = part[rows, :].reshape(NX, 8, ORB) + ghost(X, am, scale)
            V[nxt, rows, :] = new.reshape(104, ORB)

        @pl.when(rest_up)
        def _():
            up(k, cs).wait_recv()

        @pl.when(rest_up & up_mend & (k >= 1))
        def _():
            mend_sums(k)

        add_plane(V.at[nxt], mm(F[...], cr[k]) * a)
        if not last:
            return None
        sq = jnp.zeros((8, ORB), f32)
        for X in range(NX):
            padded = V[nxt, X * XS : (X + 1) * XS, :]
            cube = padded.reshape(NX + 1, 8, ORB)
            sq = sq + jnp.sum(cube * cube, 0)
            top = padded.astype(bf16)
            H2[X * XS : (X + 1) * XS, 0:128] = top
            H2[X * XS : (X + 1) * XS, 128:256] = (padded - top.astype(f32)).astype(bf16)
        return sq

    @pl.when(has_above)
    def _():
        j_copy.wait_recv()

    tc = top_col[...]
    M1[...] = jnp.concatenate([hot(tc == Jr[0:1, t * 128 : (t + 1) * 128]) for t in range(2)], 1)

    @pl.when(down_early)
    def _():
        plane_to_plane(False, M1[...])

    @pl.when(d == mid)
    def _():
        early_down(0)

    @pl.when(has_below)
    def _():
        u_copy.wait_recv()

    jc = jbot_col[...]
    F[...] = jnp.concatenate([hot(jc == Ur[0:1, t * 128 : (t + 1) * 128]) for t in range(2)], 1)

    @pl.when(up_early)
    def _():
        plane_to_plane(True, F[...])

    w = jnp.zeros((PLP, PLP), f32)
    for c in range(4):
        w = w + KttP[c] * Ur[8 + c : 9 + c, :]
    fm = F[...]
    w_hi, w_lo = halves(w)
    w = mm_nt(mm(fm, w_hi).astype(bf16), fm) + mm_nt(mm(fm, w_lo).astype(bf16), fm)
    W2[0], W2[1] = halves(w)
    early_up(0)

    @pl.when(down_early & (d != mid))
    def _():
        early_down(0)

    for c in range(4):
        KgD[c] = mm(KgP[c], M1[...]).astype(bf16)

    @pl.when(down_mend)
    def _():
        eye = hot(iota((PLP, PLP), 0) == iota((PLP, PLP), 1))
        M1T[...] = mm_nt(eye, M1[...]).astype(bf16)

    @pl.when(d == mid - 1)
    def _():
        total = KttP[0] * scale[0]
        for c in range(1, 4):
            total = total + KttP[c] * scale[c]
        WT[0], WT[1] = halves(total)

    @pl.when(up_mend)
    def _():
        for c in range(4):
            KgB[c] = mm_nt(KgP[c], F[...]).astype(bf16)

    def step(k, carry):
        cur = lax.rem(k, 2)
        @pl.when(up_mend)
        def _():
            ahead(k + 1)

        for dist in range(1, N_ZL - 1):

            @pl.when(k == 2 * dist + 1)
            def _(dist=dist):
                forward(dist, True)

        for dist in range(2):

            @pl.when(k == 4 * dist + 2)
            def _(dist=dist):
                turn(dist)

        lax.fori_loop(k * 10, jnp.minimum(k * 10 + 10, OWNP // 16), fill, 0)
        finish(k, cur, False)
        send_planes(k + 1, 1 - cur)
        bulk(k + 1, 1 - cur)
        early_up(k + 1)

        @pl.when(down_early & (k + 1 < DEGREE - 1))
        def _():
            early_down(k + 1)

        return carry

    lax.fori_loop(0, DEGREE - 1, step, 0)
    final = DEGREE - 1
    forward(3, True)
    turn(2)
    turn(3)
    H2[NR:NRL, :] = jnp.zeros((NRL - NR, 256), bf16)
    sq = finish(final, final % 2, True)

    N1s[...] = jnp.broadcast_to(jnp.sum(sq, 0, keepdims=True), (8, ORB))

    def n1(i):
        return remote(N1s, N1r.at[i], n1_send.at[i], n1_recv.at[i], x_peers[i], band)

    for i in range(3):
        n1(i).start()

    CO[...] = mm(PT[...], H2[...])
    LOW[...] = CO[:, 0:128].astype(bf16)

    def x1(i, h):
        j = i * N_ZH + h
        return remote(mpb.at[j], X1.at[j], x1_send.at[j], x1_recv.at[j], x_peers[i], band)

    for i in (1, 0, 2, 3):
        tx = (gx + 1 + i) % N_X
        for h in range(N_ZH):
            m = mm(RBT[h * N_X + tx], LOW[...])
            if i < 3:
                mpb[i * N_ZH + h] = m.astype(bf16)
                x1(i, h).start()
            else:
                M0[h] = m

    for i in range(3):
        n1(i).wait_recv()
    N2s[...] = N1s[...] + N1r[0] + N1r[1] + N1r[2]

    yz_off = [(a, b) for a in range(N_ZH) for b in range(N_Y) if (a, b) != (0, 0)]
    far_first = sorted(range(15), key=lambda i: (-yz_off[i][0], abs(yz_off[i][1] - 4)))

    def to_yz(i):
        return (zh + yz_off[i][0]) % N_ZH, (gy + yz_off[i][1]) % N_Y

    def n2(i):
        to_z, to_y = to_yz(i)
        return remote(
            N2s, N2r.at[i], n2_send.at[i], n2_recv.at[i], (to_z * N_X + gx) * N_Y + to_y, band
        )

    pl.semaphore_wait(hello, len(y_peers))
    for i in far_first:
        n2(i).start()

    for i in range(3):
        for h in range(N_ZH):
            x1(i, h).wait_recv()
    for h in range(N_ZH):
        acc = M0[h]
        for i in range(3):
            acc = acc + X1[i * N_ZH + h].astype(f32)
        for y in range(N_Y):
            to = y * 32 + h * 16
            SF[to : to + 16, :] = acc[y * 16 : y * 16 + 16]
            SB[to : to + 16, :] = acc[y * 16 : y * 16 + 16].astype(bf16)

    def x2(i):
        to_z, to_y = to_yz(i)
        return remote(
            SB.at[pl.ds(pl.multiple_of(to_y * 32 + to_z * 16, 16), 16)], X2.at[i], x2_send.at[i],
            x2_recv.at[i], (to_z * N_X + gx) * N_Y + to_y, band,
        )

    for i in far_first:
        x2(i).start()

    total = N2s[...]
    for i in range(15):
        n2(i).wait_recv()
        total = total + N2r[i]
    inverse = lax.rsqrt(total[0:1, :] + epsilon)
    OUT[...] = ((CO[:, 0:128] + CO[:, 128:256]) * inverse)[0:OWNED].astype(bf16)
    out_copy = pltpu.make_async_copy(OUT, out_ref, out_sem.at[0])
    out_copy.start()

    m = SF[pl.ds(pl.multiple_of(gy * 32 + zh * 16, 16), 16), :]
    for i in range(15):
        x2(i).wait_recv()
        m = m + X2[i].astype(f32)
    margin_ref[...] = m * inverse
    out_copy.wait()

    @pl.when(has_below)
    def _():
        j_copy.wait_send()

    @pl.when(has_above)
    def _():
        u_copy.wait_send()

    def sent(k, carry):
        @pl.when(has_below)
        def _():
            down(k, Gs).wait_send()

        @pl.when(has_above)
        def _():
            up(k, cs).wait_send()

        return carry

    lax.fori_loop(0, DEGREE, sent, 0)
    send_own(False)
    for dist in range(1, N_ZL):
        forward(dist, False)
    for i in range(3):
        n1(i).wait_send()
        for h in range(N_ZH):
            x1(i, h).wait_send()
    for i in range(15):
        n2(i).wait_send()
        x2(i).wait_send()


def per_device(start_block, resident, cell_kernel, cell_scale, potential, cell_nodes, send_rows):
    vm = lambda shape, t: pltpu.VMEM(shape, t)
    dma = lambda n: pltpu.SemaphoreType.DMA((n,))
    vmem = pl.BlockSpec(memory_space=pltpu.VMEM)
    scratch = [
        vm((OWNED, ORB), bf16),
        vm((OWNED, ORB), bf16),
        vm((343, 343), bf16),
        pltpu.SMEM((4,), f32),
        vm((1, OWNED), f32),
        vm((4, 343), jnp.int32),
        pltpu.SMEM((4, 343), jnp.int32),
        vm((1, PLANE), jnp.int32),
        vm((OWNED, ORB), bf16),
        vm((2, NRP, ORB), f32),
        vm((832, 256), bf16),
        vm((2, MR, 256), f32),
        vm((4, MR, ORB), f32),
        vm((NRP, ORB), f32),
        vm((NR, ORB), f32),
        vm((NRP, ORB), f32),
        vm((8, NRL), f32),
        vm((NR, OWNP), bf16),
        vm((OWNP, NRL), bf16),
        vm((NRL, KL), bf16),
        vm((OWNP, ORB), bf16),
        vm((KL, KL), bf16),
        vm((MR, KL), bf16),
        vm((MR, KR), bf16),
        vm((56, KR), bf16),
        vm((4, MR, PLP), bf16),
        vm((4, PLP, PLP), f32),
        vm((4, MR, PLP), bf16),
        vm((PLP, PLP), bf16),
        vm((PLP, PLP), bf16),
        vm((2, PLP, PLP), bf16),
        vm((PLP, ORB), f32),
        vm((PLP, ORB), f32),
        vm((8, OWNP), f32),
        vm((8, KL), jnp.int32),
        vm((8, PLP), f32),
        vm((8, ORB, OWNP), bf16),
        vm((832, 256), bf16),
        vm((4, MR, PLP), bf16),
        vm((PLP, PLP), bf16),
        vm((2, PLP, PLP), bf16),
        vm((PLP, PLP), bf16),
        vm((2, PLP, PLP), bf16),
        vm((2, PL, ORB), f32),
        vm((PL, ORB), f32),
        vm((DEGREE, PL, ORB), bf16),
        vm((DEGREE, PL, ORB), bf16),
        vm((DEGREE, PLP, ORB), bf16),
        vm((DEGREE, PLP, ORB), bf16),
        vm((DEGREE, PLP, ORB), bf16),
        vm((DEGREE, PLP, ORB), bf16),
        vm((8, PLP), f32),
        vm((8, PLP), f32),
        vm((16, PLP), f32),
        vm((16, PLP), f32),
        vm((8, OWNP, ORB), bf16),
        vm((NRL, 256), bf16),
        vm((OWNP, ORB), bf16),
        vm((OWNP, 256), f32),
        vm((6, 128, ORB), bf16),
        vm((6, 128, ORB), bf16),
        vm((2, 128, ORB), f32),
        vm((256, ORB), f32),
        vm((256, ORB), bf16),
        vm((15, 16, ORB), bf16),
        vm((8, ORB), f32),
        vm((3, 8, ORB), f32),
        vm((8, ORB), f32),
        vm((15, 8, ORB), f32),
        dma(8), dma(8), dma(8), dma(8), dma(2), dma(2), dma(20), dma(8),
        dma(6), dma(6), dma(15), dma(15), dma(3), dma(3), dma(15), dma(15),
        pltpu.SemaphoreType.REGULAR, dma(8), dma(1),
    ]
    return pl.pallas_call(
        kernel,
        out_shape=(
            jax.ShapeDtypeStruct((OWNED, ORB), bf16),
            jax.ShapeDtypeStruct((16, ORB), f32),
        ),
        in_specs=[pl.BlockSpec(memory_space=pl.ANY)] * 7,
        out_specs=(pl.BlockSpec(memory_space=pl.ANY), vmem),
        scratch_shapes=scratch,
        compiler_params=pltpu.CompilerParams(
            collective_id=0, has_side_effects=True, vmem_limit_bytes=56 * 1024 * 1024
        ),
        cost_estimate=pl.CostEstimate(
            flops=4_000_000_000, bytes_accessed=1_000_000, transcendentals=128
        ),
    )(
        start_block, resident, cell_kernel, cell_scale, potential.reshape(1, OWNED), cell_nodes,
        send_rows.reshape(1, PLANE),
    )


def solution(mesh):
    return jax.shard_map(
        per_device,
        mesh=mesh,
        in_specs=(
            P("domain", "band"),
            P("domain", "band"),
            P(),
            P("domain"),
            P("domain"),
            P("domain", None),
            P("domain"),
        ),
        out_specs=(P("domain", "band"), P("domain", "band")),
        check_vma=False,
    )
```

```python
import functools

import jax
import jax.numpy as jnp
from jax import lax
from jax.experimental import pallas as pl
from jax.experimental.pallas import tpu as pltpu
from jax.sharding import PartitionSpec as P

DEGREE = 8
EDGE = 7
ORB = 128
OWNED = 1014
PLANE = 169

lower_edge = 0.0
cutoff_edge = 16.0
upper_edge = 96.0
epsilon = 1e-06

NX = 13
XS = 112
NR = NX * XS
NRP = NR + 16
NRL = 1536
PL = 208
PLP = 256
MR = 392
KR = 448
KL = 384
OWNP = 1024

N_DOM = 64
N_ZH, N_X, N_Y = 2, 4, 8
N_ZL = 4

f32 = jnp.float32
bf16 = jnp.bfloat16
MESH = pl.DeviceIdType.MESH


def chebyshev_terms(degree):
    half_width = (upper_edge - cutoff_edge) / 2.0
    centre = (upper_edge + cutoff_edge) / 2.0
    sigma_now = half_width / (lower_edge - centre)
    gamma_ratio = 2.0 / sigma_now
    lead_factor = sigma_now / half_width
    recurrence = [(lead_factor, 0.0)]
    for _ in range(degree - 1):
        sigma_next = 1.0 / (gamma_ratio - sigma_now)
        recurrence.append((2.0 * sigma_next / half_width, sigma_now * sigma_next))
        sigma_now = sigma_next
    return (centre, recurrence)


CENTRE, TERMS = chebyshev_terms(DEGREE)


def mm(a, b):
    return jnp.dot(a, b, preferred_element_type=f32)


def mm_nt(a, b):
    return lax.dot_general(a, b, (((1,), (1,)), ((), ())), preferred_element_type=f32)


def mm_tn(a, b):
    return lax.dot_general(a, b, (((0,), (0,)), ((), ())), preferred_element_type=f32)


def iota(shape, dim):
    return lax.broadcasted_iota(jnp.int32, shape, dim)


def hot(cond):
    return jnp.where(cond, 1.0, 0.0).astype(bf16)


def pick(k, values):
    out = jnp.float32(values[0])
    for i in range(1, len(values)):
        out = jnp.where(k == i, jnp.float32(values[i]), out)
    return out


def kernel(
    start_hbm, res_hbm, ck_hbm, scale_hbm, pot_hbm, cn_hbm, sr_hbm,
    out_ref, margin_ref,
    start_ref, res_ref, ck_ref, scale_ref, pot_ref, cn_ref, cns_ref, sr_ref, OUT,
    V, R, O, OG, part, potc, place, prow, Pm, PT, Q, st, kpad, K1, Kp, T, KgP, KttP, KgD,
    ET, F, W2, top_col, jbot_col, pot8, cnp, srp,
    RBT, R2, KgB, M1, WT, M1T, D2, CR, CR2, Ps, Qs, Gs, cs, Gr, cr, Js, Jr, Us, Ur, RB, H2, LOW, CO, mpb, X1, M0, SF, SB, X2, N1s, N1r, N2s, N2r,
    g_send, g_recv, c_send, c_recv, j_sem, u_sem, r_send, r_recv, x1_send, x1_recv, x2_send, x2_recv,
    n1_send, n1_recv, n2_send, n2_recv, hello, in_sem, out_sem,
):
    d = lax.axis_index("domain")
    band = lax.axis_index("band")
    zh = d // (N_X * N_Y)
    gx = (d // N_Y) % N_X
    gy = d % N_Y
    zl = band // 2
    core = band % 2
    sibling = zl * 2 + (1 - core)
    has_below = d > 0
    has_above = d < N_DOM - 1
    mid = N_DOM // N_ZH
    end_y = has_above & (d % N_Y == N_Y - 1)
    first_y = has_below & (d % N_Y == 0)
    up_early = end_y | (d == mid - 2)
    up_mend = first_y | (d == mid - 1)
    down_early = first_y | (d == mid + 1)
    down_mend = end_y | (d == mid)

    given = [
        (cn_hbm, cns_ref), (cn_hbm, cn_ref), (scale_hbm, scale_ref), (sr_hbm, sr_ref),
        (start_hbm, start_ref), (ck_hbm, ck_ref), (res_hbm, res_ref), (pot_hbm, pot_ref),
    ]
    given = [pltpu.make_async_copy(a, b, in_sem.at[i]) for i, (a, b) in enumerate(given)]
    for c in given:
        c.start()

    Gr[...] = jnp.zeros_like(Gr)
    cr[...] = jnp.zeros_like(cr)
    Jr[...] = jnp.full(Jr.shape, -3.0, f32)
    Ur[0:8, :] = jnp.full((8, PLP), -4.0, f32)
    Ur[8:16, :] = jnp.zeros((8, PLP), f32)

    barrier = pltpu.get_barrier_semaphore()

    def greet(dom, bnd):
        pl.semaphore_signal(barrier, inc=1, device_id=(dom, bnd), device_id_type=MESH)

    x_peers = [(zh * N_X + (gx + i) % N_X) * N_Y + gy for i in range(1, N_X)]
    y_peers = [(zh * N_X + gx) * N_Y + (gy + i) % N_Y for i in range(1, N_Y)]
    z_peer = ((1 - zh) * N_X + gx) * N_Y + gy
    for p in [z_peer] + y_peers + x_peers:
        greet(p, band)

    @pl.when(has_below)
    def _():
        greet(d - 1, band)

    @pl.when(has_above)
    def _():
        greet(d + 1, band)

    @pl.when(zl > 0)
    def _():
        greet(d, band - 2)

    @pl.when(zl < N_ZL - 1)
    def _():
        greet(d, band + 2)

    greet(d, sibling)

    for c in given[0:3]:
        c.wait()
    corner = [cns_ref[c, 0] for c in range(4)]
    right_x = [cns_ref[c, EDGE - 1] for c in range(4)]
    right_y = [cns_ref[c, EDGE * (EDGE - 1)] for c in range(4)]
    pos = []
    for c in range(4):
        in_x = sum([jnp.where(right_x[b] == corner[c], 1, 0) for b in range(4)])
        in_y = sum([jnp.where(right_y[b] == corner[c], 1, 0) for b in range(4)])
        pos.append(in_x + 2 * in_y)
    scale = []
    for p in range(4):
        s = jnp.float32(0.0)
        for c in range(4):
            s = s + jnp.where(pos[c] == p, scale_ref[c], 0.0)
        scale.append(s)

    cnp[...] = jnp.zeros_like(cnp)
    cnp[0:4, 0:343] = cn_ref[...]
    row8 = iota((8, KL), 0)
    full = jnp.zeros((8, KL), jnp.int32)
    for c in range(4):
        line = jnp.broadcast_to(cnp[c : c + 1, :], (8, KL))
        full = full + jnp.where((row8 & 3) == pos[c], line, 0)
    cn8 = jnp.where(row8 < 4, full >> 5, full & 31).astype(f32).astype(bf16)

    rr = iota((XS, KL), 0)
    ln = iota((XS, KL), 1)
    yy = rr >> 3
    zz = rr & 7
    k_base = jnp.where(
        (zz < EDGE) & (yy < NX), zz * 49 + jnp.where(yy > 6, yy - 6, yy) * 7, -1000
    )
    diff = k_base - ln
    l8 = iota((XS, 8), 1)
    y8 = iota((XS, 8), 0) >> 3
    z128 = iota((XS, 128), 0) & 7
    y128 = iota((XS, 128), 0) >> 3
    top_row = (z128 < EDGE) & (y128 < NX)
    own_row = (z128 < EDGE - 1) & (y128 < NX)
    weights = jnp.where(iota((8, 128), 0) < 4, 32.0, 1.0).astype(bf16)
    lane = iota((XS, 128), 1).astype(f32)
    for X in range(NX):
        x = X if X <= 6 else X - 6
        one = hot(diff == -x)
        Q[X * XS : (X + 1) * XS, :] = one
        a1 = mm_nt(one, cn8)
        cell = jnp.where(y8 > 6, 2, 0) + (1 if X > 6 else 0)
        a1 = jnp.where((l8 & 3) == cell, a1, 0.0).astype(bf16)
        pl_x = mm(a1, weights)
        place[X * XS : (X + 1) * XS, :] = jnp.where(top_row, pl_x, -1.0)
        own = jnp.where(own_row, pl_x, -1.0)
        for t in range(8):
            Pm[X * XS : (X + 1) * XS, t * 128 : (t + 1) * 128] = hot(own == lane + 128.0 * t)
    place[NR:NRP, :] = jnp.full((NRP - NR, 128), -1.0, f32)

    given[3].wait()
    srp[...] = jnp.full(srp.shape, -5.0, f32)
    srp[0:1, 0:PLANE] = sr_ref[...].astype(f32)
    top_col[...] = jnp.full(top_col.shape, -1.0, f32)
    yrow = iota((16, 128), 0)
    lane16 = iota((16, 128), 1)
    ET[...] = jnp.zeros_like(ET)
    for X in range(NX):
        b0 = jnp.concatenate(
            [place[pl.ds(X * XS, 8, stride=8), :], place[pl.ds(X * XS + 64, 8, stride=8), :]], 0
        )
        b0 = jnp.where(yrow < NX, b0, -1.0)
        for t in range(2):
            ET[X * 16 : X * 16 + 16, t * 128 : (t + 1) * 128] = hot(
                b0 == srp[0:1, t * 128 : (t + 1) * 128]
            )
        t0 = jnp.concatenate(
            [place[pl.ds(X * XS + 6, 8, stride=8), :], place[pl.ds(X * XS + 54, 8, stride=8), :]],
            0,
        )
        top_col[X * 16 : X * 16 + 16, :] = jnp.where((yrow & 7) < EDGE, t0 - float(OWNED), -1.0)
    jm = iota((PLP, 128), 0).astype(f32).astype(bf16)
    p_row = iota((PLP, 128), 0)
    jb = mm(ET[...], jm)
    jbot_col[...] = jnp.where(((p_row & 15) < NX) & (p_row < PL), jb, -2.0)
    p_lane = iota((8, PLP), 1)
    p_ok = ((p_lane & 15) < NX) & (p_lane < PL)
    jr = mm_nt(iota((8, PLP), 1).astype(f32).astype(bf16), ET[...])
    Js[...] = jnp.where(p_ok, jr, -2.0)

    pr = iota((PLP, KL), 0)
    pln = iota((PLP, KL), 1)
    pX = pr >> 4
    pY = pr & 15
    ty = pr & 7
    tcy = (pr >> 3) & 1
    t_in = (pX < NX) & (ty < EDGE)
    ox = jnp.where(pX > 6, pX - 6, pX)
    q_top = hot(t_in & (294 + ty * 7 + ox == pln))
    at = mm_nt(cn8, q_top)
    lX = p_lane >> 4
    l_cell = jnp.where(lX > 6, 1, 0) + ((p_lane >> 3) & 1) * 2
    t_ok = ((p_lane & 7) < EDGE) & (p_lane < PL)
    r8 = iota((8, PLP), 0)
    at = jnp.where((r8 & 3) == l_cell, at, 0.0) * jnp.where(r8 < 4, 32.0, 1.0)
    top_line = jnp.sum(at, 0, keepdims=True) - float(OWNED)
    Us[0:8, :] = jnp.where(t_ok, jnp.broadcast_to(top_line, (8, PLP)), -1.0)
    srow = iota((8, PLP), 0)
    stile = jnp.zeros((8, PLP), f32)
    for c in range(4):
        stile = jnp.where(srow == c, scale[c], stile)
    Us[8:16, :] = stile

    given[6].wait()
    RB[band, 1008:1024, :] = jnp.zeros((16, ORB), bf16)
    RB[band, 0:OWNED, :] = res_ref[...]

    def remote(src, dst, ssem, rsem, dom, bnd):
        return pltpu.make_async_remote_copy(
            src_ref=src, dst_ref=dst, send_sem=ssem, recv_sem=rsem,
            device_id=(dom, bnd), device_id_type=MESH,
        )

    j_copy = remote(Js, Jr, j_sem.at[0], j_sem.at[1], d - 1, band)
    u_copy = remote(Us, Ur, u_sem.at[0], u_sem.at[1], d + 1, band)

    def turn(dist):
        if dist == 0:
            block(sibling, sibling, 0).wait_recv()
            RBT[band] = RB[band].T
            RBT[sibling] = RB[sibling].T
            return

        def both(src):
            other = src + 1 - 2 * core
            block(other, sibling, 0).wait_recv()
            RBT[src] = RB[src].T
            RBT[other] = RB[other].T

        @pl.when(zl >= dist)
        def _():
            both(band - 2 * dist)

        @pl.when(zl + dist <= N_ZL - 1)
        def _():
            both(band + 2 * dist)

    def block(src, to, s):
        return remote(RB.at[src], RB.at[src], r_send.at[s], r_recv.at[src], d, to)

    def send_own(start):
        def act(c):
            c.start() if start else c.wait_send()

        @pl.when(zl < N_ZL - 1)
        def _():
            act(block(band, band + 2, 0))

        @pl.when(zl > 0)
        def _():
            act(block(band, band - 2, 1))

        act(block(band, sibling, 2))

    def forward(dist, start):
        @pl.when(zl >= dist)
        def _():
            src = band - 2 * dist
            if start:
                block(src, sibling, 0).wait_recv()

            @pl.when(zl < N_ZL - 1)
            def _():
                c = block(src, band + 2, 3 * dist)
                c.start() if start else c.wait_send()

            c = block(src, sibling, 3 * dist + 1)
            c.start() if start else c.wait_send()

        @pl.when(zl + dist <= N_ZL - 1)
        def _():
            src = band + 2 * dist
            if start:
                block(src, sibling, 0).wait_recv()

            @pl.when(zl > 0)
            def _():
                c = block(src, band - 2, 9 + 3 * dist)
                c.start() if start else c.wait_send()

            c = block(src, sibling, 10 + 3 * dist)
            c.start() if start else c.wait_send()

    given[4].wait()
    st[1008:1024, :] = jnp.zeros((16, ORB), bf16)
    st[0:OWNED, :] = start_ref[...]
    V[0, 0:NR, :] = mm(Pm[...], st[...])
    V[0, NR:NRP, :] = jnp.zeros((NRP - NR, ORB), f32)
    V[1, :, :] = jnp.zeros((NRP, ORB), f32)
    part[...] = jnp.zeros_like(part)
    zero8 = jnp.zeros((8, ORB), f32)
    for X in range(NX):
        R[X * 64 : X * 64 + 64, 0:128] = V[0, X * XS : X * XS + 64, :].astype(bf16)
        R[X * 64 : X * 64 + 64, 128:256] = V[0, X * XS + 48 : X * XS + 112, :].astype(bf16)

    given[5].wait()
    kpad[...] = jnp.zeros_like(kpad)
    kpad[0:343, 0:343] = ck_ref[...]
    kmat = kpad[...]
    r56 = iota((56, KL), 0)
    k56 = jnp.where((r56 & 7) < 7, (r56 & 7) * 49 + (r56 >> 3) * 7, -1000) - iota((56, KL), 1)
    row_hot = jnp.concatenate([jnp.where(k56 == -x, 1.0, 0.0) for x in range(7)], 0).astype(bf16)
    r64 = iota((64, KL), 0)
    k64 = (
        jnp.where(((r64 & 7) < 7) & (r64 < 56), (r64 & 7) * 49 + (r64 >> 3) * 7, -1000)
        - iota((64, KL), 1)
    )
    col_hot = jnp.concatenate([hot(k64 == -x) for x in range(7)], 0)
    K1[...] = mm(row_hot, kmat).astype(bf16)
    Kp[...] = mm_nt(K1[...], col_hot).astype(bf16)
    r8k = iota((8, KL), 0)
    l8k = iota((8, KL), 1)
    kt = jnp.where(r8k < EDGE, 294 + r8k * 7, -1000) - l8k
    kb = jnp.where(r8k < EDGE, r8k * 7, -1000) - l8k
    none8 = jnp.zeros((8, KL), f32)
    t_hot = jnp.concatenate([jnp.where(kt == -x, 1.0, 0.0) for x in range(7)] + [none8], 0).astype(bf16)
    b_hot = jnp.concatenate([jnp.where(kb == -x, 1.0, 0.0) for x in range(7)] + [none8], 0).astype(bf16)
    top_k = mm(t_hot, kmat).astype(bf16)
    T[...] = mm_nt(top_k, col_hot)[0:56].astype(bf16)

    def down(k, src):
        return remote(
            src.at[k, pl.ds(0, PL)], Gr.at[k, pl.ds(0, PL)], g_send.at[k], g_recv.at[k], d - 1, band
        )

    def up(k, src):
        return remote(
            src.at[k, pl.ds(0, PL)], cr.at[k, pl.ds(0, PL)], c_send.at[k], c_recv.at[k], d + 1, band
        )

    def lowest_plane(v, out, k, more=None):
        for X in range(NX):
            lo = v[pl.ds(X * XS, 8, stride=8), :]
            hi = v[pl.ds(X * XS + 64, 8, stride=8), :]
            both = jnp.concatenate([lo, hi], 0)
            if more is not None:
                both = both + more[X * 16 : X * 16 + 16]
            out[k, X * 16 : X * 16 + 16, :] = both.astype(bf16)

    def top_sums(r, sc):
        parts = [mm(T[...], r[384 * cx : 384 * cx + KR, :]) for cx in range(2)]
        out = []
        for X in range(NX):
            tiles = []
            for cy in range(2):
                t = None
                for cx in range(2):
                    x = X - 6 * cx
                    if 0 <= x < 7:
                        p = parts[cx][x * 8 : x * 8 + 8, cy * 128 : (cy + 1) * 128] * sc[cx + 2 * cy]
                        t = p if t is None else t + p
                tiles.append(t)
            out.append((X * 16, X * 16 + 16, jnp.concatenate(tiles, 0)))
        return out

    def prepare_down(k, cur):
        Gs[k, PL:PLP, :] = jnp.zeros((PLP - PL, ORB), bf16)
        lowest_plane(V.at[cur], Gs, k)

    def prepare_up(k):
        cs[k, PL:PLP, :] = jnp.zeros((PLP - PL, ORB), bf16)
        for lo, hi, value in top_sums(R, scale):
            cs[k, lo:hi, :] = value.astype(bf16)

    def to_operand(r, X, flat):
        r[X * 64 : X * 64 + 64, 0:128] = flat[0:64].astype(bf16)
        r[X * 64 : X * 64 + 64, 128:256] = jnp.concatenate([flat[48:104], zero8], 0).astype(bf16)

    def send_planes(k, cur):
        prepare_down(k, cur)

        @pl.when(has_below & jnp.logical_not(down_early))
        def _():
            down(k, Gs).start()

        for X in range(NX):
            to_operand(R, X, V[cur, X * XS : X * XS + 104, :])

        @pl.when(jnp.logical_not(up_early))
        def _():
            prepare_up(k)

            @pl.when(has_above)
            def _():
                up(k, cs).start()

    prepare_down(0, 0)
    prepare_up(0)

    ones = lambda cond: jnp.where(cond, 1, 0)
    count = (
        ones(has_below) + ones(has_above) + ones(zl > 0) + ones(zl < N_ZL - 1)
        + 2 + len(x_peers) + len(y_peers)
    )
    pl.semaphore_wait(barrier, count)

    for p in y_peers:
        pl.semaphore_signal(hello, inc=1, device_id=(p, band), device_id_type=MESH)

    @pl.when(has_below)
    def _():
        j_copy.start()

    @pl.when(has_above)
    def _():
        u_copy.start()

    @pl.when(has_below)
    def _():
        down(0, Gs).start()

    @pl.when(has_above)
    def _():
        up(0, cs).start()

    send_own(True)

    given[7].wait()
    pot8[...] = jnp.zeros_like(pot8)
    pot = pot_ref[...]
    p_hi = pot.astype(bf16)
    rest = pot - p_hi.astype(f32)
    p_mid = rest.astype(bf16)
    p_lo = (rest - p_mid.astype(f32)).astype(bf16)
    pot8[0:1, 0:OWNED] = p_hi.astype(f32)
    pot8[1:2, 0:OWNED] = p_mid.astype(f32)
    pot8[2:3, 0:OWNED] = p_lo.astype(f32)
    pcol = mm_nt(Pm[...], pot8[...].astype(bf16)).astype(bf16)
    potc[...] = mm(pcol, jnp.ones((8, 128), bf16)) - CENTRE

    q_l = iota((PLP, 64), 1)
    q_p = iota((PLP, 64), 0)
    q_in = ((q_l & 7) < EDGE) & (q_l < 56)

    def in_top(c):
        cx, cy = c % 2, c // 2
        y_ok = (((q_p >> 3) & 1) == cy) & ((q_p & 7) == (q_l & 7))
        return hot(((q_p >> 4) - 6 * cx == (q_l >> 3)) & y_ok & q_in)

    def in_bottom(c):
        cx, cy = c % 2, c // 2
        return hot(((q_p >> 4) - 6 * cx == (q_l >> 3)) & ((q_p & 15) - 6 * cy == (q_l & 7)) & q_in)

    k_tt = mm_nt(top_k, t_hot).astype(bf16)
    k_g = mm_nt(K1[...], t_hot).astype(bf16)
    for c in range(4):
        e_top = in_top(c)
        KgP[c] = mm_nt(k_g, e_top).astype(bf16)
        KttP[c] = mm_nt(mm(e_top, k_tt).astype(bf16), e_top)

    lin = iota((8, NRL), 1)
    lin_x = jnp.floor((lin.astype(f32) + 0.5) * (1.0 / XS)).astype(jnp.int32)
    lin_r = lin - lin_x * XS
    lin_y = lin_r >> 3
    lin_z = lin_r & 7
    lin_cell = jnp.where(lin_x > 6, 1, 0) + jnp.where(lin_y > 6, 2, 0)
    lin_8 = iota((8, NRL), 0)
    Q[NR:NRL, :] = jnp.zeros((NRL - NR, KL), bf16)
    ar = mm_nt(cn8, Q[...])
    ar = jnp.where((lin_8 & 3) == lin_cell, ar, 0.0) * jnp.where(lin_8 < 4, 32.0, 1.0)
    ar = jnp.broadcast_to(jnp.sum(ar, 0, keepdims=True), (8, NRL))
    prow[...] = jnp.where((lin_x < NX) & (lin_y < NX) & (lin_z < EDGE - 1), ar, -1.0)
    n16 = iota((16, NRL), 0).astype(f32)

    def fill(i, carry):
        base = (i * 16).astype(f32)
        PT[pl.ds(pl.multiple_of(i * 16, 16), 16), :] = hot(prow[0:1, :] == n16 + base)
        return carry


    mask8 = jnp.where(iota((8, ORB), 0) < EDGE - 1, 1.0, 0.0)

    def spread(ref_of, X, factor):
        lo, hi = None, None
        for cx in range(2):
            x = X - 6 * cx
            if 0 <= x < 7:
                a = ref_of(cx, 0, x).reshape(7, 8, ORB) * factor(cx, 0)
                b = ref_of(cx, 1, x).reshape(7, 8, ORB) * factor(cx, 1)
                lo = a if lo is None else lo + a
                hi = b if hi is None else hi + b
        return jnp.concatenate([lo[0:6], lo[6:7] + hi[0:1], hi[1:7]], 0)

    def bulk(k, cur):
        nxt = 1 - cur
        a = pick(k, [t[0] for t in TERMS])
        b = pick(k, [t[1] for t in TERMS])
        am = mask8 * a
        for cx in range(2):
            O[cx] = mm(Kp[...], R[384 * cx : 384 * cx + KR, :])
        for X in range(NX):
            rows = slice(X * XS, X * XS + 104)
            s = spread(
                lambda cx, cy, x: O[cx, x * 56 : x * 56 + 56, cy * 128 : (cy + 1) * 128],
                X,
                lambda cx, cy: scale[cx + 2 * cy],
            )
            v = V[cur, rows, :].reshape(NX, 8, ORB)
            u = V[nxt, rows, :].reshape(NX, 8, ORB)
            pc = potc[rows, :].reshape(NX, 8, ORB)
            new = (s + pc * v) * am[None] - b * u
            part[rows, :] = new.reshape(104, ORB)

    bulk(0, 0)

    def halves(v):
        hi = v.astype(bf16)
        return hi, (v - hi.astype(f32)).astype(bf16)

    def plane_to_plane(rows_top, onward):
        total = jnp.zeros((PLP, PLP), f32)
        if rows_top:
            block_k = mm_nt(top_k, b_hot).astype(bf16)
        else:
            block_k = mm_nt(mm(b_hot, kmat).astype(bf16), t_hot).astype(bf16)
        for c in range(4):
            one, two = (in_top(c), in_bottom(c)) if rows_top else (in_bottom(c), in_top(c))
            total = total + mm_nt(mm(one, block_k).astype(bf16), two) * scale[c]
        hi = total.astype(bf16)
        lo = (total - hi.astype(f32)).astype(bf16)
        total = mm(hi, onward) + mm(lo, onward)
        hi = total.astype(bf16)
        D2[0] = hi
        D2[1] = (total - hi.astype(f32)).astype(bf16)

    def add_plane(v, e):
        for X in range(NX):
            lo = pl.ds(X * XS, 8, stride=8)
            hi = pl.ds(X * XS + 64, 8, stride=8)
            v[lo, :] = v[lo, :] + e[X * 16 : X * 16 + 8]
            v[hi, :] = v[hi, :] + e[X * 16 + 8 : X * 16 + 16]

    def ghost(X, am, sc):
        return spread(
            lambda cx, cy, x: OG[cx + 2 * cy, x * 56 : x * 56 + 56, :],
            X,
            lambda cx, cy: (am * sc[cx + 2 * cy])[None],
        )

    def ahead(k):
        am = mask8 * pick(k - 1, [t[0] for t in TERMS])
        sb = [Ur[8 + c : 9 + c, 0:128] for c in range(4)]
        for c in range(4):
            OG[c] = mm(KgB[c], Gs[k - 1])
        for X in range(NX):
            to_operand(R2, X, ghost(X, am, sb).reshape(104, ORB))
        for lo, hi, value in top_sums(R2, sb):
            CR[lax.rem(k, 2), lo:hi, :] = value

    def mend_sums(k):
        cr[k, 0:PL, :] = (cr[k, 0:PL, :].astype(f32) + CR[lax.rem(k, 2)]).astype(bf16)

    def mend_plane(k):
        before = pick(k - 1, [t[0] for t in TERMS])

        @pl.when((k != 1) | (d != mid - 1))
        def _():
            Gr[k] = (Gr[k].astype(f32) + mm(M1T[...], cs[k - 1]) * before).astype(bf16)

        @pl.when((k == 1) & (d == mid - 1))
        def _():
            own = mm(M1[...], Gr[0]).astype(bf16)
            sums = cs[0].astype(f32) + mm(WT[0], own) + mm(WT[1], own)
            Gr[k] = (Gr[k].astype(f32) + mm(M1T[...], sums.astype(bf16)) * before).astype(bf16)

    def early_up(k):
        a = pick(k, [t[0] for t in TERMS])
        g = Gs[k]
        add_plane(part, (mm(W2[0], g) + mm(W2[1], g)) * a)

        @pl.when(up_early & (k < DEGREE - 1))
        def _():
            for X in range(NX):
                to_operand(R2, X, part[X * XS : X * XS + 104, :])
            for lo, hi, value in top_sums(R2, scale):
                CR2[lo:hi, :] = value

            @pl.when(has_below)
            def _():
                up(k, cs).wait_recv()

            @pl.when(up_mend & (k >= 1))
            def _():
                mend_sums(k)

            more = (mm(D2[0], cr[k]) + mm(D2[1], cr[k])) * a
            Ps[k + 1] = (CR2[...] + more[0:PL]).astype(bf16)
            up(k + 1, Ps).start()

    def early_down(k):
        a = pick(k, [t[0] for t in TERMS])

        @pl.when(has_above)
        def _():
            down(k, Gs).wait_recv()

        @pl.when(down_mend & (k >= 1))
        def _():
            mend_plane(k)

        more = (mm(D2[0], Gr[k]) + mm(D2[1], Gr[k])) * a
        lowest_plane(part, Qs, k + 1, more)
        down(k + 1, Qs).start()

    def finish(k, cur, last):
        nxt = 1 - cur
        a = pick(k, [t[0] for t in TERMS])
        am = mask8 * a
        rest_down = has_above if last else has_above & jnp.logical_not(down_early)
        rest_up = has_below if last else has_below & jnp.logical_not(up_early)

        @pl.when(rest_down)
        def _():
            down(k, Gs).wait_recv()

        @pl.when(rest_down & down_mend & (k >= 1))
        def _():
            mend_plane(k)

        for c in range(4):
            OG[c] = mm(KgD[c], Gr[k])
        for X in range(NX):
            rows = slice(X * XS, X * XS + 104)
            new = part[rows, :].reshape(NX, 8, ORB) + ghost(X, am, scale)
            V[nxt, rows, :] = new.reshape(104, ORB)

        @pl.when(rest_up)
        def _():
            up(k, cs).wait_recv()

        @pl.when(rest_up & up_mend & (k >= 1))
        def _():
            mend_sums(k)

        add_plane(V.at[nxt], mm(F[...], cr[k]) * a)
        if not last:
            return None
        sq = jnp.zeros((8, ORB), f32)
        for X in range(NX):
            padded = V[nxt, X * XS : (X + 1) * XS, :]
            cube = padded.reshape(NX + 1, 8, ORB)
            sq = sq + jnp.sum(cube * cube, 0)
            top = padded.astype(bf16)
            H2[X * XS : (X + 1) * XS, 0:128] = top
            H2[X * XS : (X + 1) * XS, 128:256] = (padded - top.astype(f32)).astype(bf16)
        return sq

    @pl.when(has_above)
    def _():
        j_copy.wait_recv()

    tc = top_col[...]
    M1[...] = jnp.concatenate([hot(tc == Jr[0:1, t * 128 : (t + 1) * 128]) for t in range(2)], 1)

    @pl.when(down_early)
    def _():
        plane_to_plane(False, M1[...])

    @pl.when(d == mid)
    def _():
        early_down(0)

    @pl.when(has_below)
    def _():
        u_copy.wait_recv()

    jc = jbot_col[...]
    F[...] = jnp.concatenate([hot(jc == Ur[0:1, t * 128 : (t + 1) * 128]) for t in range(2)], 1)

    @pl.when(up_early)
    def _():
        plane_to_plane(True, F[...])

    w = jnp.zeros((PLP, PLP), f32)
    for c in range(4):
        w = w + KttP[c] * Ur[8 + c : 9 + c, :]
    fm = F[...]
    w_hi, w_lo = halves(w)
    w = mm_nt(mm(fm, w_hi).astype(bf16), fm) + mm_nt(mm(fm, w_lo).astype(bf16), fm)
    W2[0], W2[1] = halves(w)
    early_up(0)

    @pl.when(down_early & (d != mid))
    def _():
        early_down(0)

    for c in range(4):
        KgD[c] = mm(KgP[c], M1[...]).astype(bf16)

    @pl.when(down_mend)
    def _():
        eye = hot(iota((PLP, PLP), 0) == iota((PLP, PLP), 1))
        M1T[...] = mm_nt(eye, M1[...]).astype(bf16)

    @pl.when(d == mid - 1)
    def _():
        total = KttP[0] * scale[0]
        for c in range(1, 4):
            total = total + KttP[c] * scale[c]
        WT[0], WT[1] = halves(total)

    @pl.when(up_mend)
    def _():
        for c in range(4):
            KgB[c] = mm_nt(KgP[c], F[...]).astype(bf16)

    def step(k, carry):
        cur = lax.rem(k, 2)
        @pl.when(up_mend)
        def _():
            ahead(k + 1)

        for dist in range(1, N_ZL - 1):

            @pl.when(k == 2 * dist + 1)
            def _(dist=dist):
                forward(dist, True)

        for dist in range(2):

            @pl.when(k == 4 * dist + 2)
            def _(dist=dist):
                turn(dist)

        lax.fori_loop(k * 10, jnp.minimum(k * 10 + 10, OWNP // 16), fill, 0)
        finish(k, cur, False)
        send_planes(k + 1, 1 - cur)
        bulk(k + 1, 1 - cur)
        early_up(k + 1)

        @pl.when(up_early)
        def _():
            prepare_up(k + 1)

        @pl.when(down_early & (k + 1 < DEGREE - 1))
        def _():
            early_down(k + 1)

        return carry

    lax.fori_loop(0, DEGREE - 1, step, 0)
    final = DEGREE - 1
    forward(3, True)
    turn(2)
    turn(3)
    H2[NR:NRL, :] = jnp.zeros((NRL - NR, 256), bf16)
    sq = finish(final, final % 2, True)

    N1s[...] = jnp.broadcast_to(jnp.sum(sq, 0, keepdims=True), (8, ORB))

    def n1(i):
        return remote(N1s, N1r.at[i], n1_send.at[i], n1_recv.at[i], x_peers[i], band)

    for i in range(3):
        n1(i).start()

    CO[...] = mm(PT[...], H2[...])
    LOW[...] = CO[:, 0:128].astype(bf16)

    def x1(i, h):
        j = i * N_ZH + h
        return remote(mpb.at[j], X1.at[j], x1_send.at[j], x1_recv.at[j], x_peers[i], band)

    for i in (1, 0, 2, 3):
        tx = (gx + 1 + i) % N_X
        for h in range(N_ZH):
            m = mm(RBT[h * N_X + tx], LOW[...])
            if i < 3:
                mpb[i * N_ZH + h] = m.astype(bf16)
                x1(i, h).start()
            else:
                M0[h] = m

    for i in range(3):
        n1(i).wait_recv()
    N2s[...] = N1s[...] + N1r[0] + N1r[1] + N1r[2]

    yz_off = [(a, b) for a in range(N_ZH) for b in range(N_Y) if (a, b) != (0, 0)]
    far_first = sorted(range(15), key=lambda i: (-yz_off[i][0], abs(yz_off[i][1] - 4)))

    def to_yz(i):
        return (zh + yz_off[i][0]) % N_ZH, (gy + yz_off[i][1]) % N_Y

    def n2(i):
        to_z, to_y = to_yz(i)
        return remote(
            N2s, N2r.at[i], n2_send.at[i], n2_recv.at[i], (to_z * N_X + gx) * N_Y + to_y, band
        )

    pl.semaphore_wait(hello, len(y_peers))
    for i in far_first:
        n2(i).start()

    for i in range(3):
        for h in range(N_ZH):
            x1(i, h).wait_recv()
    for h in range(N_ZH):
        acc = M0[h]
        for i in range(3):
            acc = acc + X1[i * N_ZH + h].astype(f32)
        for y in range(N_Y):
            to = y * 32 + h * 16
            SF[to : to + 16, :] = acc[y * 16 : y * 16 + 16]
            SB[to : to + 16, :] = acc[y * 16 : y * 16 + 16].astype(bf16)

    def x2(i):
        to_z, to_y = to_yz(i)
        return remote(
            SB.at[pl.ds(pl.multiple_of(to_y * 32 + to_z * 16, 16), 16)], X2.at[i], x2_send.at[i],
            x2_recv.at[i], (to_z * N_X + gx) * N_Y + to_y, band,
        )

    for i in far_first:
        x2(i).start()

    total = N2s[...]
    for i in range(15):
        n2(i).wait_recv()
        total = total + N2r[i]
    inverse = lax.rsqrt(total[0:1, :] + epsilon)
    OUT[...] = ((CO[:, 0:128] + CO[:, 128:256]) * inverse)[0:OWNED].astype(bf16)
    out_copy = pltpu.make_async_copy(OUT, out_ref, out_sem.at[0])
    out_copy.start()

    m = SF[pl.ds(pl.multiple_of(gy * 32 + zh * 16, 16), 16), :]
    for i in range(15):
        x2(i).wait_recv()
        m = m + X2[i].astype(f32)
    margin_ref[...] = m * inverse
    out_copy.wait()

    @pl.when(has_below)
    def _():
        j_copy.wait_send()

    @pl.when(has_above)
    def _():
        u_copy.wait_send()

    def sent(k, carry):
        @pl.when(has_below)
        def _():
            down(k, Gs).wait_send()

        @pl.when(has_above)
        def _():
            up(k, cs).wait_send()

        return carry

    lax.fori_loop(0, DEGREE, sent, 0)
    send_own(False)
    for dist in range(1, N_ZL):
        forward(dist, False)
    for i in range(3):
        n1(i).wait_send()
        for h in range(N_ZH):
            x1(i, h).wait_send()
    for i in range(15):
        n2(i).wait_send()
        x2(i).wait_send()


def per_device(start_block, resident, cell_kernel, cell_scale, potential, cell_nodes, send_rows):
    vm = lambda shape, t: pltpu.VMEM(shape, t)
    dma = lambda n: pltpu.SemaphoreType.DMA((n,))
    vmem = pl.BlockSpec(memory_space=pltpu.VMEM)
    scratch = [
        vm((OWNED, ORB), bf16),
        vm((OWNED, ORB), bf16),
        vm((343, 343), bf16),
        pltpu.SMEM((4,), f32),
        vm((1, OWNED), f32),
        vm((4, 343), jnp.int32),
        pltpu.SMEM((4, 343), jnp.int32),
        vm((1, PLANE), jnp.int32),
        vm((OWNED, ORB), bf16),
        vm((2, NRP, ORB), f32),
        vm((832, 256), bf16),
        vm((2, MR, 256), f32),
        vm((4, MR, ORB), f32),
        vm((NRP, ORB), f32),
        vm((NR, ORB), f32),
        vm((NRP, ORB), f32),
        vm((8, NRL), f32),
        vm((NR, OWNP), bf16),
        vm((OWNP, NRL), bf16),
        vm((NRL, KL), bf16),
        vm((OWNP, ORB), bf16),
        vm((KL, KL), bf16),
        vm((MR, KL), bf16),
        vm((MR, KR), bf16),
        vm((56, KR), bf16),
        vm((4, MR, PLP), bf16),
        vm((4, PLP, PLP), f32),
        vm((4, MR, PLP), bf16),
        vm((PLP, PLP), bf16),
        vm((PLP, PLP), bf16),
        vm((2, PLP, PLP), bf16),
        vm((PLP, ORB), f32),
        vm((PLP, ORB), f32),
        vm((8, OWNP), f32),
        vm((8, KL), jnp.int32),
        vm((8, PLP), f32),
        vm((8, ORB, OWNP), bf16),
        vm((832, 256), bf16),
        vm((4, MR, PLP), bf16),
        vm((PLP, PLP), bf16),
        vm((2, PLP, PLP), bf16),
        vm((PLP, PLP), bf16),
        vm((2, PLP, PLP), bf16),
        vm((2, PL, ORB), f32),
        vm((PL, ORB), f32),
        vm((DEGREE, PL, ORB), bf16),
        vm((DEGREE, PL, ORB), bf16),
        vm((DEGREE, PLP, ORB), bf16),
        vm((DEGREE, PLP, ORB), bf16),
        vm((DEGREE, PLP, ORB), bf16),
        vm((DEGREE, PLP, ORB), bf16),
        vm((8, PLP), f32),
        vm((8, PLP), f32),
        vm((16, PLP), f32),
        vm((16, PLP), f32),
        vm((8, OWNP, ORB), bf16),
        vm((NRL, 256), bf16),
        vm((OWNP, ORB), bf16),
        vm((OWNP, 256), f32),
        vm((6, 128, ORB), bf16),
        vm((6, 128, ORB), bf16),
        vm((2, 128, ORB), f32),
        vm((256, ORB), f32),
        vm((256, ORB), bf16),
        vm((15, 16, ORB), bf16),
        vm((8, ORB), f32),
        vm((3, 8, ORB), f32),
        vm((8, ORB), f32),
        vm((15, 8, ORB), f32),
        dma(8), dma(8), dma(8), dma(8), dma(2), dma(2), dma(20), dma(8),
        dma(6), dma(6), dma(15), dma(15), dma(3), dma(3), dma(15), dma(15),
        pltpu.SemaphoreType.REGULAR, dma(8), dma(1),
    ]
    return pl.pallas_call(
        kernel,
        out_shape=(
            jax.ShapeDtypeStruct((OWNED, ORB), bf16),
            jax.ShapeDtypeStruct((16, ORB), f32),
        ),
        in_specs=[pl.BlockSpec(memory_space=pl.ANY)] * 7,
        out_specs=(pl.BlockSpec(memory_space=pl.ANY), vmem),
        scratch_shapes=scratch,
        compiler_params=pltpu.CompilerParams(
            collective_id=0, has_side_effects=True, vmem_limit_bytes=56 * 1024 * 1024
        ),
        cost_estimate=pl.CostEstimate(
            flops=4_000_000_000, bytes_accessed=1_000_000, transcendentals=128
        ),
    )(
        start_block, resident, cell_kernel, cell_scale, potential.reshape(1, OWNED), cell_nodes,
        send_rows.reshape(1, PLANE),
    )


def solution(mesh):
    return jax.shard_map(
        per_device,
        mesh=mesh,
        in_specs=(
            P("domain", "band"),
            P("domain", "band"),
            P(),
            P("domain"),
            P("domain"),
            P("domain", None),
            P("domain"),
        ),
        out_specs=(P("domain", "band"), P("domain", "band")),
        check_vma=False,
    )
```
